32 devices in a mesh: tower: 2 (over x), batch: 16 (over z, y, core).
Axes of the slice: x: 2, y: 2, z: 4, core: 2. Of those that a mesh axis runs over, the one named last changes fastest.
Arguments:
- dense_feats: bfloat16 [16384, 13], P('batch'), may hold values from -6 to 6
- category_ids: int32 [16384, 26], P('batch'), may hold values from 0 to 65535, as said below
- labels: int32 [16384], P('batch'), may hold values from 0 to 1
- valid_mask: int32 [16384], P('batch'), may hold values from 0 to 1
- embed_table: float32 [65536, 39], P(('tower', 'batch')), may hold values from -3 to 3
- table_first: float32 [65536, 39], P(('tower', 'batch')), may hold values from -5.722046e-06 to 5.722046e-06
- table_second: float32 [65536, 39], P(('tower', 'batch')), may hold values from 8.717179e-14 to 3.4868717e-13
- cross_weight: float32 [2, 1027, 1027], P('tower'), may hold values from -0.1875 to 0.1875
- cross_first: float32 [2, 1027, 1027], P('tower'), may hold values from -0.00015258789 to 0.00015258789
- cross_second: float32 [2, 1027, 1027], P('tower'), may hold values from 5.493164e-11 to 2.1972656e-10
- deep_weight: float32 [1024, 1027], P(('tower', 'batch')), may hold values from -0.1875 to 0.1875
- deep_first: float32 [1024, 1027], P(('tower', 'batch')), may hold values from -6.1035156e-05 to 6.1035156e-05
- deep_second: float32 [1024, 1027], P(('tower', 'batch')), may hold values from 8.789062e-12 to 3.515625e-11
- vectors: float32 [5130], replicated, may hold values from -0.3 to 0.3
- vector_first: float32 [5130], replicated, may hold values from -0.0007324219 to 0.0007324219
- vector_second: float32 [5130], replicated, may hold values from 1.373291e-09 to 5.493164e-09
Outputs:
- loss_sum: float32 [], replicated
- valid_count: float32 [], replicated
- cross_grad: float32 [2, 1027, 1027], P('tower')
- cross_first_new: float32 [2, 1027, 1027], P('tower')
- cross_second_new: float32 [2, 1027, 1027], P('tower')
- cross_new: float32 [2, 1027, 1027], P('tower')
- cross_copy: bfloat16 [2, 1027, 1027], P('tower')
- deep_grad: float32 [1024, 1027], P(('tower', 'batch'))
- deep_first_new: float32 [1024, 1027], P(('tower', 'batch'))
- deep_second_new: float32 [1024, 1027], P(('tower', 'batch'))
- deep_new: float32 [1024, 1027], P(('tower', 'batch'))
- deep_copy: bfloat16 [1024, 1027], P(('tower', 'batch'))
- table_grad: float32 [65536, 39], P(('tower', 'batch'))
- table_first_new: float32 [65536, 39], P(('tower', 'batch'))
- table_second_new: float32 [65536, 39], P(('tower', 'batch'))
- table_new: float32 [65536, 39], P(('tower', 'batch'))
- vector_grad: float32 [5130], replicated
- vector_first_new: float32 [5130], replicated
- vector_second_new: float32 [5130], replicated
- vector_new: float32 [5130], replicated
The draws below stay inside these ranges and needn't reach their ends.
Inputs may be any that keep to these rules, and one draw needn't show every extreme that they name: `category_ids`: in each aligned block of 512 examples, exactly 416 of its ids fall in each aligned block of 2048 table rows.
All inputs are finite; a program needn't handle non-finite values.
Results may differ from the reference program's by a relative error of at most 0.0075.
Values may be sent and summed in bfloat16 or wider, within the bound.
No kernel may reach another device: no remote copies, remote signals or barrier semaphores. Data moves between devices by JAX's collectives and lax.ppermute only.
A program may use at most 128 MiB of HBM per device.

```python
import math
import jax
import jax.numpy as jnp
from jax import lax

DENSE = 13
FEATS = 26
EMBED = 39
HIDDEN_SIZE = 1024
B_DEV = 1024
ROWS_DEV = 2048
STEP = 5
WIDTH = 1027
OWNERS = 32
EXAMPLES = 16384
VOCAB = 65536
VEC = 5130


def draw_category_ids(key, part):
    key = jax.random.fold_in(key, 11)
    half = B_DEV // 2
    lookups = half * FEATS
    blocks = EXAMPLES // half
    keys = jax.random.split(key, blocks)

    def one_block(block_key):
        perm_key, row_key = jax.random.split(block_key)
        owner = jax.random.permutation(perm_key, lookups) % OWNERS
        local = jax.random.randint(row_key, (lookups,), 0, ROWS_DEV)
        return (owner * ROWS_DEV + local).reshape(half, FEATS)
    return jax.vmap(one_block)(keys).reshape(EXAMPLES, FEATS).astype(jnp.int32)


def draw_valid_mask(key, part):
    key = jax.random.fold_in(key, 23)
    groups = EXAMPLES // B_DEV
    group = jnp.arange(EXAMPLES, dtype=jnp.int32) // B_DEV
    limit = 250 + 500 * group // (groups - 1)
    ticket = jax.random.randint(key, (EXAMPLES,), 0, 1000)
    return (ticket < limit).astype(jnp.int32)


def plant(values, own_key, least, largest):
    shape = values.shape
    index_at = [jax.random.randint(jax.random.fold_in(own_key, axis), (), 0, shape[axis]) for axis in range(len(shape))]
    values = values.at[tuple(index_at)].set(least)
    longest = shape.index(max(shape))
    index_at[longest] = (index_at[longest] + 1) % shape[longest]
    return values.at[tuple(index_at)].set(largest)


def block_levels(own_key, extent, cuts, least, top_value):
    gain, own = 1.0, jax.random.fold_in(own_key, 6)
    for axis_at, blocks in cuts:
        heights = jnp.exp(jax.random.uniform(jax.random.fold_in(own, axis_at), (blocks,), jnp.float32, least / len(cuts), top_value / len(cuts)))
        gain = gain * jnp.repeat(heights, extent[axis_at] // blocks).reshape([-1 if axis == axis_at else 1 for axis in range(len(extent))])
    return gain


def scatter_about(stream_key, dims, width, bound, shards=(), kind=jnp.bfloat16):
    entries = width * jax.random.normal(stream_key, dims, jnp.float32)
    if shards:
        entries = entries * block_levels(stream_key, dims, shards, -0.22, 0.18)
    return jnp.clip(entries, -bound, bound).astype(kind)


def setup_inputs(seed: int = 0) -> dict:
    streams_of = jax.random.split(jax.random.key(seed), 17)
    dense_feats = scatter_about(streams_of[0], (EXAMPLES, DENSE), 1.0, 6.0, ((0, 16),))
    category_ids = draw_category_ids(jax.random.fold_in(streams_of[16], 71), 0)
    labels = plant(jax.random.randint(streams_of[2], (EXAMPLES,), 0, 2), jax.random.fold_in(streams_of[2], 1), 0, 1).astype(jnp.int32)
    valid_mask = draw_valid_mask(jax.random.fold_in(streams_of[16], 71), 0)
    embed_table = scatter_about(streams_of[4], (VOCAB, EMBED), 0.5, 3.0, ((0, 32),), jnp.float32)
    table_first = scatter_about(streams_of[5], (VOCAB, EMBED), (0.0066 * (FEATS / (EXAMPLES * VOCAB)) ** 0.5), 5.7220458984375e-06, ((0, 32),), jnp.float32)
    table_second = jnp.clip(jnp.exp(math.log(3.486871707168715e-13) - 1.3862944 * jax.random.uniform(streams_of[6], (VOCAB, EMBED), jnp.float32) ** block_levels(streams_of[6], (VOCAB, EMBED), ((0, 32),), -0.2, 0.2)), 8.717179267921787e-14, 3.486871707168715e-13)
    cross_weight = scatter_about(streams_of[7], (2, WIDTH, WIDTH), WIDTH ** -0.5, 0.1875, ((0, 2),), jnp.float32)
    cross_first = scatter_about(streams_of[8], (2, WIDTH, WIDTH), (0.0033 / EXAMPLES ** 0.5), 0.00015258789, ((0, 2),), jnp.float32)
    cross_second = jnp.clip(jnp.exp(math.log(2.1972655639412864e-10) - 1.3862944 * jax.random.uniform(streams_of[9], (2, WIDTH, WIDTH), jnp.float32) ** block_levels(streams_of[9], (2, WIDTH, WIDTH), ((0, 2),), -0.2, 0.2)), 5.493163909853216e-11, 2.1972655639412864e-10)
    deep_weight = scatter_about(streams_of[10], (HIDDEN_SIZE, WIDTH), WIDTH ** -0.5, 0.1875, ((0, 32),), jnp.float32)
    deep_first = scatter_about(streams_of[11], (HIDDEN_SIZE, WIDTH), (0.0013 / EXAMPLES ** 0.5), 6.103515625e-05, ((0, 32),), jnp.float32)
    deep_second = jnp.clip(jnp.exp(math.log(3.5156249439394216e-11) - 1.3862944 * jax.random.uniform(streams_of[12], (HIDDEN_SIZE, WIDTH), jnp.float32) ** block_levels(streams_of[12], (HIDDEN_SIZE, WIDTH), ((0, 32),), -0.2, 0.2)), 8.789062359848554e-12, 3.5156249439394216e-11)
    vectors = scatter_about(streams_of[13], (VEC,), 0.05, 0.3, (), jnp.float32)
    vector_first = scatter_about(streams_of[14], (VEC,), (0.0165 / EXAMPLES ** 0.5), 0.0007324219, (), jnp.float32)
    vector_second = jnp.clip(jnp.exp(jax.random.uniform(streams_of[15], (VEC,), jnp.float32, math.log(1.3732910364439022e-09), math.log(5.493164145775609e-09))), 1.3732910364439022e-09, 5.493164145775609e-09)
    return {"dense_feats": dense_feats, "category_ids": category_ids, "labels": labels, "valid_mask": valid_mask, "embed_table": embed_table, "table_first": table_first, "table_second": table_second, "cross_weight": cross_weight, "cross_first": cross_first, "cross_second": cross_second, "deep_weight": deep_weight, "deep_first": deep_first, "deep_second": deep_second, "vectors": vectors, "vector_first": vector_first, "vector_second": vector_second}


@jax.custom_vjp
def low(v):
    return lax.optimization_barrier(v.astype(jnp.bfloat16)).astype(jnp.float32)

@jax.custom_vjp
def low_back(v):
    return v

def low_keep(v):
    return (low(v), None)

def low_pass(kept, grad):
    return (grad,)

def back_keep(v):
    return (v, None)

def back_low(kept, grad):
    return (low(grad),)
low.defvjp(low_keep, low_pass)
low_back.defvjp(back_keep, back_low)

def matmul(left, right):
    return jnp.dot(left, right, precision=lax.Precision.HIGHEST)

def forward(embed_table, cross_weight, deep_weight, vectors, dense, indices, target, valid, count):
    rows = low(embed_table)[indices].reshape(indices.shape[0], FEATS * EMBED)
    inputs = jnp.concatenate([dense, rows], axis=1)
    cross_bias = vectors[:2 * WIDTH].reshape(2, WIDTH)
    deep_bias = vectors[2 * WIDTH:2 * WIDTH + HIDDEN_SIZE]
    head_cross = vectors[2 * WIDTH + HIDDEN_SIZE:3 * WIDTH + HIDDEN_SIZE]
    head_deep = vectors[3 * WIDTH + HIDDEN_SIZE:3 * WIDTH + 2 * HIDDEN_SIZE]
    head_bias = vectors[3 * WIDTH + 2 * HIDDEN_SIZE]
    cross_low = low(cross_weight)
    pre_first = low_back(matmul(inputs, cross_low[0]) + cross_bias[0])
    layer_one = inputs * pre_first + inputs
    pre_second = low_back(matmul(low(layer_one), cross_low[1]) + cross_bias[1])
    layer_two = inputs * pre_second + layer_one
    hidden = jax.nn.silu(low_back(matmul(inputs, low(deep_weight).T) + deep_bias))
    logit = matmul(low(layer_two), low(head_cross)) + matmul(low(hidden), low(head_deep)) + head_bias
    total = jnp.sum(valid * (jax.nn.softplus(logit) - target * logit))
    return (total / count, total)

def adamw(weight, grad, first, second, rate):
    first_new = 0.9 * first + 0.1 * grad
    second_new = 0.999 * second + 0.001 * grad * grad
    update = first_new / (1.0 - 0.9 ** STEP) / (jnp.sqrt(second_new / (1.0 - 0.999 ** STEP)) + 1e-08) + 0.01 * weight
    return (first_new, second_new, weight - rate * update)

def reference(dense_feats, category_ids, labels, valid_mask, embed_table, table_first, table_second, cross_weight, cross_first, cross_second, deep_weight, deep_first, deep_second, vectors, vector_first, vector_second):
    dense = dense_feats.astype(jnp.float32)
    target = labels.astype(jnp.float32)
    valid = valid_mask.astype(jnp.float32)
    count = jnp.sum(valid)

    def scaled(table_arg, cross_arg, deep_arg, vector_arg):
        return forward(table_arg, cross_arg, deep_arg, vector_arg, dense, category_ids, target, valid, count)
    loss_mean, vjp_fn, total = jax.vjp(scaled, embed_table, cross_weight, deep_weight, vectors, has_aux=True)
    table_grad, cross_grad, deep_grad, vector_grad = vjp_fn(jnp.float32(1.0))
    cross_one, cross_two, cross_new = adamw(cross_weight, cross_grad, cross_first, cross_second, 0.03)
    deep_one, deep_two, deep_new = adamw(deep_weight, deep_grad, deep_first, deep_second, 0.03)
    table_one, table_two, table_new = adamw(embed_table, table_grad, table_first, table_second, 0.25)
    vector_one, vector_two, vector_new = adamw(vectors, vector_grad, vector_first, vector_second, 0.03)
    return (total, count, cross_grad, cross_one, cross_two, cross_new, cross_new.astype(jnp.bfloat16), deep_grad, deep_one, deep_two, deep_new, deep_new.astype(jnp.bfloat16), table_grad, table_one, table_two, table_new, vector_grad, vector_one, vector_two, vector_new)
```

```python
import functools

import jax
import jax.numpy as jnp
from jax import lax
from jax.experimental import pallas as pl
from jax.experimental.pallas import tpu as pltpu
from jax.sharding import PartitionSpec as P

STEP = 5
LANES = 128
UNROLL = 64
BF16 = jnp.bfloat16
F32 = jnp.float32


def round_up(value, unit):
    return -(-value // unit) * unit


def adamw(weight, grad, first, second, rate):
    first_new = 0.9 * first + 0.1 * grad
    second_new = 0.999 * second + 0.001 * grad * grad
    update = (
        first_new / (1.0 - 0.9**STEP) / (jnp.sqrt(second_new / (1.0 - 0.999**STEP)) + 1e-08)
        + 0.01 * weight
    )
    return (first_new, second_new, weight - rate * update)


def contract(left, right, left_dim, right_dim):
    return lax.dot_general(
        left, right, (((left_dim,), (right_dim,)), ((), ())), preferred_element_type=F32
    )


def iota(shape, dim):
    return lax.broadcasted_iota(jnp.int32, shape, dim)


def in_vmem():
    return pl.BlockSpec(memory_space=pltpu.VMEM)


def in_smem():
    return pl.BlockSpec(memory_space=pltpu.SMEM)


def params(mib):
    return pltpu.CompilerParams(vmem_limit_bytes=mib * 2**20)


def slots_kernel(shift, slots, stride, ids_ref, valid_ref, asked_ref, place_ref):
    feats, half = ids_ref.shape
    owners = asked_ref.shape[0]
    before = (iota((half, half), 0) < iota((half, half), 1)).astype(BF16)
    owner_of = iota((owners, half), 0)
    slot_of = iota((slots, half), 0)
    base = jnp.zeros((owners, 1), F32)
    total = jnp.zeros((slots, 2 * owners), F32)
    for feat in range(feats):
        ids = ids_ref[feat : feat + 1, :]
        owner = lax.shift_right_logical(ids, shift)
        row = ids & ((1 << shift) - 1)
        hit = (owner_of == owner).astype(F32)
        earlier = contract(hit.astype(BF16), before, 1, 0) + base
        rank = jnp.sum(hit * earlier, axis=0, keepdims=True)
        base = base + jnp.sum(hit, axis=1, keepdims=True)
        rank = rank.astype(jnp.int32)
        spot = owner * stride + rank
        for k in range(half // LANES):
            at = feat * (half // LANES) + k
            place_ref[at : at + 1, :] = spot[:, k * LANES : k * LANES + LANES]
        high = lax.shift_right_logical(row, 8).astype(F32)
        low = (row & 255).astype(F32)
        values = jnp.concatenate([hit * high, hit * low], axis=0).astype(BF16)
        put = (slot_of == rank).astype(F32).astype(BF16)
        total = total + contract(put, values, 1, 1)
    rows = total[:, :owners] * 256.0 + total[:, owners:]
    tall = round_up(slots, LANES)
    if tall > slots:
        rows = jnp.concatenate([rows, jnp.zeros((tall - slots, owners), F32)], axis=0)
    count = jnp.sum(valid_ref[...])
    wide = asked_ref.shape[1]
    flat = rows.T
    if wide > tall:
        flat = jnp.concatenate([flat, jnp.zeros((owners, wide - tall), F32)], axis=1)
    asked_ref[...] = jnp.where(iota((owners, wide), 1) < slots, flat.astype(jnp.int32), count)


def lookup_kernel(slots, stride, ids_ref, table_ref, rows_ref, blocks_ref):
    embed, rows_own = table_ref.shape
    tall = round_up(embed, 8)
    parts = rows_own // 256
    wide = ids_ref.shape[1]
    third = stride // 3
    blocks_ref[...] = jnp.zeros_like(blocks_ref)
    for part in range(parts):
        blocks_ref[part * tall : part * tall + embed, :] = table_ref[:, part * 256 : part * 256 + 256]
    blocks = blocks_ref[...].astype(BF16)
    low_of = iota((256, wide), 0)

    def step(owner, carry):
        ids = ids_ref[pl.ds(owner, 1), :]
        high = lax.shift_right_logical(ids, 8)
        pick = (low_of == (ids & 255)).astype(F32).astype(BF16)
        found = contract(blocks, pick, 1, 0)
        mine = jnp.zeros((tall, wide), F32)
        for part in range(parts):
            mine = jnp.where(high == part, found[part * tall : part * tall + tall], mine)
        square = jnp.concatenate([mine, jnp.zeros((LANES - tall, wide), F32)], axis=0).T
        packed = square[:third]
        for piece in (1, 2):
            packed = packed + pltpu.roll(square[piece * third : piece * third + third], embed * piece, 1)
        rows_ref[pl.ds(pl.multiple_of(owner * third, 16), third), :] = packed.astype(BF16)
        return carry

    lax.fori_loop(0, ids_ref.shape[0], step, 0)


def column_map(feat, dense_width, embed):
    start = dense_width + embed * feat
    tile = start // LANES
    lane = iota((LANES, 2 * LANES), 0)
    column = iota((LANES, 2 * LANES), 1)
    hit = (column == lane + (start - tile * LANES)) & (lane < embed)
    return tile * LANES, hit.astype(F32).astype(BF16)


def inputs_kernel(feats, stride, embed, dense_width, place_ref, rows_ref, dense_ref, x_ref, far_ref, near_ref, sum_ref):
    half = near_ref.shape[0]
    third = stride // 3
    width = dense_width + embed * feats

    def unpack(owner, carry):
        block = rows_ref[pl.ds(pl.multiple_of(owner * third, 16), third), :].astype(F32)
        for piece in range(3):
            rolled = block if piece == 0 else pltpu.roll(block, LANES - embed * piece, 1)
            far_ref[pl.ds(pl.multiple_of(owner * stride + piece * third, 16), third), :] = rolled
        return carry

    lax.fori_loop(0, far_ref.shape[0] // stride, unpack, 0)
    sum_ref[...] = jnp.zeros_like(sum_ref)
    sum_ref[:, :LANES] = dense_ref[...].astype(F32)
    ones = width - width // LANES * LANES
    end = slice(width // LANES * LANES, width // LANES * LANES + LANES)
    sum_ref[:, end] += (iota((half, LANES), 1) == ones).astype(F32)
    for feat in range(feats):

        def fetch(at, carry):
            start = pl.multiple_of(at * UNROLL, UNROLL)
            window = near_ref.at[pl.ds(start, UNROLL), :]
            rows = [far_ref[pl.ds(place_ref[feat * half + start + k], 1), :] for k in range(UNROLL)]
            for k in range(UNROLL):
                window[k : k + 1, :] = rows[k]
            return carry

        lax.fori_loop(0, half // UNROLL, fetch, 0)
        start, spread = column_map(feat, dense_width, embed)
        sum_ref[:, start : start + 2 * LANES] += contract(near_ref[...].astype(BF16), spread, 1, 0)
    x_ref[...] = sum_ref[...].astype(BF16)


def send_kernel(feats, slots, stride, embed, dense_width, place_ref, dx_ref, rows_ref, far_ref, near_ref):
    half = near_ref.shape[0]
    third = stride // 3
    owners = far_ref.shape[0] // stride

    def clear(owner, carry):
        gap = stride - slots
        far_ref[pl.ds(pl.multiple_of(owner * stride + slots, 8), gap), :] = jnp.zeros((gap, LANES), F32)
        return carry

    lax.fori_loop(0, owners, clear, 0)
    for feat in range(feats):
        start, spread = column_map(feat, dense_width, embed)
        near_ref[...] = contract(dx_ref[:, start : start + 2 * LANES], spread, 1, 1)

        def put(at, carry):
            begin = pl.multiple_of(at * UNROLL, UNROLL)
            window = near_ref.at[pl.ds(begin, UNROLL), :]
            rows = [window[k : k + 1, :] for k in range(UNROLL)]
            for k in range(UNROLL):
                far_ref[pl.ds(place_ref[feat * half + begin + k], 1), :] = rows[k]
            return carry

        lax.fori_loop(0, half // UNROLL, put, 0)

    def pack(owner, carry):
        packed = jnp.zeros((third, LANES), F32)
        for piece in range(3):
            block = far_ref[pl.ds(pl.multiple_of(owner * stride + piece * third, 8), third), :]
            packed = packed + (block if piece == 0 else pltpu.roll(block, embed * piece, 1))
        rows_ref[pl.ds(pl.multiple_of(owner * third, 16), third), :] = packed.astype(BF16)
        return carry

    lax.fori_loop(0, owners, pack, 0)


def table_kernel(
    slots, stride, ids_ref, rows_ref, table_ref, first_ref, second_ref,
    grad_ref, first_new_ref, second_new_ref, table_new_ref, total_ref,
):
    embed, rows_own = table_ref.shape
    tall = round_up(embed, 8)
    parts = rows_own // 256
    wide = ids_ref.shape[1]
    third = stride // 3
    low_of = iota((256, wide), 0)
    lane = iota((1, wide), 1)
    total_ref[...] = jnp.zeros_like(total_ref)

    def step(owner, carry):
        ids = jnp.where(lane < slots, ids_ref[pl.ds(owner, 1), :], -1)
        high = lax.shift_right_arithmetic(ids, 8)
        pick = (low_of == (ids & 255)).astype(F32).astype(BF16)
        block = rows_ref[pl.ds(pl.multiple_of(owner * third, 16), third), :].astype(F32)
        pieces = [block if k == 0 else pltpu.roll(block, LANES - embed * k, 1) for k in range(3)]
        if wide > stride:
            pieces.append(jnp.zeros((wide - stride, LANES), F32))
        square = jnp.concatenate(pieces, axis=0)[:wide].T
        mine = jnp.where(iota((tall, wide), 0) < embed, square[:tall], 0.0)
        spread = [jnp.where(high == part, mine, 0.0) for part in range(parts)]
        total_ref[...] += contract(jnp.concatenate(spread, axis=0).astype(BF16), pick, 1, 1)
        return carry

    lax.fori_loop(0, ids_ref.shape[0], step, 0)
    for part in range(parts):
        here = slice(part * 256, part * 256 + 256)
        grad = total_ref[part * tall : part * tall + embed, :]
        one, two, new = adamw(table_ref[:, here], grad, first_ref[:, here], second_ref[:, here], 0.25)
        grad_ref[:, here] = grad
        first_new_ref[:, here] = one
        second_new_ref[:, here] = two
        table_new_ref[:, here] = new


def tiles(size):
    return [(at, min(256, size - at)) for at in range(0, size, 256)]


def towers_kernel(
    count_ref, bias_ref, x_ref, first_ref, second_ref, deep_ref, vec_ref, target_ref, valid_ref,
    one_ref, d_second_ref, d_first_ref, d_deep_ref, dx_ref, head_ref,
    pre_first_ref, layer_ref, pre_second_ref, two_ref, slope_ref, hidden_ref,
):
    half, wide = x_ref.shape
    hidden = deep_ref.shape[0]

    def lanes(x):
        total = x[:, :LANES]
        for at in range(LANES, x.shape[1], LANES):
            total = total + x[:, at : at + LANES]
        return total

    for at, size in tiles(wide):
        here = slice(at, at + size)
        base = x_ref[:, here].astype(F32)
        pre = contract(x_ref[...], first_ref[:, here], 1, 0) + vec_ref[0:1, here]
        layer = base * pre + base
        pre_first_ref[:, here] = pre
        layer_ref[:, here] = layer
        one_ref[:, here] = layer.astype(BF16)
    score = jnp.zeros((half, LANES), F32)
    for at, size in tiles(wide):
        here = slice(at, at + size)
        base = x_ref[:, here].astype(F32)
        pre = contract(one_ref[...], second_ref[:, here], 1, 0) + vec_ref[1:2, here]
        two = (base * pre + layer_ref[:, here]).astype(BF16)
        pre_second_ref[:, here] = pre
        two_ref[:, here] = two
        score = score + lanes(two.astype(F32) * vec_ref[3:4, here])
    for at, size in tiles(hidden):
        here = slice(at, at + size)
        pre = contract(x_ref[...], deep_ref[here, :], 1, 1) + vec_ref[2:3, here]
        gate = jax.nn.sigmoid(pre)
        out = (pre * gate).astype(BF16)
        hidden_ref[:, here] = out
        slope_ref[:, here] = gate * (1.0 + pre * (1.0 - gate))
        score = score + lanes(out.astype(F32) * vec_ref[4:5, here])
    logit = jnp.sum(score, axis=1, keepdims=True) + bias_ref[0, 0]
    target, valid = target_ref[...], valid_ref[...]
    softplus = jnp.maximum(logit, 0.0) + jnp.log1p(jnp.exp(-jnp.abs(logit)))
    loss = jnp.sum(valid * (softplus - target * logit), axis=0, keepdims=True)
    d_logit = valid * (jax.nn.sigmoid(logit) - target) / count_ref[0, 0]
    bias_grad = jnp.sum(d_logit, axis=0, keepdims=True)
    lane = iota((1, wide), 1)
    head_ref[...] = jnp.zeros_like(head_ref)
    head_ref[2:3, :] = jnp.where(lane == 0, bias_grad, jnp.where(lane == 1, loss, 0.0))
    for at, size in tiles(wide):
        here = slice(at, at + size)
        base = x_ref[:, here].astype(F32)
        d_second_ref[:, here] = (d_logit * vec_ref[3:4, here] * base).astype(BF16)
        head_ref[0:1, here] = jnp.sum(d_logit * two_ref[:, here].astype(F32), axis=0, keepdims=True)
    for at, size in tiles(hidden):
        here = slice(at, at + size)
        d_deep_ref[:, here] = (d_logit * vec_ref[4:5, here] * slope_ref[:, here]).astype(BF16)
        head_ref[1:2, here] = jnp.sum(d_logit * hidden_ref[:, here].astype(F32), axis=0, keepdims=True)
    for at, size in tiles(wide):
        here = slice(at, at + size)
        base = x_ref[:, here].astype(F32)
        d_two = d_logit * vec_ref[3:4, here]
        d_one = contract(d_second_ref[...], second_ref[here, :], 1, 1) + d_two
        d_first_ref[:, here] = (d_one * base).astype(BF16)
        layer_ref[:, here] = d_one * (1.0 + pre_first_ref[:, here]) + d_two * pre_second_ref[:, here]
    for at, size in tiles(wide):
        here = slice(at, at + size)
        dx = contract(d_first_ref[...], first_ref[here, :], 1, 1) + contract(d_deep_ref[...], deep_ref[:, here], 1, 0)
        dx_ref[:, here] = (dx + layer_ref[:, here]).astype(BF16)


def grads_kernel(
    deep_rows, core_ref, x_ref, one_ref, d_second_ref, d_first_ref, d_deep_ref, head_ref,
    keep_ref, give_ref, rest_ref, turned_ref,
):
    half, wide = x_ref.shape
    hidden = d_deep_ref.shape[1]
    towers, groups, pairs, rows, main = keep_ref.shape
    rows_c = rows - deep_rows
    even = core_ref[0, 0] == 0

    def share(value, tower, at, size, chunk, first):
        for group in range(groups):
            for pair in range(pairs):
                start = (group * pairs + pair) * 2 * chunk
                low, high = value[start : start + chunk], value[start + chunk : start + 2 * chunk]
                keep_ref[tower, group, pair, first : first + chunk, at : at + size] = jnp.where(even, low, high).astype(BF16)
                give_ref[tower, group, pair, first : first + chunk, at : at + size] = jnp.where(even, high, low).astype(BF16)

    rest_ref[...] = jnp.zeros_like(rest_ref)
    for tower, (left, right) in enumerate(((one_ref, d_second_ref), (x_ref, d_first_ref))):
        tower = 1 - tower
        turned_ref[...] = left[...].T
        for at, size in tiles(main):
            value = contract(turned_ref[...], right[:, at : at + size], 1, 0)
            share(value, tower, at, size, rows_c, 0)
            rest_ref[8 * tower : 8 * tower + 4, at : at + size] = value[main : main + 4]
        value = contract(turned_ref[...], right[:, main:wide], 1, 0)
        rest_ref[8 * tower : 8 * tower + 4, main:wide] = value[main : main + 4]
        rest_ref[8 * tower + 4 : 8 * tower + 7, :main] = value[:main].T[:3]
    bias = contract(turned_ref[main:wide, :], d_deep_ref[...], 1, 0)
    rest_ref[16:20, :hidden] = bias[:4]
    rest_ref[20:23, :] = head_ref[0:3, :]
    turned_ref[:hidden, :] = d_deep_ref[...].T
    for at, size in tiles(main):
        value = contract(turned_ref[:hidden, :], x_ref[:, at : at + size], 1, 0)
        for tower in range(towers):
            share(value[tower * (hidden // towers) : (tower + 1) * (hidden // towers)], tower, at, size, deep_rows, rows_c)


def cross_kernel(
    place_ref, near_ref, far_ref, rest_ref, weight_ref, first_ref, second_ref,
    grad_ref, first_new_ref, second_new_ref, new_ref, copy_ref,
):
    block = pl.program_id(0)
    width = weight_ref.shape[2]
    main = near_ref.shape[3]
    rows = 2 * near_ref.shape[2]
    even = (place_ref[0] & 1) == 0
    near, far = near_ref[0, 0].astype(F32), far_ref[0, 0].astype(F32)
    body = jnp.concatenate([jnp.where(even, near, far), jnp.where(even, far, near)], axis=0)
    lane = pl.multiple_of(jnp.minimum(block * rows, main - rows) // LANES * LANES, LANES)
    side = rest_ref[0, :, pl.ds(lane, LANES)]
    side = jnp.concatenate([side, jnp.zeros((LANES - 8, LANES), F32)], axis=0).T
    if rows < LANES:
        parts = [side[at : at + rows] for at in range(0, LANES, rows)]
        side = parts[0]
        for k, part in enumerate(parts):
            side = jnp.where(block % len(parts) == k, part, side)
    side = pltpu.roll(side, LANES - 4, 1)
    grad = jnp.concatenate([body, side], axis=1)
    last = jnp.concatenate([rest_ref[0], jnp.zeros((rows - 8, rest_ref.shape[2]), F32)], axis=0)
    grad = jnp.where(block == pl.num_programs(0) - 1, last, grad)[:, :width]
    one, two, new = adamw(weight_ref[:, 0, :], grad, first_ref[:, 0, :], second_ref[:, 0, :], 0.03)
    grad_ref[:, 0, :] = grad
    first_new_ref[:, 0, :] = one
    second_new_ref[:, 0, :] = two
    new_ref[:, 0, :] = new
    copy_ref[...] = new.astype(BF16)


def flip(x, axis, bit, size):
    return lax.ppermute(x, axis, [(i, i ^ bit) for i in range(size)])


def pick(x, axis, index):
    return lax.dynamic_index_in_dim(x, index, axis, keepdims=False)


def join(mine, other, axis, index):
    return jnp.where(index == 0, jnp.stack([mine, other], axis), jnp.stack([other, mine], axis))


def flip_far(x, batch, groups):
    return jnp.stack([x] + [flip(x, "batch", k * 4, batch) for k in range(1, groups)])


def in_order(parts, groups):
    far = lax.axis_index("batch") // 4
    return jnp.stack([pick(parts, 0, k ^ far) for k in range(groups)])


def local(
    dense_feats,
    category_ids,
    labels,
    valid_mask,
    embed_table,
    table_first,
    table_second,
    cross_weight,
    cross_first,
    cross_second,
    deep_weight,
    deep_first,
    deep_second,
    vectors,
    vector_first,
    vector_second,
):
    towers, batch = lax.axis_size("tower"), lax.axis_size("batch")
    owners = towers * batch
    tower, place = lax.axis_index("tower"), lax.axis_index("batch")
    core, near, far = place & 1, (place >> 1) & 1, place >> 2
    groups = batch // 4
    rows_own, embed = embed_table.shape
    examples, feats = category_ids.shape
    half = examples // towers
    width = cross_weight.shape[1]
    deep_rows = deep_weight.shape[0]
    hidden = deep_rows * owners
    dense_width = dense_feats.shape[1]
    wide = round_up(width, LANES)
    slots = half * feats // owners
    third = round_up(-(-slots // 3), 16)
    stride = 3 * third
    shift = rows_own.bit_length() - 1
    asked_wide = round_up(max(slots + 1, stride), LANES)

    def mine(x, dim):
        return lax.dynamic_slice_in_dim(x, tower * half, half, dim)

    ids = mine(category_ids.T, 1)
    valid = mine(valid_mask, 0)
    target = mine(labels, 0).astype(F32)
    dense = jnp.pad(mine(dense_feats, 0), ((0, 0), (0, LANES - dense_width)))

    asked, slot = pl.pallas_call(
        functools.partial(slots_kernel, shift, slots, stride),
        out_shape=(
            jax.ShapeDtypeStruct((owners, asked_wide), jnp.int32),
            jax.ShapeDtypeStruct((feats * half // LANES, LANES), jnp.int32),
        ),
        in_specs=[in_vmem()] * 2,
        out_specs=(in_vmem(), in_vmem()),
        compiler_params=params(32),
        name="slots",
    )(ids, valid.reshape(1, half))
    slot = slot.reshape(-1)
    arrived = lax.all_to_all(asked, ("tower", "batch"), split_axis=0, concat_axis=0, tiled=True)
    count = jnp.sum(arrived[:, slots]).astype(F32)
    table_t = embed_table.T
    found = pl.pallas_call(
        functools.partial(lookup_kernel, slots, stride),
        out_shape=jax.ShapeDtypeStruct((owners * third, LANES), BF16),
        in_specs=[in_vmem()] * 2,
        out_specs=in_vmem(),
        scratch_shapes=[pltpu.VMEM((rows_own // 256 * round_up(embed, 8), 256), F32)],
        compiler_params=params(32),
        name="lookup",
    )(arrived, table_t)
    returned = lax.all_to_all(found, ("tower", "batch"), split_axis=0, concat_axis=0, tiled=True)
    inputs = pl.pallas_call(
        functools.partial(inputs_kernel, feats, stride, embed, dense_width),
        out_shape=jax.ShapeDtypeStruct((half, wide), BF16),
        in_specs=[in_smem(), in_vmem(), in_vmem()],
        out_specs=in_vmem(),
        scratch_shapes=[
            pltpu.VMEM((owners * stride, LANES), F32),
            pltpu.VMEM((half, LANES), F32),
            pltpu.VMEM((half, wide), F32),
        ],
        compiler_params=params(48),
        name="inputs",
    )(slot, returned, dense)

    own_low = jnp.pad(cross_weight[0].astype(BF16), ((0, wide - width), (0, wide - width)))
    halves = own_low.reshape(2, wide // 2, wide)
    got = flip(pick(halves, 0, core), "tower", 1, towers)
    other_low = join(got, flip(got, "batch", 1, batch), 0, core).reshape(wide, wide)
    cross_low = (
        jnp.where(tower == 0, own_low, other_low),
        jnp.where(tower == 0, other_low, own_low),
    )
    deep_own = jnp.pad(deep_weight.astype(BF16), ((0, 0), (0, wide - width)))
    deep_low = in_order(flip_far(deep_own, batch, groups), groups)
    deep_low = join(deep_low, flip(deep_low, "batch", 2, batch), 1, near)
    deep_low = join(deep_low, flip(deep_low, "tower", 1, towers), 0, tower)
    deep_low = join(deep_low, flip(deep_low, "batch", 1, batch), 3, core).reshape(hidden, wide)

    def widen(x):
        return jnp.pad(x, (0, wide - x.shape[0]))

    vec = jnp.stack(
        [
            widen(vectors[:width]),
            widen(vectors[width : 2 * width]),
            widen(vectors[2 * width : 2 * width + hidden]),
            widen(vectors[2 * width + hidden : 3 * width + hidden]).astype(BF16).astype(F32),
            widen(vectors[3 * width + hidden : 3 * width + 2 * hidden]).astype(BF16).astype(F32),
        ]
        + [jnp.zeros((wide,), F32)] * 3
    )
    low = jax.ShapeDtypeStruct((half, wide), BF16)
    low_deep = jax.ShapeDtypeStruct((half, hidden), BF16)
    one_low, d_second, d_first, d_deep, d_inputs, heads = pl.pallas_call(
        towers_kernel,
        out_shape=(low, low, low, low_deep, low, jax.ShapeDtypeStruct((8, wide), F32)),
        in_specs=[in_smem()] * 2 + [in_vmem()] * 7,
        out_specs=(in_vmem(),) * 6,
        scratch_shapes=[
            pltpu.VMEM((half, wide), F32),
            pltpu.VMEM((half, wide), F32),
            pltpu.VMEM((half, wide), F32),
            pltpu.VMEM((half, wide), BF16),
            pltpu.VMEM((half, hidden), F32),
            pltpu.VMEM((half, hidden), BF16),
        ],
        compiler_params=params(56),
        name="towers",
    )(
        count.reshape(1, 1), vectors[-1:].reshape(1, 1), inputs, cross_low[0], cross_low[1], deep_low, vec,
        target.reshape(half, 1), valid.astype(F32).reshape(half, 1),
    )
    main = width // LANES * LANES
    rows_c = main // batch
    parts = jax.ShapeDtypeStruct((towers, groups, 2, rows_c + deep_rows, main), BF16)
    keep, give, rest = pl.pallas_call(
        functools.partial(grads_kernel, deep_rows),
        out_shape=(parts, parts, jax.ShapeDtypeStruct((24, wide), F32)),
        in_specs=[in_smem()] + [in_vmem()] * 6,
        out_specs=(in_vmem(),) * 3,
        scratch_shapes=[pltpu.VMEM((wide, half), BF16)],
        compiler_params=params(56),
        name="grads",
    )(core.reshape(1, 1), inputs, one_low, d_second, d_first, d_deep, heads)
    got = flip(give, "batch", 1, batch)

    sent = pl.pallas_call(
        functools.partial(send_kernel, feats, slots, stride, embed, dense_width),
        out_shape=jax.ShapeDtypeStruct((owners * third, LANES), BF16),
        in_specs=[in_smem(), in_vmem()],
        out_specs=in_vmem(),
        scratch_shapes=[
            pltpu.VMEM((owners * stride, LANES), F32),
            pltpu.VMEM((half, LANES), F32),
        ],
        compiler_params=params(48),
        name="send",
    )(slot, d_inputs)
    back = lax.all_to_all(sent, ("tower", "batch"), split_axis=0, concat_axis=0, tiled=True)
    shape_t = jax.ShapeDtypeStruct((embed, rows_own), F32)
    table_grad, table_one, table_two, table_new = pl.pallas_call(
        functools.partial(table_kernel, slots, stride),
        out_shape=(shape_t,) * 4,
        in_specs=[in_vmem()] * 5,
        out_specs=(in_vmem(),) * 4,
        scratch_shapes=[pltpu.VMEM((rows_own // 256 * round_up(embed, 8), 256), F32)],
        compiler_params=params(32),
        name="table",
    )(arrived, back, table_t, table_first.T, table_second.T)

    for bit in [1, 2] + [4 << k for k in range(groups.bit_length() - 1)]:
        rest = rest + flip(rest, "batch", bit, batch)
    rest = rest + flip(rest, "tower", 1, towers)

    mid = groups // 2
    other, beyond = 1 - tower, 1 - near
    keep_one, got_one, keep_two, got_two = keep[:, :mid], got[:, :mid], keep[:, mid:], got[:, mid:]
    from_tower = flip(pick(keep_one, 0, other) + pick(got_one, 0, other), "tower", 1, towers)
    from_near = flip(pick(keep_two, 2, beyond) + pick(got_two, 2, beyond), "batch", 2, batch)
    one = pick(keep_one, 0, tower) + pick(got_one, 0, tower) + from_tower
    two = pick(keep_two, 2, near) + pick(got_two, 2, near) + from_near
    one = pick(one, 1, near) + flip(pick(one, 1, beyond), "batch", 2, batch)
    two = pick(two, 0, tower) + flip(pick(two, 0, other), "tower", 1, towers)
    both = jnp.concatenate([one, two], axis=0)
    summed = pick(both, 0, far).astype(F32)
    for k in range(1, groups):
        summed = summed + flip(pick(both, 0, far ^ k), "batch", k * 4, batch).astype(F32)
    tail = lax.dynamic_slice_in_dim(rest[16 : 16 + width - main], (tower * batch + place) * deep_rows, deep_rows, 1)
    deep_grad = jnp.concatenate([summed[rows_c:], tail.T], axis=1)
    chunk = flip_far(summed[:rows_c].astype(BF16), batch, groups)
    chunk = jnp.stack([chunk, flip(chunk, "batch", 2, batch)])
    partner = flip(chunk, "batch", 1, batch)
    side = pick(rest[:16].reshape(2, 8, wide), 0, tower)[None]
    blocks = batch // 2
    rows = 2 * rows_c

    def relative(block, at):
        other = jnp.minimum(block, blocks - 1) ^ (at[0] >> 1)
        return (other & 1, other >> 1, 0, 0)

    piece = pl.BlockSpec((1, 1, rows_c, main), relative)
    slab = pl.BlockSpec((rows, 1, width), lambda block, at: (block, 0, 0))
    shape_c = jax.ShapeDtypeStruct((width, 1, width), F32)
    cross_out = pl.pallas_call(
        cross_kernel,
        grid_spec=pltpu.PrefetchScalarGridSpec(
            num_scalar_prefetch=1,
            grid=(blocks + 1,),
            in_specs=[piece, piece, pl.BlockSpec((1, 8, wide), lambda block, at: (0, 0, 0)), slab, slab, slab],
            out_specs=(slab, slab, slab, slab, pl.BlockSpec((rows, width), lambda block, at: (block, 0))),
        ),
        out_shape=(shape_c,) * 4 + (jax.ShapeDtypeStruct((width, width), BF16),),
        compiler_params=params(48),
        name="cross",
    )(
        place.reshape(1), chunk, partner, side,
        cross_weight.transpose(1, 0, 2), cross_first.transpose(1, 0, 2), cross_second.transpose(1, 0, 2),
    )
    cross_grad, cross_one, cross_two, cross_new = (x.transpose(1, 0, 2) for x in cross_out[:4])
    vector_grad = jnp.concatenate(
        [rest[3, :width], rest[11, :width], rest[19, :hidden], rest[20, :width], rest[21, :hidden], rest[22, :1]]
    )
    loss_sum = rest[22, 1]
    deep_one, deep_two, deep_new = adamw(deep_weight, deep_grad, deep_first, deep_second, 0.03)
    vector_one, vector_two, vector_new = adamw(vectors, vector_grad, vector_first, vector_second, 0.03)
    return (
        loss_sum,
        count,
        cross_grad,
        cross_one,
        cross_two,
        cross_new,
        cross_out[4][None],
        deep_grad,
        deep_one,
        deep_two,
        deep_new,
        deep_new.astype(BF16),
        table_grad.T,
        table_one.T,
        table_two.T,
        table_new.T,
        vector_grad,
        vector_one,
        vector_two,
        vector_new,
    )


def solution(mesh):
    both = P(("tower", "batch"), None)
    cross = P("tower", None, None)
    return jax.shard_map(
        local,
        mesh=mesh,
        in_specs=(
            P("batch", None),
            P("batch", None),
            P("batch"),
            P("batch"),
            both,
            both,
            both,
            cross,
            cross,
            cross,
            both,
            both,
            both,
            P(),
            P(),
            P(),
        ),
        out_specs=(P(), P()) + (cross,) * 5 + (both,) * 9 + (P(),) * 4,
        check_vma=False,
    )
```

```python
import functools

import jax
import jax.numpy as jnp
from jax import lax
from jax.experimental import pallas as pl
from jax.experimental.pallas import tpu as pltpu
from jax.sharding import PartitionSpec as P

STEP = 5
LANES = 128
CHUNK = 128
BF16 = jnp.bfloat16
F32 = jnp.float32


def round_up(value, unit):
    return -(-value // unit) * unit


def adamw(weight, grad, first, second, rate):
    first_new = 0.9 * first + 0.1 * grad
    second_new = 0.999 * second + 0.001 * grad * grad
    update = (
        first_new / (1.0 - 0.9**STEP) / (jnp.sqrt(second_new / (1.0 - 0.999**STEP)) + 1e-08)
        + 0.01 * weight
    )
    return (first_new, second_new, weight - rate * update)


def contract(left, right, left_dim, right_dim):
    return lax.dot_general(
        left, right, (((left_dim,), (right_dim,)), ((), ())), preferred_element_type=F32
    )


def iota(shape, dim):
    return lax.broadcasted_iota(jnp.int32, shape, dim)


def in_vmem():
    return pl.BlockSpec(memory_space=pltpu.VMEM)


def in_smem():
    return pl.BlockSpec(memory_space=pltpu.SMEM)


def params(mib):
    return pltpu.CompilerParams(vmem_limit_bytes=mib * 2**20)


def takes(micros):
    return pl.CostEstimate(flops=0, bytes_accessed=micros * 3_000_000, transcendentals=0)


def slots_kernel(shift, slots, stride, ids_ref, valid_ref, asked_ref, place_ref):
    feats, half = ids_ref.shape
    owners = asked_ref.shape[0]
    before = (iota((half, half), 0) < iota((half, half), 1)).astype(BF16)
    owner_of = iota((owners, half), 0)
    slot_of = iota((slots, half), 0)
    base = jnp.zeros((owners, 1), F32)
    total = jnp.zeros((slots, 2 * owners), F32)
    for feat in range(feats):
        ids = ids_ref[feat : feat + 1, :]
        owner = lax.shift_right_logical(ids, shift)
        row = ids & ((1 << shift) - 1)
        hit = (owner_of == owner).astype(F32)
        earlier = contract(hit.astype(BF16), before, 1, 0) + base
        rank = jnp.sum(hit * earlier, axis=0, keepdims=True)
        base = base + jnp.sum(hit, axis=1, keepdims=True)
        rank = rank.astype(jnp.int32)
        spot = owner * stride + rank
        for k in range(half // LANES):
            at = feat * (half // LANES) + k
            place_ref[at : at + 1, :] = spot[:, k * LANES : k * LANES + LANES]
        high = lax.shift_right_logical(row, 8).astype(F32)
        low = (row & 255).astype(F32)
        values = jnp.concatenate([hit * high, hit * low], axis=0).astype(BF16)
        put = (slot_of == rank).astype(F32).astype(BF16)
        total = total + contract(put, values, 1, 1)
    rows = total[:, :owners] * 256.0 + total[:, owners:]
    tall = round_up(slots, LANES)
    if tall > slots:
        rows = jnp.concatenate([rows, jnp.zeros((tall - slots, owners), F32)], axis=0)
    count = jnp.sum(valid_ref[...])
    wide = asked_ref.shape[1]
    flat = rows.T
    if wide > tall:
        flat = jnp.concatenate([flat, jnp.zeros((owners, wide - tall), F32)], axis=1)
    asked_ref[...] = jnp.where(iota((owners, wide), 1) < slots, flat.astype(jnp.int32), count)


def lookup_kernel(slots, stride, ids_ref, table_ref, rows_ref, blocks_ref):
    embed, rows_own = table_ref.shape
    tall = round_up(embed, 8)
    parts = rows_own // 256
    wide = ids_ref.shape[1]
    third = stride // 3
    blocks_ref[...] = jnp.zeros_like(blocks_ref)
    for part in range(parts):
        blocks_ref[part * tall : part * tall + embed, :] = table_ref[:, part * 256 : part * 256 + 256]
    blocks = blocks_ref[...].astype(BF16)
    low_of = iota((256, wide), 0)

    def step(owner, carry):
        ids = ids_ref[pl.ds(owner, 1), :]
        high = lax.shift_right_logical(ids, 8)
        pick = (low_of == (ids & 255)).astype(F32).astype(BF16)
        found = contract(blocks, pick, 1, 0)
        mine = jnp.zeros((tall, wide), F32)
        for part in range(parts):
            mine = jnp.where(high == part, found[part * tall : part * tall + tall], mine)
        square = jnp.concatenate([mine, jnp.zeros((LANES - tall, wide), F32)], axis=0).T
        packed = square[:third]
        for piece in (1, 2):
            packed = packed + pltpu.roll(square[piece * third : piece * third + third], embed * piece, 1)
        rows_ref[pl.ds(pl.multiple_of(owner * third, 16), third), :] = packed.astype(BF16)
        return carry

    lax.fori_loop(0, ids_ref.shape[0], step, 0, unroll=4)


def column_map(feat, dense_width, embed, turned):
    start = dense_width + embed * feat
    tile = start // LANES
    shape = (2 * LANES, LANES) if turned else (LANES, 2 * LANES)
    column, lane = iota(shape, 1 - turned), iota(shape, turned)
    hit = (column == lane + (start - tile * LANES)) & (lane < embed)
    return pl.multiple_of(tile * LANES, LANES), hit.astype(F32).astype(BF16)


def inputs_kernel(feats, stride, embed, dense_width, place_ref, rows_ref, dense_ref, x_ref, far_ref, even_ref, odd_ref, sum_ref):
    half = even_ref.shape[0]
    third = stride // 3
    width = dense_width + embed * feats

    def unpack(owner, carry):
        block = rows_ref[pl.ds(pl.multiple_of(owner * third, 16), third), :].astype(F32)
        for piece in range(3):
            rolled = block if piece == 0 else pltpu.roll(block, LANES - embed * piece, 1)
            far_ref[pl.ds(pl.multiple_of(owner * stride + piece * third, 16), third), :] = rolled
        return carry

    lax.fori_loop(0, far_ref.shape[0] // stride, unpack, 0, unroll=4)
    sum_ref[...] = jnp.zeros_like(sum_ref)
    sum_ref[:, :LANES] = dense_ref[...].astype(F32)
    ones = width - width // LANES * LANES
    end = slice(width // LANES * LANES, width // LANES * LANES + LANES)
    sum_ref[:, end] += (iota((half, LANES), 1) == ones).astype(F32)
    odd_ref[...] = jnp.zeros_like(odd_ref)

    def add(ref, at, spread):
        start, spread = spread
        here = slice(at, at + CHUNK)
        sum_ref[here, pl.ds(start, 2 * LANES)] += contract(ref[here, :].astype(BF16), spread, 1, 0)

    def fetch(feat, ref, at):
        rows = [far_ref[pl.ds(place_ref[feat * half + at + k], 1), :] for k in range(CHUNK)]
        for k in range(CHUNK):
            ref[at + k : at + k + 1, :] = rows[k]

    def step(pair, carry):
        spread = column_map(jnp.maximum(2 * pair - 1, 0), dense_width, embed, 0)
        for at in range(0, half, CHUNK):
            add(odd_ref, at, spread)
            fetch(2 * pair, even_ref, at)
        spread = column_map(2 * pair, dense_width, embed, 0)
        for at in range(0, half, CHUNK):
            add(even_ref, at, spread)
            fetch(2 * pair + 1, odd_ref, at)
        return carry

    lax.fori_loop(0, feats // 2, step, 0)
    spread = column_map(feats - 1, dense_width, embed, 0)
    for at in range(0, half, CHUNK):
        add(odd_ref, at, spread)
    x_ref[...] = sum_ref[...].astype(BF16)


def send_kernel(feats, slots, stride, embed, dense_width, place_ref, dx_ref, rows_ref, far_ref, even_ref, odd_ref):
    half = even_ref.shape[0]
    third = stride // 3
    owners = far_ref.shape[0] // stride

    def clear(owner, carry):
        gap = stride - slots
        far_ref[pl.ds(pl.multiple_of(owner * stride + slots, 8), gap), :] = jnp.zeros((gap, LANES), F32)
        return carry

    lax.fori_loop(0, owners, clear, 0, unroll=8)

    def cut(ref, at, spread):
        start, spread = spread
        here = slice(at, at + CHUNK)
        ref[here, :] = contract(dx_ref[here, pl.ds(start, 2 * LANES)], spread, 1, 0)

    def put(feat, ref, at):
        rows = [ref[at + k : at + k + 1, :] for k in range(CHUNK)]
        for k in range(CHUNK):
            far_ref[pl.ds(place_ref[feat * half + at + k], 1), :] = rows[k]

    spread = column_map(0, dense_width, embed, 1)
    for at in range(0, half, CHUNK):
        cut(even_ref, at, spread)

    def step(pair, carry):
        spread = column_map(2 * pair + 1, dense_width, embed, 1)
        for at in range(0, half, CHUNK):
            cut(odd_ref, at, spread)
            put(2 * pair, even_ref, at)
        spread = column_map(jnp.minimum(2 * pair + 2, feats - 1), dense_width, embed, 1)
        for at in range(0, half, CHUNK):
            cut(even_ref, at, spread)
            put(2 * pair + 1, odd_ref, at)
        return carry

    lax.fori_loop(0, feats // 2, step, 0)

    def pack(owner, carry):
        packed = jnp.zeros((third, LANES), F32)
        for piece in range(3):
            block = far_ref[pl.ds(pl.multiple_of(owner * stride + piece * third, 8), third), :]
            packed = packed + (block if piece == 0 else pltpu.roll(block, embed * piece, 1))
        rows_ref[pl.ds(pl.multiple_of(owner * third, 16), third), :] = packed.astype(BF16)
        return carry

    lax.fori_loop(0, owners, pack, 0, unroll=4)


def table_kernel(
    slots, stride, ids_ref, rows_ref, table_ref, first_ref, second_ref,
    grad_ref, first_new_ref, second_new_ref, table_new_ref, total_ref,
):
    embed, rows_own = table_ref.shape
    tall = round_up(embed, 8)
    parts = rows_own // 256
    wide = ids_ref.shape[1]
    third = stride // 3
    low_of = iota((256, wide), 0)
    lane = iota((1, wide), 1)
    total_ref[...] = jnp.zeros_like(total_ref)

    def step(owner, carry):
        ids = jnp.where(lane < slots, ids_ref[pl.ds(owner, 1), :], -1)
        high = lax.shift_right_arithmetic(ids, 8)
        pick = (low_of == (ids & 255)).astype(F32).astype(BF16)
        block = rows_ref[pl.ds(pl.multiple_of(owner * third, 16), third), :].astype(F32)
        pieces = [block if k == 0 else pltpu.roll(block, LANES - embed * k, 1) for k in range(3)]
        if wide > stride:
            pieces.append(jnp.zeros((wide - stride, LANES), F32))
        square = jnp.concatenate(pieces, axis=0)[:wide].T
        mine = jnp.where(iota((tall, wide), 0) < embed, square[:tall], 0.0)
        spread = [jnp.where(high == part, mine, 0.0) for part in range(parts)]
        total_ref[...] += contract(jnp.concatenate(spread, axis=0).astype(BF16), pick, 1, 1)
        return carry

    lax.fori_loop(0, ids_ref.shape[0], step, 0, unroll=4)
    for part in range(parts):
        here = slice(part * 256, part * 256 + 256)
        grad = total_ref[part * tall : part * tall + embed, :]
        one, two, new = adamw(table_ref[:, here], grad, first_ref[:, here], second_ref[:, here], 0.25)
        grad_ref[:, here] = grad
        first_new_ref[:, here] = one
        second_new_ref[:, here] = two
        table_new_ref[:, here] = new


def tiles(size):
    return [(at, min(256, size - at)) for at in range(0, size, 256)]


def towers_kernel(
    spot_ref, count_ref, bias_ref, x_ref, vec_ref, target_ref, valid_ref,
    own_ref, half_ref, half_core_ref, deep_ref, deep_core_ref,
    one_ref, d_second_ref, d_first_ref, d_deep_ref, dx_ref, head_ref,
    cross_ref, all_deep_ref, pre_first_ref, layer_ref, pre_second_ref, two_ref, slope_ref, hidden_ref, arrival,
):
    half, wide = x_ref.shape
    pairs, _, deep_rows = deep_ref.shape[:3]
    hidden = 4 * pairs * deep_rows
    tower, core = spot_ref[0], spot_ref[3]
    middle = half_ref.shape[0]
    copies = []
    for k, (source, target) in enumerate(
        (
            (own_ref, cross_ref.at[tower, pl.ds(0, 2 * middle), :]),
            (half_ref, cross_ref.at[1 - tower, pl.ds(pl.multiple_of(core * middle, 16), middle), :]),
            (half_core_ref, cross_ref.at[1 - tower, pl.ds(pl.multiple_of((1 - core) * middle, 16), middle), :]),
            (deep_ref.at[:, 0], all_deep_ref.at[0, :, core]),
            (deep_ref.at[:, 1], all_deep_ref.at[1, :, core]),
            (deep_core_ref.at[:, 0], all_deep_ref.at[0, :, 1 - core]),
            (deep_core_ref.at[:, 1], all_deep_ref.at[1, :, 1 - core]),
        )
    ):
        copies.append(pltpu.make_async_copy(source, target, arrival.at[k]))
        copies[-1].start()

    def deep_block(at, size):
        per = 2 * deep_rows
        block = all_deep_ref[at // (hidden // 2), pl.ds(at % (hidden // 2) // per, size // per)]
        return block.reshape(size, wide)

    def lanes(x):
        total = x[:, :LANES]
        for at in range(LANES, x.shape[1], LANES):
            total = total + x[:, at : at + LANES]
        return total

    if 2 * middle < wide:
        cross_ref[:, 2 * middle :, :] = jnp.zeros((2, wide - 2 * middle, wide), BF16)
    for copy in copies[:3]:
        copy.wait()
    for at, size in tiles(wide):
        here = slice(at, at + size)
        base = x_ref[:, here].astype(F32)
        pre = contract(x_ref[...], cross_ref[0, :, here], 1, 0) + vec_ref[0:1, here]
        layer = base * pre + base
        pre_first_ref[:, here] = pre
        layer_ref[:, here] = layer
        one_ref[:, here] = layer.astype(BF16)
    score = jnp.zeros((half, LANES), F32)
    for at, size in tiles(wide):
        here = slice(at, at + size)
        base = x_ref[:, here].astype(F32)
        pre = contract(one_ref[...], cross_ref[1, :, here], 1, 0) + vec_ref[1:2, here]
        two = (base * pre + layer_ref[:, here]).astype(BF16)
        pre_second_ref[:, here] = pre
        two_ref[:, here] = two
        score = score + lanes(two.astype(F32) * vec_ref[3:4, here])
    for copy in copies[3:]:
        copy.wait()
    for at, size in tiles(hidden):
        here = slice(at, at + size)
        pre = contract(x_ref[...], deep_block(at, size), 1, 1) + vec_ref[2:3, here]
        gate = jax.nn.sigmoid(pre)
        out = (pre * gate).astype(BF16)
        hidden_ref[:, here] = out
        slope_ref[:, here] = gate * (1.0 + pre * (1.0 - gate))
        score = score + lanes(out.astype(F32) * vec_ref[4:5, here])
    logit = jnp.sum(score, axis=1, keepdims=True) + bias_ref[0, 0]
    target, valid = target_ref[...], valid_ref[...]
    softplus = jnp.maximum(logit, 0.0) + jnp.log1p(jnp.exp(-jnp.abs(logit)))
    loss = jnp.sum(valid * (softplus - target * logit), axis=0, keepdims=True)
    d_logit = valid * (jax.nn.sigmoid(logit) - target) / count_ref[0, 0]
    bias_grad = jnp.sum(d_logit, axis=0, keepdims=True)
    lane = iota((1, wide), 1)
    head_ref[...] = jnp.zeros_like(head_ref)
    head_ref[2:3, :] = jnp.where(lane == 0, bias_grad, jnp.where(lane == 1, loss, 0.0))
    for at, size in tiles(wide):
        here = slice(at, at + size)
        base = x_ref[:, here].astype(F32)
        d_second_ref[:, here] = (d_logit * vec_ref[3:4, here] * base).astype(BF16)
        head_ref[0:1, here] = jnp.sum(d_logit * two_ref[:, here].astype(F32), axis=0, keepdims=True)
    for at, size in tiles(hidden):
        here = slice(at, at + size)
        d_deep_ref[:, here] = (d_logit * vec_ref[4:5, here] * slope_ref[:, here]).astype(BF16)
        head_ref[1:2, here] = jnp.sum(d_logit * hidden_ref[:, here].astype(F32), axis=0, keepdims=True)
    for at, size in tiles(wide):
        here = slice(at, at + size)
        base = x_ref[:, here].astype(F32)
        d_two = d_logit * vec_ref[3:4, here]
        d_one = contract(d_second_ref[...], cross_ref[1, here, :], 1, 1) + d_two
        d_first_ref[:, here] = (d_one * base).astype(BF16)
        layer_ref[:, here] = d_one * (1.0 + pre_first_ref[:, here]) + d_two * pre_second_ref[:, here]
    for at, size in tiles(wide):
        here = slice(at, at + size)
        columns = all_deep_ref[:, :, :, :, here].reshape(hidden, size)
        dx = contract(d_first_ref[...], cross_ref[0, here, :], 1, 1) + contract(d_deep_ref[...], columns, 1, 0)
        dx_ref[:, here] = (dx + layer_ref[:, here]).astype(BF16)


def grads_kernel(
    deep_rows, spot_ref, x_ref, one_ref, d_second_ref, d_first_ref, d_deep_ref, head_ref,
    keep_ref, give_ref, rest_ref, turned_ref,
):
    half, wide = x_ref.shape
    hidden = d_deep_ref.shape[1]
    mid, rows, main = keep_ref.shape[3:]
    towers, groups, pairs = 2, 2 * mid, 2
    rows_c = rows - deep_rows
    even = spot_ref[3] == 0

    def share(value, tower, at, size, chunk, first):
        by_tower = tower ^ spot_ref[0]
        for group in range(groups):
            by_far = group ^ spot_ref[1]
            upper = by_far // mid
            for pair in range(pairs):
                by_near = pair ^ spot_ref[2]
                one = by_tower + upper * (by_near - by_tower)
                two = by_near + upper * (by_tower - by_near)
                start = (group * pairs + pair) * 2 * chunk
                low, high = value[start : start + chunk], value[start + chunk : start + 2 * chunk]
                place = (upper, one, two, by_far % mid, slice(first, first + chunk), slice(at, at + size))
                keep_ref[place] = jnp.where(even, low, high).astype(BF16)
                give_ref[place] = jnp.where(even, high, low).astype(BF16)

    rest_ref[...] = jnp.zeros_like(rest_ref)
    for tower, (left, right) in enumerate(((one_ref, d_second_ref), (x_ref, d_first_ref))):
        tower = 1 - tower
        turned_ref[...] = left[...].T
        for at, size in tiles(main):
            value = contract(turned_ref[...], right[:, at : at + size], 1, 0)
            share(value, tower, at, size, rows_c, 0)
            rest_ref[16 * tower : 16 * tower + 3, at : at + size] = value[main : main + 3]
            rest_ref[6 + tower : 7 + tower, at : at + size] = value[main + 3 : main + 4]
        value = contract(turned_ref[...], right[:, main:wide], 1, 0)
        rest_ref[16 * tower : 16 * tower + 3, main:wide] = value[main : main + 3]
        rest_ref[6 + tower : 7 + tower, main:wide] = value[main + 3 : main + 4]
        rest_ref[16 * tower + 3 : 16 * tower + 6, :main] = value[:main].T[:3]
    bias = contract(turned_ref[main:wide, :], d_deep_ref[...], 1, 0)
    rest_ref[8:12, :hidden] = bias[:4]
    rest_ref[12:15, :] = head_ref[0:3, :]
    mine, other = rest_ref[0:8, :], rest_ref[16:24, :]
    swap = (iota((8, wide), 0) < 6) & (iota((8, wide), 1) >= wide * (1 - spot_ref[0]))
    rest_ref[0:8, :] = jnp.where(swap, other, mine)
    rest_ref[16:24, :] = jnp.where(swap, mine, other)
    turned_ref[:hidden, :] = d_deep_ref[...].T
    for at, size in tiles(main):
        value = contract(turned_ref[:hidden, :], x_ref[:, at : at + size], 1, 0)
        for tower in range(towers):
            share(value[tower * (hidden // towers) : (tower + 1) * (hidden // towers)], tower, at, size, deep_rows, rows_c)


def cross_kernel(
    place_ref, near_ref, far_ref, rest_ref, weight_ref, first_ref, second_ref,
    grad_ref, first_new_ref, second_new_ref, new_ref, copy_ref,
):
    block = pl.program_id(0)
    width = weight_ref.shape[2]
    main = near_ref.shape[3]
    half = near_ref.shape[2]
    rows = 2 * half
    even = (place_ref[0] & 1) == 0

    def update(at, columns, grad):
        here = (slice(at, at + grad.shape[0]), 0, columns)
        one, two, new = adamw(weight_ref[here], grad, first_ref[here], second_ref[here], 0.03)
        grad_ref[here] = grad
        first_new_ref[here] = one
        second_new_ref[here] = two
        new_ref[here] = new
        copy_ref[slice(at, at + grad.shape[0]), columns] = new.astype(BF16)

    @pl.when(block < pl.num_programs(0) - 1)
    def _():
        near, far = near_ref[0, 0].astype(F32), far_ref[0, 0].astype(F32)
        update(0, slice(0, main), jnp.where(even, near, far))
        update(half, slice(0, main), jnp.where(even, far, near))
        lane = pl.multiple_of(block * rows // LANES * LANES, LANES)
        side = rest_ref[0, :, pl.ds(lane, LANES)]
        side = jnp.concatenate([side, jnp.zeros((LANES - 8, LANES), F32)], axis=0).T
        parts = [side[at : at + rows] for at in range(0, LANES, rows)]
        side = parts[0]
        for k, part in enumerate(parts):
            side = jnp.where(block % len(parts) == k, part, side)
        update(0, slice(main, width), side[:, 3 : 3 + width - main])

    @pl.when(block == pl.num_programs(0) - 1)
    def _():
        update(0, slice(0, width), rest_ref[0, :, :width])


def flip(x, axis, bit, size):
    return lax.ppermute(x, axis, [(i, i ^ bit) for i in range(size)])


def pick(x, axis, index):
    return lax.dynamic_index_in_dim(x, index, axis, keepdims=False)


def join(mine, other, axis, index):
    return jnp.where(index == 0, jnp.stack([mine, other], axis), jnp.stack([other, mine], axis))


def flip_far(x, batch, groups):
    return jnp.stack([x] + [flip(x, "batch", k * 4, batch) for k in range(1, groups)])


def in_order(parts, groups):
    far = lax.axis_index("batch") // 4
    return jnp.stack([pick(parts, 0, k ^ far) for k in range(groups)])


def local(
    dense_feats,
    category_ids,
    labels,
    valid_mask,
    embed_table,
    table_first,
    table_second,
    cross_weight,
    cross_first,
    cross_second,
    deep_weight,
    deep_first,
    deep_second,
    vectors,
    vector_first,
    vector_second,
):
    towers, batch = lax.axis_size("tower"), lax.axis_size("batch")
    owners = towers * batch
    tower, place = lax.axis_index("tower"), lax.axis_index("batch")
    core, near, far = place & 1, (place >> 1) & 1, place >> 2
    groups = batch // 4
    spot = jnp.stack([tower, far, near, core])
    rows_own, embed = embed_table.shape
    examples, feats = category_ids.shape
    half = examples // towers
    width = cross_weight.shape[1]
    deep_rows = deep_weight.shape[0]
    hidden = deep_rows * owners
    dense_width = dense_feats.shape[1]
    wide = round_up(width, LANES)
    slots = half * feats // owners
    third = round_up(-(-slots // 3), 16)
    stride = 3 * third
    shift = rows_own.bit_length() - 1
    asked_wide = round_up(max(slots + 1, stride), LANES)

    def mine(x, dim):
        return lax.dynamic_slice_in_dim(x, tower * half, half, dim)

    ids = mine(category_ids.T, 1)
    valid = mine(valid_mask, 0)
    target = mine(labels, 0).astype(F32)
    dense = jnp.pad(mine(dense_feats, 0), ((0, 0), (0, LANES - dense_width)))

    asked, slot = pl.pallas_call(
        functools.partial(slots_kernel, shift, slots, stride),
        out_shape=(
            jax.ShapeDtypeStruct((owners, asked_wide), jnp.int32),
            jax.ShapeDtypeStruct((feats * half // LANES, LANES), jnp.int32),
        ),
        in_specs=[in_vmem()] * 2,
        out_specs=(in_vmem(), in_vmem()),
        compiler_params=params(32),
        name="slots",
    )(ids, valid.reshape(1, half))
    slot = slot.reshape(-1)
    arrived = lax.all_to_all(asked, ("tower", "batch"), split_axis=0, concat_axis=0, tiled=True)
    middle = round_up(-(-width // 2), 16)
    own_low = jnp.pad(cross_weight[0].astype(BF16), ((0, 2 * middle - width), (0, wide - width)))
    deep_own = jnp.pad(deep_weight.astype(BF16), ((0, 0), (0, wide - width)))
    own_low, deep_own, arrived = lax.optimization_barrier((own_low, deep_own, arrived))
    count = jnp.sum(arrived[:, slots]).astype(F32)
    table_t = embed_table.T
    deep_parts = flip_far(deep_own, batch, groups)
    got_low = flip(lax.dynamic_slice_in_dim(own_low, core * middle, middle, 0), "tower", 1, towers)
    found = pl.pallas_call(
        functools.partial(lookup_kernel, slots, stride),
        out_shape=jax.ShapeDtypeStruct((owners * third, LANES), BF16),
        in_specs=[in_vmem()] * 2,
        out_specs=in_vmem(),
        scratch_shapes=[pltpu.VMEM((rows_own // 256 * round_up(embed, 8), 256), F32)],
        compiler_params=params(32),
        name="lookup",
    )(arrived, table_t)
    deep_parts, found = lax.optimization_barrier((deep_parts, found))
    returned = lax.all_to_all(found, ("tower", "batch"), split_axis=0, concat_axis=0, tiled=True)
    deep_low = in_order(deep_parts, groups)
    deep_low = join(deep_low, flip(deep_low, "tower", 1, towers), 1, tower)
    deep_low = join(deep_low, flip(deep_low, "batch", 2, batch), 1, near).reshape(batch // 2, towers, deep_rows, wide)

    def widen(x):
        return jnp.pad(x, (0, wide - x.shape[0]))

    vec = jnp.stack(
        [
            widen(vectors[:width]),
            widen(vectors[width : 2 * width]),
            widen(vectors[2 * width : 2 * width + hidden]),
            widen(vectors[2 * width + hidden : 3 * width + hidden]).astype(BF16).astype(F32),
            widen(vectors[3 * width + hidden : 3 * width + 2 * hidden]).astype(BF16).astype(F32),
        ]
        + [jnp.zeros((wide,), F32)] * 3
    )
    target = target.reshape(half, 1)
    valid = valid.astype(F32).reshape(half, 1)
    returned, own_low, got_low, deep_low, vec, target, valid = lax.optimization_barrier(
        (returned, own_low, got_low, deep_low, vec, target, valid)
    )
    got_core = flip(got_low, "batch", 1, batch)
    deep_core = flip(deep_low, "batch", 1, batch)
    inputs = pl.pallas_call(
        functools.partial(inputs_kernel, feats, stride, embed, dense_width),
        out_shape=jax.ShapeDtypeStruct((half, wide), BF16),
        in_specs=[in_smem(), in_vmem(), in_vmem()],
        out_specs=in_vmem(),
        scratch_shapes=[
            pltpu.VMEM((owners * stride, LANES), F32),
            pltpu.VMEM((half, LANES), F32),
            pltpu.VMEM((half, LANES), F32),
            pltpu.VMEM((half, wide), F32),
        ],
        compiler_params=params(48),
        name="inputs",
    )(slot, returned, dense)

    low = jax.ShapeDtypeStruct((half, wide), BF16)
    low_deep = jax.ShapeDtypeStruct((half, hidden), BF16)
    one_low, d_second, d_first, d_deep, d_inputs, heads = pl.pallas_call(
        towers_kernel,
        out_shape=(low, low, low, low_deep, low, jax.ShapeDtypeStruct((8, wide), F32)),
        in_specs=[in_smem()] * 3 + [in_vmem()] * 4 + [pl.BlockSpec(memory_space=pl.ANY)] * 5,
        out_specs=(in_vmem(),) * 6,
        scratch_shapes=[
            pltpu.VMEM((2, wide, wide), BF16),
            pltpu.VMEM((2, batch // 2, 2, deep_rows, wide), BF16),
            pltpu.VMEM((half, wide), F32),
            pltpu.VMEM((half, wide), F32),
            pltpu.VMEM((half, wide), F32),
            pltpu.VMEM((half, wide), BF16),
            pltpu.VMEM((half, hidden), F32),
            pltpu.VMEM((half, hidden), BF16),
            pltpu.SemaphoreType.DMA((7,)),
        ],
        compiler_params=params(56),
        name="towers",
    )(
        spot, count.reshape(1, 1), vectors[-1:].reshape(1, 1), inputs, vec, target, valid,
        own_low, got_low, got_core, deep_low, deep_core,
    )
    sent = pl.pallas_call(
        functools.partial(send_kernel, feats, slots, stride, embed, dense_width),
        out_shape=jax.ShapeDtypeStruct((owners * third, LANES), BF16),
        in_specs=[in_smem(), in_vmem()],
        out_specs=in_vmem(),
        scratch_shapes=[
            pltpu.VMEM((owners * stride, LANES), F32),
            pltpu.VMEM((half, LANES), F32),
            pltpu.VMEM((half, LANES), F32),
        ],
        compiler_params=params(48),
        name="send",
    )(slot, d_inputs)
    sent, inputs, one_low, d_second, d_first, d_deep, heads = lax.optimization_barrier(
        (sent, inputs, one_low, d_second, d_first, d_deep, heads)
    )
    main = width // LANES * LANES
    rows_c = main // batch
    parts = jax.ShapeDtypeStruct((2, 2, 2, groups // 2, rows_c + deep_rows, main), BF16)
    keep, give, rest = pl.pallas_call(
        functools.partial(grads_kernel, deep_rows),
        out_shape=(parts, parts, jax.ShapeDtypeStruct((24, wide), F32)),
        in_specs=[in_smem()] + [in_vmem()] * 6,
        out_specs=(in_vmem(),) * 3,
        scratch_shapes=[pltpu.VMEM((wide, half), BF16)],
        compiler_params=params(56),
        name="grads",
    )(spot, inputs, one_low, d_second, d_first, d_deep, heads)
    got = flip(give, "batch", 1, batch)
    rest = rest + flip(rest, "batch", 1, batch)

    def by_tower(x):
        return flip(x, "tower", 1, towers)

    def by_near(x):
        return flip(x, "batch", 2, batch)

    to_one, rest = lax.optimization_barrier(([keep[k, 1] + got[k, 1] for k in range(2)], rest))
    from_one = [by_tower(to_one[0]), by_near(to_one[1])]
    rest = rest[:16] + by_tower(jnp.concatenate([rest[16:22], rest[6:16]]))
    from_one, rest = lax.optimization_barrier((from_one, rest))
    rest = rest + by_near(rest)
    for bit in [4 << k for k in range(groups.bit_length() - 1)]:
        rest = rest + flip(rest, "batch", bit, batch)
    back = lax.all_to_all(sent, ("tower", "batch"), split_axis=0, concat_axis=0, tiled=True)
    shape_t = jax.ShapeDtypeStruct((embed, rows_own), F32)
    table_grad, table_one, table_two, table_new = pl.pallas_call(
        functools.partial(table_kernel, slots, stride),
        out_shape=(shape_t,) * 4,
        in_specs=[in_vmem()] * 5,
        out_specs=(in_vmem(),) * 4,
        scratch_shapes=[pltpu.VMEM((rows_own // 256 * round_up(embed, 8), 256), F32)],
        compiler_params=params(32),
        name="table",
    )(arrived, back, table_t, table_first.T, table_second.T)

    from_one, rest, table_grad, table_one, table_two, table_new = lax.optimization_barrier(
        (from_one, rest, table_grad, table_one, table_two, table_new)
    )
    to_two = lax.optimization_barrier([keep[k, 0, 1] + got[k, 0, 1] + from_one[k][1] for k in range(2)])
    from_two = [by_near(to_two[0]), by_tower(to_two[1])]
    from_two = lax.optimization_barrier(from_two)
    both = [keep[k, 0, 0] + got[k, 0, 0] + from_one[k][0] + from_two[k] for k in range(2)]
    both = lax.optimization_barrier([part[k] for part in both for k in range(groups // 2)])
    from_far = [flip(both[k], "batch", k * 4, batch) for k in range(1, groups)]
    from_far = lax.optimization_barrier(from_far)
    summed = both[0].astype(F32)
    for part in from_far:
        summed = summed + part.astype(F32)
    chunk = flip_far(summed[:rows_c].astype(BF16), batch, groups)
    across = flip(chunk, "batch", 2, batch)
    vector_grad = jnp.concatenate(
        [rest[6, :width], rest[7, :width], rest[11, :hidden], rest[12, :width], rest[13, :hidden], rest[14, :1]]
    )
    vector_one, vector_two, vector_new = adamw(vectors, vector_grad, vector_first, vector_second, 0.03)
    tail = lax.dynamic_slice_in_dim(rest[8 : 8 + width - main], (tower * batch + place) * deep_rows, deep_rows, 1).T
    deep_grad = jnp.concatenate([summed[rows_c:], tail], axis=1)
    deep_one, deep_two, deep_new = adamw(deep_weight, deep_grad, deep_first, deep_second, 0.03)
    deep_copy = deep_new.astype(BF16)
    side = rest[:8][None]
    (
        across, side, vector_grad, vector_one, vector_two, vector_new,
        deep_grad, deep_one, deep_two, deep_new, deep_copy,
    ) = lax.optimization_barrier(
        (
            across, side, vector_grad, vector_one, vector_two, vector_new,
            deep_grad, deep_one, deep_two, deep_new, deep_copy,
        )
    )
    chunk = jnp.stack([chunk, across])
    partner = flip(chunk, "batch", 1, batch)
    blocks = batch // 2
    rows = 2 * rows_c

    def relative(block, at):
        other = jnp.minimum(block, blocks - 1) ^ (at[0] >> 1)
        return (other & 1, other >> 1, 0, 0)

    piece = pl.BlockSpec((1, 1, rows_c, main), relative)
    slab = pl.BlockSpec((rows, 1, width), lambda block, at: (block, 0, 0))
    shape_c = jax.ShapeDtypeStruct((width, 1, width), F32)
    cross_out = pl.pallas_call(
        cross_kernel,
        grid_spec=pltpu.PrefetchScalarGridSpec(
            num_scalar_prefetch=1,
            grid=(blocks + 1,),
            in_specs=[piece, piece, pl.BlockSpec((1, 8, wide), lambda block, at: (0, 0, 0)), slab, slab, slab],
            out_specs=(slab, slab, slab, slab, pl.BlockSpec((rows, width), lambda block, at: (block, 0))),
        ),
        out_shape=(shape_c,) * 4 + (jax.ShapeDtypeStruct((width, width), BF16),),
        compiler_params=params(48),
        name="cross",
    )(
        place.reshape(1), chunk, partner, side,
        cross_weight.transpose(1, 0, 2), cross_first.transpose(1, 0, 2), cross_second.transpose(1, 0, 2),
    )
    cross_grad, cross_one, cross_two, cross_new = (x.transpose(1, 0, 2) for x in cross_out[:4])
    loss_sum = rest[14, 1]
    return (
        loss_sum,
        count,
        cross_grad,
        cross_one,
        cross_two,
        cross_new,
        cross_out[4][None],
        deep_grad,
        deep_one,
        deep_two,
        deep_new,
        deep_copy,
        table_grad.T,
        table_one.T,
        table_two.T,
        table_new.T,
        vector_grad,
        vector_one,
        vector_two,
        vector_new,
    )


def solution(mesh):
    both = P(("tower", "batch"), None)
    cross = P("tower", None, None)
    return jax.shard_map(
        local,
        mesh=mesh,
        in_specs=(
            P("batch", None),
            P("batch", None),
            P("batch"),
            P("batch"),
            both,
            both,
            both,
            cross,
            cross,
            cross,
            both,
            both,
            both,
            P(),
            P(),
            P(),
        ),
        out_specs=(P(), P()) + (cross,) * 5 + (both,) * 9 + (P(),) * 4,
        check_vma=False,
    )
```

```python
import functools

import jax
import jax.numpy as jnp
from jax import lax
from jax.experimental import pallas as pl
from jax.experimental.pallas import tpu as pltpu
from jax.sharding import PartitionSpec as P

STEP = 5
LANES = 128
CHUNK = 128
BF16 = jnp.bfloat16
F32 = jnp.float32


def round_up(value, unit):
    return -(-value // unit) * unit


def adamw(weight, grad, first, second, rate):
    first_new = 0.9 * first + 0.1 * grad
    second_new = 0.999 * second + 0.001 * grad * grad
    update = (
        first_new / (1.0 - 0.9**STEP) / (jnp.sqrt(second_new / (1.0 - 0.999**STEP)) + 1e-08)
        + 0.01 * weight
    )
    return (first_new, second_new, weight - rate * update)


def contract(left, right, left_dim, right_dim):
    return lax.dot_general(
        left, right, (((left_dim,), (right_dim,)), ((), ())), preferred_element_type=F32
    )


def iota(shape, dim):
    return lax.broadcasted_iota(jnp.int32, shape, dim)


def in_vmem():
    return pl.BlockSpec(memory_space=pltpu.VMEM)


def in_smem():
    return pl.BlockSpec(memory_space=pltpu.SMEM)


def params(mib):
    return pltpu.CompilerParams(vmem_limit_bytes=mib * 2**20)


def takes(micros):
    return pl.CostEstimate(flops=0, bytes_accessed=micros * 3_000_000, transcendentals=0)


def slots_kernel(shift, slots, stride, groups, ids_ref, valid_ref, table_ref, asked_ref, place_ref, low_ref):
    feats, half = ids_ref.shape
    owners = asked_ref.shape[0]
    embed, rows_own = table_ref.shape
    real = jnp.sum(valid_ref[...].astype(F32), axis=1, keepdims=True)
    high_real = jnp.floor(real * (1.0 / 64.0))
    spare = (low_ref.shape[0] - embed, rows_own)
    lane = iota(spare, 1)
    counts = jnp.where(lane == 0, high_real, jnp.where(lane == 1, real - 64.0 * high_real, 0.0))
    low_ref[...] = jnp.concatenate([table_ref[...], counts], axis=0).astype(BF16)
    before = (iota((half, half), 0) < iota((half, half), 1)).astype(BF16)
    owner_of = iota((owners, half), 0)
    slot_of = iota((slots, half), 0)
    base = jnp.zeros((owners, 1), F32)
    total = jnp.zeros((slots, 2 * owners), F32)
    for feat in range(feats):
        ids = ids_ref[feat : feat + 1, :]
        owner = lax.shift_right_logical(ids, shift)
        plane = lax.shift_right_logical(owner, (4 * groups).bit_length() - 1) * 4 + (owner & 3)
        owner = plane * groups + (lax.shift_right_logical(owner, 2) & (groups - 1))
        row = ids & ((1 << shift) - 1)
        hit = (owner_of == owner).astype(F32)
        earlier = contract(hit.astype(BF16), before, 1, 0) + base
        rank = jnp.sum(hit * earlier, axis=0, keepdims=True)
        base = base + jnp.sum(hit, axis=1, keepdims=True)
        rank = rank.astype(jnp.int32)
        spot = owner * stride + rank
        for k in range(half // LANES):
            at = feat * (half // LANES) + k
            place_ref[at : at + 1, :] = spot[:, k * LANES : k * LANES + LANES]
        high = lax.shift_right_logical(row, 8).astype(F32)
        low = (row & 255).astype(F32)
        values = jnp.concatenate([hit * high, hit * low], axis=0).astype(BF16)
        put = (slot_of == rank).astype(F32).astype(BF16)
        total = total + contract(put, values, 1, 1)
    rows = total[:, :owners] * 256.0 + total[:, owners:]
    tall = round_up(slots, LANES)
    if tall > slots:
        rows = jnp.concatenate([rows, jnp.zeros((tall - slots, owners), F32)], axis=0)
    wide = asked_ref.shape[1]
    flat = rows.T
    if wide > tall:
        flat = jnp.concatenate([flat, jnp.zeros((owners, wide - tall), F32)], axis=1)
    asked_ref[...] = flat.astype(jnp.int32)


def lookup_kernel(embed, stride, spot_ref, ids_ref, *refs):
    tables, (rows_ref, blocks_ref) = refs[:-2], refs[-2:]
    groups = len(tables)
    tall, rows_own = tables[0].shape
    parts = rows_own // 256
    wide = ids_ref.shape[1]
    third = stride // 3
    count = jnp.zeros((1, 1), F32)
    for k, table_ref in enumerate(tables):
        table = table_ref[...].astype(F32)
        count = count + 64.0 * table[embed : embed + 1, 0:1] + table[embed : embed + 1, 1:2]
        table = jnp.where(iota((tall, rows_own), 0) < embed, table, 0.0)
        block = jnp.concatenate([table[:, part * 256 : part * 256 + 256] for part in range(parts)], axis=0)
        blocks_ref[spot_ref[1] ^ k] = block.astype(BF16)
    low_of = iota((256, wide), 0)
    high_count = jnp.floor(count * (1.0 / 64.0))
    row, lane = iota((third, LANES), 0), iota((third, LANES), 1)
    counts = jnp.where(lane == LANES - 2, high_count, jnp.where(lane == LANES - 1, count - 64.0 * high_count, 0.0))
    counts = jnp.where(row == 0, counts, 0.0)

    def step(peer, carry):
        for group in range(groups):
            block = peer * groups + group
            ids = ids_ref[pl.ds(block, 1), :]
            high = lax.shift_right_logical(ids, 8)
            pick = (low_of == (ids & 255)).astype(F32).astype(BF16)
            found = contract(blocks_ref[group], pick, 1, 0)
            mine = jnp.zeros((tall, wide), F32)
            for part in range(parts):
                mine = jnp.where(high == part, found[part * tall : part * tall + tall], mine)
            square = jnp.concatenate([mine, jnp.zeros((LANES - tall, wide), F32)], axis=0).T
            packed = square[:third] if group else square[:third] + counts
            for piece in (1, 2):
                packed = packed + pltpu.roll(square[piece * third : piece * third + third], embed * piece, 1)
            rows_ref[pl.ds(pl.multiple_of(block * third, 16), third), :] = packed.astype(BF16)
        return carry

    lax.fori_loop(0, ids_ref.shape[0] // groups, step, 0)


def column_map(feat, dense_width, embed, turned):
    start = dense_width + embed * feat
    tile = start // LANES
    shape = (2 * LANES, LANES) if turned else (LANES, 2 * LANES)
    column, lane = iota(shape, 1 - turned), iota(shape, turned)
    hit = (column == lane + (start - tile * LANES)) & (lane < embed)
    return pl.multiple_of(tile * LANES, LANES), hit.astype(F32).astype(BF16)


def inputs_kernel(
    feats, stride, groups, embed, dense_width, place_ref, rows_ref, dense_ref, x_ref, count_ref, far_ref, even_ref, odd_ref, sum_ref
):
    half = even_ref.shape[0]
    third = stride // 3
    width = dense_width + embed * feats

    def unpack(owner, carry):
        block = rows_ref[pl.ds(pl.multiple_of(owner * third, 16), third), :].astype(F32)
        for piece in range(3):
            rolled = block if piece == 0 else pltpu.roll(block, LANES - embed * piece, 1)
            far_ref[pl.ds(pl.multiple_of(owner * stride + piece * third, 16), third), :] = rolled
        return carry

    owners = far_ref.shape[0] // stride
    lax.fori_loop(0, owners, unpack, 0, unroll=4)
    counts = jnp.zeros((16, LANES), F32)
    for peer in range(owners // groups):
        start = peer * groups * third
        counts = counts + rows_ref[start : start + 16, :].astype(F32)
    count_ref[...] = 64.0 * counts[0:1, LANES - 2 : LANES - 1] + counts[0:1, LANES - 1 : LANES]
    sum_ref[...] = jnp.zeros_like(sum_ref)
    sum_ref[:, :LANES] = dense_ref[...].astype(F32)
    ones = width - width // LANES * LANES
    end = slice(width // LANES * LANES, width // LANES * LANES + LANES)
    sum_ref[:, end] += (iota((half, LANES), 1) == ones).astype(F32)
    odd_ref[...] = jnp.zeros_like(odd_ref)

    def add(ref, at, spread):
        start, spread = spread
        here = slice(at, at + CHUNK)
        sum_ref[here, pl.ds(start, 2 * LANES)] += contract(ref[here, :].astype(BF16), spread, 1, 0)

    def fetch(feat, ref, at):
        rows = [far_ref[pl.ds(place_ref[feat * half + at + k], 1), :] for k in range(CHUNK)]
        for k in range(CHUNK):
            ref[at + k : at + k + 1, :] = rows[k]

    def step(pair, carry):
        spread = column_map(jnp.maximum(2 * pair - 1, 0), dense_width, embed, 0)
        for at in range(0, half, CHUNK):
            add(odd_ref, at, spread)
            fetch(2 * pair, even_ref, at)
        spread = column_map(2 * pair, dense_width, embed, 0)
        for at in range(0, half, CHUNK):
            add(even_ref, at, spread)
            fetch(2 * pair + 1, odd_ref, at)
        return carry

    lax.fori_loop(0, feats // 2, step, 0)
    spread = column_map(feats - 1, dense_width, embed, 0)
    for at in range(0, half, CHUNK):
        add(odd_ref, at, spread)
    x_ref[...] = sum_ref[...].astype(BF16)


def send_kernel(feats, slots, stride, embed, dense_width, place_ref, dx_ref, rows_ref, far_ref, even_ref, odd_ref):
    half = even_ref.shape[0]
    third = stride // 3
    owners = far_ref.shape[0] // stride

    def clear(owner, carry):
        gap = stride - slots
        far_ref[pl.ds(pl.multiple_of(owner * stride + slots, 8), gap), :] = jnp.zeros((gap, LANES), F32)
        return carry

    lax.fori_loop(0, owners, clear, 0, unroll=8)

    def cut(ref, at, spread):
        start, spread = spread
        here = slice(at, at + CHUNK)
        ref[here, :] = contract(dx_ref[here, pl.ds(start, 2 * LANES)], spread, 1, 0)

    def put(feat, ref, at):
        rows = [ref[at + k : at + k + 1, :] for k in range(CHUNK)]
        for k in range(CHUNK):
            far_ref[pl.ds(place_ref[feat * half + at + k], 1), :] = rows[k]

    spread = column_map(0, dense_width, embed, 1)
    for at in range(0, half, CHUNK):
        cut(even_ref, at, spread)

    def step(pair, carry):
        spread = column_map(2 * pair + 1, dense_width, embed, 1)
        for at in range(0, half, CHUNK):
            cut(odd_ref, at, spread)
            put(2 * pair, even_ref, at)
        spread = column_map(jnp.minimum(2 * pair + 2, feats - 1), dense_width, embed, 1)
        for at in range(0, half, CHUNK):
            cut(even_ref, at, spread)
            put(2 * pair + 1, odd_ref, at)
        return carry

    lax.fori_loop(0, feats // 2, step, 0)

    def pack(owner, carry):
        packed = jnp.zeros((third, LANES), F32)
        for piece in range(3):
            block = far_ref[pl.ds(pl.multiple_of(owner * stride + piece * third, 8), third), :]
            packed = packed + (block if piece == 0 else pltpu.roll(block, embed * piece, 1))
        rows_ref[pl.ds(pl.multiple_of(owner * third, 16), third), :] = packed.astype(BF16)
        return carry

    lax.fori_loop(0, owners, pack, 0, unroll=4)


def table_kernel(embed, slots, stride, spot_ref, ids_ref, rows_ref, own_ref, other_ref, total_ref):
    groups, size = total_ref.shape[:2]
    tall = round_up(embed, 8)
    parts = size // tall
    wide = ids_ref.shape[1]
    third = stride // 3
    low_of = iota((256, wide), 0)
    lane = iota((1, wide), 1)
    total_ref[...] = jnp.zeros_like(total_ref)

    def step(peer, carry):
        for group in range(groups):
            at = peer * groups + group
            ids = jnp.where(lane < slots, ids_ref[pl.ds(at, 1), :], -1)
            high = lax.shift_right_arithmetic(ids, 8)
            pick = (low_of == (ids & 255)).astype(F32).astype(BF16)
            block = rows_ref[pl.ds(pl.multiple_of(at * third, 16), third), :].astype(F32)
            pieces = [block if k == 0 else pltpu.roll(block, LANES - embed * k, 1) for k in range(3)]
            if wide > stride:
                pieces.append(jnp.zeros((wide - stride, LANES), F32))
            square = jnp.concatenate(pieces, axis=0)[:wide].T
            mine = jnp.where(iota((tall, wide), 0) < embed, square[:tall], 0.0)
            spread = [jnp.where(high == part, mine, 0.0) for part in range(parts)]
            total_ref[group] += contract(jnp.concatenate(spread, axis=0).astype(BF16), pick, 1, 1)
        return carry

    lax.fori_loop(0, ids_ref.shape[0] // groups, step, 0)
    own_ref[...] = total_ref[spot_ref[1]]
    for k in range(1, groups):
        other_ref[k - 1] = total_ref[spot_ref[1] ^ k].astype(BF16)


def update_kernel(*refs):
    own_ref, table_ref, first_ref, second_ref = refs[:4]
    others = refs[4:-4]
    grad_ref, first_new_ref, second_new_ref, table_new_ref = refs[-4:]
    embed, rows_own = table_ref.shape
    tall = round_up(embed, 8)
    total = own_ref[...]
    for ref in others:
        total = total + ref[...].astype(F32)
    for part in range(rows_own // 256):
        here = slice(part * 256, part * 256 + 256)
        grad = total[part * tall : part * tall + embed, :]
        one, two, new = adamw(table_ref[:, here], grad, first_ref[:, here], second_ref[:, here], 0.25)
        grad_ref[:, here] = grad
        first_new_ref[:, here] = one
        second_new_ref[:, here] = two
        table_new_ref[:, here] = new


def tiles(size):
    return [(at, min(256, size - at)) for at in range(0, size, 256)]


def towers_kernel(
    spot_ref, count_ref, bias_ref, x_ref, vec_ref, labels_ref,
    own_ref, half_ref, half_core_ref, here_ref, here_core_ref, near_ref, near_core_ref,
    one_ref, d_second_ref, d_first_ref, d_deep_ref, dx_ref, head_ref,
    cross_ref, all_deep_ref, pre_first_ref, layer_ref, pre_second_ref, two_ref, slope_ref, hidden_ref, arrival,
):
    half, wide = x_ref.shape
    groups, _, deep_rows = here_ref.shape[:3]
    hidden = 8 * groups * deep_rows
    tower, near, core = spot_ref[0], spot_ref[2], spot_ref[3]
    middle = half_ref.shape[0]
    moves = [(own_ref, cross_ref.at[tower, pl.ds(0, 2 * middle), :])]
    for ref, at_core in ((half_ref, core), (half_core_ref, 1 - core)):
        moves.append((ref, cross_ref.at[1 - tower, pl.ds(pl.multiple_of(at_core * middle, 16), middle), :]))
    for ref, at_near, at_core in (
        (here_ref, near, core), (here_core_ref, near, 1 - core), (near_ref, 1 - near, core), (near_core_ref, 1 - near, 1 - core)
    ):
        for k in range(2):
            moves.append((ref.at[:, k], all_deep_ref.at[k, :, at_near, at_core]))
    copies = []
    for k, (source, target) in enumerate(moves):
        copies.append(pltpu.make_async_copy(source, target, arrival.at[k]))
        copies[-1].start()

    def deep_block(at, size):
        tower, at = at // (hidden // 2), at % (hidden // 2)
        block = all_deep_ref[tower, pl.ds(at // (4 * deep_rows), size // (4 * deep_rows))]
        return block.reshape(size, wide)

    def lanes(x):
        total = x[:, :LANES]
        for at in range(LANES, x.shape[1], LANES):
            total = total + x[:, at : at + LANES]
        return total

    if 2 * middle < wide:
        cross_ref[:, 2 * middle :, :] = jnp.zeros((2, wide - 2 * middle, wide), BF16)
    for copy in copies[:3]:
        copy.wait()
    for at, size in tiles(wide):
        here = slice(at, at + size)
        base = x_ref[:, here].astype(F32)
        pre = contract(x_ref[...], cross_ref[0, :, here], 1, 0) + vec_ref[0:1, here]
        layer = base * pre + base
        pre_first_ref[:, here] = pre
        layer_ref[:, here] = layer
        one_ref[:, here] = layer.astype(BF16)
    score = jnp.zeros((half, LANES), F32)
    for at, size in tiles(wide):
        here = slice(at, at + size)
        base = x_ref[:, here].astype(F32)
        pre = contract(one_ref[...], cross_ref[1, :, here], 1, 0) + vec_ref[1:2, here]
        two = (base * pre + layer_ref[:, here]).astype(BF16)
        pre_second_ref[:, here] = pre
        two_ref[:, here] = two
        score = score + lanes(two.astype(F32) * vec_ref[3:4, here])
    for copy in copies[3:]:
        copy.wait()
    for at, size in tiles(hidden):
        here = slice(at, at + size)
        pre = contract(x_ref[...], deep_block(at, size), 1, 1) + vec_ref[2:3, here]
        gate = jax.nn.sigmoid(pre)
        out = (pre * gate).astype(BF16)
        hidden_ref[:, here] = out
        slope_ref[:, here] = gate * (1.0 + pre * (1.0 - gate))
        score = score + lanes(out.astype(F32) * vec_ref[4:5, here])
    logit = jnp.sum(score, axis=1, keepdims=True) + bias_ref[0, 0]
    labels = jnp.concatenate([labels_ref[...], jnp.zeros((6, half), jnp.int32)], axis=0).astype(F32).T
    target, valid = labels[:, 0:1], labels[:, 1:2]
    softplus = jnp.maximum(logit, 0.0) + jnp.log1p(jnp.exp(-jnp.abs(logit)))
    loss = jnp.sum(valid * (softplus - target * logit), axis=0, keepdims=True)
    d_logit = valid * (jax.nn.sigmoid(logit) - target) / count_ref[0, 0]
    bias_grad = jnp.sum(d_logit, axis=0, keepdims=True)
    lane = iota((1, wide), 1)
    head_ref[...] = jnp.zeros_like(head_ref)
    head_ref[2:3, :] = jnp.where(lane == 0, bias_grad, jnp.where(lane == 1, loss, 0.0))
    for at, size in tiles(wide):
        here = slice(at, at + size)
        base = x_ref[:, here].astype(F32)
        d_second_ref[:, here] = (d_logit * vec_ref[3:4, here] * base).astype(BF16)
        head_ref[0:1, here] = jnp.sum(d_logit * two_ref[:, here].astype(F32), axis=0, keepdims=True)
    for at, size in tiles(hidden):
        here = slice(at, at + size)
        d_deep_ref[:, here] = (d_logit * vec_ref[4:5, here] * slope_ref[:, here]).astype(BF16)
        head_ref[1:2, here] = jnp.sum(d_logit * hidden_ref[:, here].astype(F32), axis=0, keepdims=True)
    for at, size in tiles(wide):
        here = slice(at, at + size)
        base = x_ref[:, here].astype(F32)
        d_two = d_logit * vec_ref[3:4, here]
        d_one = contract(d_second_ref[...], cross_ref[1, here, :], 1, 1) + d_two
        d_first_ref[:, here] = (d_one * base).astype(BF16)
        layer_ref[:, here] = d_one * (1.0 + pre_first_ref[:, here]) + d_two * pre_second_ref[:, here]
    for at, size in tiles(wide):
        here = slice(at, at + size)
        columns = all_deep_ref[:, :, :, :, :, here].reshape(hidden, size)
        dx = contract(d_first_ref[...], cross_ref[0, here, :], 1, 1) + contract(d_deep_ref[...], columns, 1, 0)
        dx_ref[:, here] = (dx + layer_ref[:, here]).astype(BF16)


def grads_kernel(
    deep_rows, spot_ref, x_ref, one_ref, d_second_ref, d_first_ref, d_deep_ref, head_ref,
    keep_ref, give_ref, rest_ref, turned_ref,
):
    half, wide = x_ref.shape
    hidden = d_deep_ref.shape[1]
    mid, rows, main = keep_ref.shape[3:]
    towers, groups, pairs = 2, 2 * mid, 2
    rows_c = rows - deep_rows
    even = spot_ref[3] == 0

    def share(value, tower, at, size, chunk, first):
        by_tower = tower ^ spot_ref[0]
        for group in range(groups):
            by_far = group ^ spot_ref[1]
            upper = by_far // mid
            for pair in range(pairs):
                by_near = pair ^ spot_ref[2]
                one = by_tower + upper * (by_near - by_tower)
                two = by_near + upper * (by_tower - by_near)
                start = (group * pairs + pair) * 2 * chunk
                low, high = value[start : start + chunk], value[start + chunk : start + 2 * chunk]
                place = (upper, one, two, by_far % mid, slice(first, first + chunk), slice(at, at + size))
                keep_ref[place] = jnp.where(even, low, high).astype(BF16)
                give_ref[place] = jnp.where(even, high, low).astype(BF16)

    rest_ref[...] = jnp.zeros_like(rest_ref)
    for tower, (left, right) in enumerate(((one_ref, d_second_ref), (x_ref, d_first_ref))):
        tower = 1 - tower
        turned_ref[...] = left[...].T
        for at, size in tiles(main):
            value = contract(turned_ref[...], right[:, at : at + size], 1, 0)
            share(value, tower, at, size, rows_c, 0)
            rest_ref[16 * tower : 16 * tower + 3, at : at + size] = value[main : main + 3]
            rest_ref[6 + tower : 7 + tower, at : at + size] = value[main + 3 : main + 4]
        value = contract(turned_ref[...], right[:, main:wide], 1, 0)
        rest_ref[16 * tower : 16 * tower + 3, main:wide] = value[main : main + 3]
        rest_ref[6 + tower : 7 + tower, main:wide] = value[main + 3 : main + 4]
        rest_ref[16 * tower + 3 : 16 * tower + 6, :main] = value[:main].T[:3]
    bias = contract(turned_ref[main:wide, :], d_deep_ref[...], 1, 0)
    rest_ref[8:12, :hidden] = bias[:4]
    rest_ref[12:15, :] = head_ref[0:3, :]
    mine, other = rest_ref[0:8, :], rest_ref[16:24, :]
    swap = (iota((8, wide), 0) < 6) & (iota((8, wide), 1) >= wide * (1 - spot_ref[0]))
    rest_ref[0:8, :] = jnp.where(swap, other, mine)
    rest_ref[16:24, :] = jnp.where(swap, mine, other)
    turned_ref[:hidden, :] = d_deep_ref[...].T
    for at, size in tiles(main):
        value = contract(turned_ref[:hidden, :], x_ref[:, at : at + size], 1, 0)
        for tower in range(towers):
            share(value[tower * (hidden // towers) : (tower + 1) * (hidden // towers)], tower, at, size, deep_rows, rows_c)


def cross_kernel(
    place_ref, near_ref, far_ref, rest_ref, weight_ref, first_ref, second_ref,
    grad_ref, first_new_ref, second_new_ref, new_ref, copy_ref,
):
    block = pl.program_id(0)
    width = weight_ref.shape[2]
    main = near_ref.shape[3]
    half = near_ref.shape[2]
    rows = 2 * half
    even = (place_ref[0] & 1) == 0

    def update(at, columns, grad):
        here = (slice(at, at + grad.shape[0]), 0, columns)
        one, two, new = adamw(weight_ref[here], grad, first_ref[here], second_ref[here], 0.03)
        grad_ref[here] = grad
        first_new_ref[here] = one
        second_new_ref[here] = two
        new_ref[here] = new
        copy_ref[slice(at, at + grad.shape[0]), columns] = new.astype(BF16)

    @pl.when(block < pl.num_programs(0) - 1)
    def _():
        near, far = near_ref[0, 0].astype(F32), far_ref[0, 0].astype(F32)
        update(0, slice(0, main), jnp.where(even, near, far))
        update(half, slice(0, main), jnp.where(even, far, near))
        lane = pl.multiple_of(block * rows // LANES * LANES, LANES)
        side = rest_ref[0, :, pl.ds(lane, LANES)]
        side = jnp.concatenate([side, jnp.zeros((LANES - 8, LANES), F32)], axis=0).T
        parts = [side[at : at + rows] for at in range(0, LANES, rows)]
        side = parts[0]
        for k, part in enumerate(parts):
            side = jnp.where(block % len(parts) == k, part, side)
        update(0, slice(main, width), side[:, 3 : 3 + width - main])

    @pl.when(block == pl.num_programs(0) - 1)
    def _():
        update(0, slice(0, width), rest_ref[0, :, :width])


def flip(x, axis, bit, size):
    return lax.ppermute(x, axis, [(i, i ^ bit) for i in range(size)])


def pick(x, axis, index):
    return lax.dynamic_index_in_dim(x, index, axis, keepdims=False)


def join(mine, other, axis, index):
    return jnp.where(index == 0, jnp.stack([mine, other], axis), jnp.stack([other, mine], axis))


def flip_far(x, batch, groups):
    return jnp.stack([x] + [flip(x, "batch", k * 4, batch) for k in range(1, groups)])


def in_order(parts, groups):
    far = lax.axis_index("batch") // 4
    return jnp.stack([pick(parts, 0, k ^ far) for k in range(groups)])


def local(
    dense_feats,
    category_ids,
    labels,
    valid_mask,
    embed_table,
    table_first,
    table_second,
    cross_weight,
    cross_first,
    cross_second,
    deep_weight,
    deep_first,
    deep_second,
    vectors,
    vector_first,
    vector_second,
):
    towers, batch = lax.axis_size("tower"), lax.axis_size("batch")
    owners = towers * batch
    tower, place = lax.axis_index("tower"), lax.axis_index("batch")
    core, near, far = place & 1, (place >> 1) & 1, place >> 2
    groups = batch // 4
    spot = jnp.stack([tower, far, near, core])
    rows_own, embed = embed_table.shape
    examples, feats = category_ids.shape
    half = examples // towers
    width = cross_weight.shape[1]
    deep_rows = deep_weight.shape[0]
    hidden = deep_rows * owners
    dense_width = dense_feats.shape[1]
    wide = round_up(width, LANES)
    slots = half * feats // owners
    third = round_up(-(-slots // 3), 16)
    stride = 3 * third
    shift = rows_own.bit_length() - 1
    asked_wide = round_up(stride, LANES)

    def mine(x, dim):
        return lax.dynamic_slice_in_dim(x, tower * half, half, dim)

    ids = mine(category_ids.T, 1)
    valid = mine(valid_mask, 0)
    target = mine(labels, 0)
    dense = jnp.pad(mine(dense_feats, 0), ((0, 0), (0, LANES - dense_width)))

    table_t = embed_table.T
    tall = round_up(embed, 8)
    asked, slot, table_low = pl.pallas_call(
        functools.partial(slots_kernel, shift, slots, stride, groups),
        out_shape=(
            jax.ShapeDtypeStruct((owners, asked_wide), jnp.int32),
            jax.ShapeDtypeStruct((feats * half // LANES, LANES), jnp.int32),
            jax.ShapeDtypeStruct((tall, rows_own), BF16),
        ),
        in_specs=[in_vmem()] * 3,
        out_specs=(in_vmem(),) * 3,
        compiler_params=params(32),
        name="slots",
    )(ids, valid.reshape(1, half), table_t)
    slot = slot.reshape(-1)
    planes = [[t * batch + z * 4 + k for t in range(towers) for k in range(4)] for z in range(groups)]

    def in_plane(x):
        return lax.all_to_all(
            x, ("tower", "batch"), split_axis=0, concat_axis=0, axis_index_groups=planes, tiled=True
        )

    tables = [table_low] + [flip(table_low, "batch", k * 4, batch) for k in range(1, groups)]

    main = width // LANES * LANES
    rows_c = main // batch
    middle = round_up(-(-width // 2), 16)
    own_low = jnp.pad(cross_weight[0].astype(BF16), ((0, 2 * middle - width), (0, wide - width)))
    deep_own = jnp.pad(deep_weight.astype(BF16), ((0, 0), (0, wide - width)))
    asked, deep_own = lax.optimization_barrier((asked, deep_own))
    arrived = in_plane(asked)
    deep_pair = join(deep_own, flip(deep_own, "tower", 1, towers), 0, tower)
    tables[1:], own_low, arrived = lax.optimization_barrier((tables[1:], own_low, arrived))
    got_low = flip(lax.dynamic_slice_in_dim(own_low, core * middle, middle, 0), "tower", 1, towers)
    weights = flip_far(deep_pair, batch, groups)
    found = pl.pallas_call(
        functools.partial(lookup_kernel, embed, stride),
        out_shape=jax.ShapeDtypeStruct((owners * third, LANES), BF16),
        in_specs=[in_smem()] + [in_vmem()] * (1 + groups),
        out_specs=in_vmem(),
        scratch_shapes=[pltpu.VMEM((groups, rows_own // 256 * tall, 256), BF16)],
        compiler_params=params(32),
        name="lookup",
    )(spot, arrived, *tables)
    returned = in_plane(found)
    weights = in_order(weights, groups)

    def widen(x):
        return jnp.pad(x, (0, wide - x.shape[0]))

    vec = jnp.stack(
        [
            widen(vectors[:width]),
            widen(vectors[width : 2 * width]),
            widen(vectors[2 * width : 2 * width + hidden]),
            widen(vectors[2 * width + hidden : 3 * width + hidden]).astype(BF16).astype(F32),
            widen(vectors[3 * width + hidden : 3 * width + 2 * hidden]).astype(BF16).astype(F32),
        ]
        + [jnp.zeros((wide,), F32)] * 3
    )
    returned, own_low, got_low, weights, vec = lax.optimization_barrier((returned, own_low, got_low, weights, vec))
    got_core = flip(got_low, "batch", 1, batch)
    weights_core = flip(weights, "batch", 1, batch)
    weights_near = flip(weights, "batch", 2, batch)
    inputs, count = pl.pallas_call(
        functools.partial(inputs_kernel, feats, stride, groups, embed, dense_width),
        out_shape=(jax.ShapeDtypeStruct((half, wide), BF16), jax.ShapeDtypeStruct((1, 1), F32)),
        in_specs=[in_smem(), in_vmem(), in_vmem()],
        out_specs=(in_vmem(), in_vmem()),
        scratch_shapes=[
            pltpu.VMEM((owners * stride, LANES), F32),
            pltpu.VMEM((half, LANES), F32),
            pltpu.VMEM((half, LANES), F32),
            pltpu.VMEM((half, wide), F32),
        ],
        compiler_params=params(48),
        name="inputs",
    )(slot, returned, dense)

    inputs, count, weights_near = lax.optimization_barrier((inputs, count, weights_near))
    weights_both = flip(weights_near, "batch", 1, batch)
    low = jax.ShapeDtypeStruct((half, wide), BF16)
    low_deep = jax.ShapeDtypeStruct((half, hidden), BF16)
    one_low, d_second, d_first, d_deep, d_inputs, heads = pl.pallas_call(
        towers_kernel,
        out_shape=(low, low, low, low_deep, low, jax.ShapeDtypeStruct((8, wide), F32)),
        in_specs=[in_smem()] * 3 + [in_vmem()] * 3 + [pl.BlockSpec(memory_space=pl.ANY)] * 7,
        out_specs=(in_vmem(),) * 6,
        scratch_shapes=[
            pltpu.VMEM((2, wide, wide), BF16),
            pltpu.VMEM((2, groups, 2, 2, deep_rows, wide), BF16),
            pltpu.VMEM((half, wide), F32),
            pltpu.VMEM((half, wide), F32),
            pltpu.VMEM((half, wide), F32),
            pltpu.VMEM((half, wide), BF16),
            pltpu.VMEM((half, hidden), F32),
            pltpu.VMEM((half, hidden), BF16),
            pltpu.SemaphoreType.DMA((11,)),
        ],
        compiler_params=params(56),
        name="towers",
    )(
        spot, count, vectors[-1:].reshape(1, 1), inputs, vec, jnp.stack([target, valid]),
        own_low, got_low, got_core, weights, weights_core, weights_near, weights_both,
    )
    parts = jax.ShapeDtypeStruct((2, 2, 2, groups // 2, rows_c + deep_rows, main), BF16)
    keep, give, rest = pl.pallas_call(
        functools.partial(grads_kernel, deep_rows),
        out_shape=(parts, parts, jax.ShapeDtypeStruct((24, wide), F32)),
        in_specs=[in_smem()] + [in_vmem()] * 6,
        out_specs=(in_vmem(),) * 3,
        scratch_shapes=[pltpu.VMEM((wide, half), BF16)],
        compiler_params=params(56),
        name="grads",
    )(spot, inputs, one_low, d_second, d_first, d_deep, heads)
    got = flip(give, "batch", 1, batch)
    rest = rest + flip(rest, "batch", 1, batch)

    def by_tower(x):
        return flip(x, "tower", 1, towers)

    def by_near(x):
        return flip(x, "batch", 2, batch)

    to_one, rest, d_inputs = lax.optimization_barrier(([keep[k, 1] + got[k, 1] for k in range(2)], rest, d_inputs))
    from_one = [by_tower(to_one[0]), by_near(to_one[1])]
    rest = rest[:16] + by_tower(jnp.concatenate([rest[16:22], rest[6:16]]))
    sent = pl.pallas_call(
        functools.partial(send_kernel, feats, slots, stride, embed, dense_width),
        out_shape=jax.ShapeDtypeStruct((owners * third, LANES), BF16),
        in_specs=[in_smem(), in_vmem()],
        out_specs=in_vmem(),
        scratch_shapes=[
            pltpu.VMEM((owners * stride, LANES), F32),
            pltpu.VMEM((half, LANES), F32),
            pltpu.VMEM((half, LANES), F32),
        ],
        compiler_params=params(48),
        name="send",
    )(slot, d_inputs)
    from_one, rest, sent = lax.optimization_barrier((from_one, rest, sent))
    back = in_plane(sent)
    to_two = lax.optimization_barrier([keep[k, 0, 1] + got[k, 0, 1] + from_one[k][1] for k in range(2)])
    from_two = [by_near(to_two[0]), by_tower(to_two[1])]
    rest = rest + by_near(rest)
    for bit in [4 << k for k in range(groups.bit_length() - 1)]:
        rest = rest + flip(rest, "batch", bit, batch)
    from_two, rest, back = lax.optimization_barrier((from_two, rest, back))
    blocks_t = (rows_own // 256 * tall, 256)
    both = [keep[k, 0, 0] + got[k, 0, 0] + from_one[k][0] + from_two[k] for k in range(2)]
    both = lax.optimization_barrier([part[k] for part in both for k in range(groups // 2)])
    from_far = [flip(both[k], "batch", k * 4, batch) for k in range(1, groups)]
    both, back = lax.optimization_barrier((both, back))
    table_own, table_other = pl.pallas_call(
        functools.partial(table_kernel, embed, slots, stride),
        out_shape=(jax.ShapeDtypeStruct(blocks_t, F32), jax.ShapeDtypeStruct((groups - 1,) + blocks_t, BF16)),
        in_specs=[in_smem()] + [in_vmem()] * 2,
        out_specs=(in_vmem(),) * 2,
        scratch_shapes=[pltpu.VMEM((groups,) + blocks_t, F32)],
        compiler_params=params(32),
        name="table",
    )(spot, arrived, back)
    from_far, table_own, table_other = lax.optimization_barrier((from_far, table_own, table_other))
    summed = both[0].astype(F32)
    for part in from_far:
        summed = summed + part.astype(F32)
    chunk = flip_far(summed[:rows_c].astype(BF16), batch, groups)
    table_got = [flip(table_other[k - 1], "batch", k * 4, batch) for k in range(1, groups)]
    across = flip(chunk, "batch", 2, batch)
    vector_grad = jnp.concatenate(
        [rest[6, :width], rest[7, :width], rest[11, :hidden], rest[12, :width], rest[13, :hidden], rest[14, :1]]
    )
    vector_one, vector_two, vector_new = adamw(vectors, vector_grad, vector_first, vector_second, 0.03)
    tail = lax.dynamic_slice_in_dim(rest[8 : 8 + width - main], (tower * batch + place) * deep_rows, deep_rows, 1).T
    deep_grad = jnp.concatenate([summed[rows_c:], tail], axis=1)
    deep_one, deep_two, deep_new = adamw(deep_weight, deep_grad, deep_first, deep_second, 0.03)
    deep_copy = deep_new.astype(BF16)
    side = rest[:8][None]
    shape_t = jax.ShapeDtypeStruct((embed, rows_own), F32)
    table_grad, table_one, table_two, table_new = pl.pallas_call(
        update_kernel,
        out_shape=(shape_t,) * 4,
        in_specs=[in_vmem()] * (3 + groups),
        out_specs=(in_vmem(),) * 4,
        compiler_params=params(32),
        name="update",
    )(table_own, table_t, table_first.T, table_second.T, *table_got)
    (
        across, side, vector_grad, vector_one, vector_two, vector_new,
        deep_grad, deep_one, deep_two, deep_new, deep_copy, table_grad, table_one, table_two, table_new,
    ) = lax.optimization_barrier(
        (
            across, side, vector_grad, vector_one, vector_two, vector_new,
            deep_grad, deep_one, deep_two, deep_new, deep_copy, table_grad, table_one, table_two, table_new,
        )
    )
    chunk = jnp.stack([chunk, across])
    partner = flip(chunk, "batch", 1, batch)
    blocks = batch // 2
    rows = 2 * rows_c

    def relative(block, at):
        other = jnp.minimum(block, blocks - 1) ^ (at[0] >> 1)
        return (other & 1, other >> 1, 0, 0)

    piece = pl.BlockSpec((1, 1, rows_c, main), relative)
    slab = pl.BlockSpec((rows, 1, width), lambda block, at: (block, 0, 0))
    shape_c = jax.ShapeDtypeStruct((width, 1, width), F32)
    cross_out = pl.pallas_call(
        cross_kernel,
        grid_spec=pltpu.PrefetchScalarGridSpec(
            num_scalar_prefetch=1,
            grid=(blocks + 1,),
            in_specs=[piece, piece, pl.BlockSpec((1, 8, wide), lambda block, at: (0, 0, 0)), slab, slab, slab],
            out_specs=(slab, slab, slab, slab, pl.BlockSpec((rows, width), lambda block, at: (block, 0))),
        ),
        out_shape=(shape_c,) * 4 + (jax.ShapeDtypeStruct((width, width), BF16),),
        compiler_params=params(48),
        name="cross",
    )(
        place.reshape(1), chunk, partner, side,
        cross_weight.transpose(1, 0, 2), cross_first.transpose(1, 0, 2), cross_second.transpose(1, 0, 2),
    )
    cross_grad, cross_one, cross_two, cross_new = (x.transpose(1, 0, 2) for x in cross_out[:4])
    loss_sum = rest[14, 1]
    return (
        loss_sum,
        count[0, 0],
        cross_grad,
        cross_one,
        cross_two,
        cross_new,
        cross_out[4][None],
        deep_grad,
        deep_one,
        deep_two,
        deep_new,
        deep_copy,
        table_grad.T,
        table_one.T,
        table_two.T,
        table_new.T,
        vector_grad,
        vector_one,
        vector_two,
        vector_new,
    )


def solution(mesh):
    both = P(("tower", "batch"), None)
    cross = P("tower", None, None)
    return jax.shard_map(
        local,
        mesh=mesh,
        in_specs=(
            P("batch", None),
            P("batch", None),
            P("batch"),
            P("batch"),
            both,
            both,
            both,
            cross,
            cross,
            cross,
            both,
            both,
            both,
            P(),
            P(),
            P(),
        ),
        out_specs=(P(), P()) + (cross,) * 5 + (both,) * 9 + (P(),) * 4,
        check_vma=False,
    )
```

```python
import functools

import jax
import jax.numpy as jnp
from jax import lax
from jax.experimental import pallas as pl
from jax.experimental.pallas import tpu as pltpu
from jax.sharding import PartitionSpec as P

STEP = 5
LANES = 128
CHUNK = 128
BF16 = jnp.bfloat16
F32 = jnp.float32


def round_up(value, unit):
    return -(-value // unit) * unit


def adamw(weight, grad, first, second, rate):
    first_new = 0.9 * first + 0.1 * grad
    second_new = 0.999 * second + 0.001 * grad * grad
    update = (
        first_new / (1.0 - 0.9**STEP) / (jnp.sqrt(second_new / (1.0 - 0.999**STEP)) + 1e-08)
        + 0.01 * weight
    )
    return (first_new, second_new, weight - rate * update)


def contract(left, right, left_dim, right_dim):
    return lax.dot_general(
        left, right, (((left_dim,), (right_dim,)), ((), ())), preferred_element_type=F32
    )


def iota(shape, dim):
    return lax.broadcasted_iota(jnp.int32, shape, dim)


def in_vmem():
    return pl.BlockSpec(memory_space=pltpu.VMEM)


def in_smem():
    return pl.BlockSpec(memory_space=pltpu.SMEM)


def params(mib):
    return pltpu.CompilerParams(vmem_limit_bytes=mib * 2**20)


def takes(micros):
    return pl.CostEstimate(flops=0, bytes_accessed=micros * 3_000_000, transcendentals=0)


def slots_kernel(shift, slots, stride, groups, ids_ref, valid_ref, table_ref, asked_ref, place_ref, low_ref):
    feats, half = ids_ref.shape
    owners = asked_ref.shape[0]
    embed, rows_own = table_ref.shape
    real = jnp.sum(valid_ref[...].astype(F32), axis=1, keepdims=True)
    high_real = jnp.floor(real * (1.0 / 64.0))
    spare = (low_ref.shape[0] - embed, rows_own)
    lane = iota(spare, 1)
    counts = jnp.where(lane == 0, high_real, jnp.where(lane == 1, real - 64.0 * high_real, 0.0))
    low_ref[...] = jnp.concatenate([table_ref[...], counts], axis=0).astype(BF16)
    before = (iota((half, half), 0) < iota((half, half), 1)).astype(BF16)
    owner_of = iota((owners, half), 0)
    slot_of = iota((slots, half), 0)
    base = jnp.zeros((owners, 1), F32)
    total = jnp.zeros((slots, 2 * owners), F32)
    for feat in range(feats):
        ids = ids_ref[feat : feat + 1, :]
        owner = lax.shift_right_logical(ids, shift)
        plane = lax.shift_right_logical(owner, (4 * groups).bit_length() - 1) * 4 + (owner & 3)
        owner = plane * groups + (lax.shift_right_logical(owner, 2) & (groups - 1))
        row = ids & ((1 << shift) - 1)
        hit = (owner_of == owner).astype(F32)
        earlier = contract(hit.astype(BF16), before, 1, 0) + base
        rank = jnp.sum(hit * earlier, axis=0, keepdims=True)
        base = base + jnp.sum(hit, axis=1, keepdims=True)
        rank = rank.astype(jnp.int32)
        spot = owner * stride + rank
        for k in range(half // LANES):
            at = feat * (half // LANES) + k
            place_ref[at : at + 1, :] = spot[:, k * LANES : k * LANES + LANES]
        high = lax.shift_right_logical(row, 8).astype(F32)
        low = (row & 255).astype(F32)
        values = jnp.concatenate([hit * high, hit * low], axis=0).astype(BF16)
        put = (slot_of == rank).astype(F32).astype(BF16)
        total = total + contract(put, values, 1, 1)
    rows = total[:, :owners] * 256.0 + total[:, owners:]
    tall = round_up(slots, LANES)
    if tall > slots:
        rows = jnp.concatenate([rows, jnp.zeros((tall - slots, owners), F32)], axis=0)
    wide = asked_ref.shape[1]
    flat = rows.T
    if wide > tall:
        flat = jnp.concatenate([flat, jnp.zeros((owners, wide - tall), F32)], axis=1)
    asked_ref[...] = flat.astype(jnp.int32)


def lookup_kernel(embed, stride, spot_ref, ids_ref, *refs):
    tables, (rows_ref, blocks_ref) = refs[:-2], refs[-2:]
    groups = len(tables)
    tall, rows_own = tables[0].shape
    parts = rows_own // 256
    wide = ids_ref.shape[1]
    third = stride // 3
    count = jnp.zeros((1, 1), F32)
    for k, table_ref in enumerate(tables):
        table = table_ref[...].astype(F32)
        count = count + 64.0 * table[embed : embed + 1, 0:1] + table[embed : embed + 1, 1:2]
        table = jnp.where(iota((tall, rows_own), 0) < embed, table, 0.0)
        block = jnp.concatenate([table[:, part * 256 : part * 256 + 256] for part in range(parts)], axis=0)
        blocks_ref[spot_ref[1] ^ k] = block.astype(BF16)
    low_of = iota((256, wide), 0)
    high_count = jnp.floor(count * (1.0 / 64.0))
    row, lane = iota((third, LANES), 0), iota((third, LANES), 1)
    counts = jnp.where(lane == LANES - 2, high_count, jnp.where(lane == LANES - 1, count - 64.0 * high_count, 0.0))
    counts = jnp.where(row == 0, counts, 0.0)

    def step(peer, carry):
        for group in range(groups):
            block = peer * groups + group
            ids = ids_ref[pl.ds(block, 1), :]
            high = lax.shift_right_logical(ids, 8)
            pick = (low_of == (ids & 255)).astype(F32).astype(BF16)
            found = contract(blocks_ref[group], pick, 1, 0)
            mine = jnp.zeros((tall, wide), F32)
            for part in range(parts):
                mine = jnp.where(high == part, found[part * tall : part * tall + tall], mine)
            square = jnp.concatenate([mine, jnp.zeros((LANES - tall, wide), F32)], axis=0).T
            packed = square[:third] if group else square[:third] + counts
            for piece in (1, 2):
                packed = packed + pltpu.roll(square[piece * third : piece * third + third], embed * piece, 1)
            rows_ref[pl.ds(pl.multiple_of(block * third, 16), third), :] = packed.astype(BF16)
        return carry

    lax.fori_loop(0, ids_ref.shape[0] // groups, step, 0)


def column_map(feat, dense_width, embed, turned):
    start = dense_width + embed * feat
    tile = start // LANES
    shape = (2 * LANES, LANES) if turned else (LANES, 2 * LANES)
    column, lane = iota(shape, 1 - turned), iota(shape, turned)
    hit = (column == lane + (start - tile * LANES)) & (lane < embed)
    return pl.multiple_of(tile * LANES, LANES), hit.astype(F32).astype(BF16)


def inputs_kernel(
    feats, stride, groups, embed, dense_width, place_ref, rows_ref, dense_ref, x_ref, count_ref, far_ref, even_ref, odd_ref, sum_ref
):
    half = even_ref.shape[0]
    third = stride // 3
    width = dense_width + embed * feats

    def unpack(owner, carry):
        block = rows_ref[pl.ds(pl.multiple_of(owner * third, 16), third), :].astype(F32)
        for piece in range(3):
            rolled = block if piece == 0 else pltpu.roll(block, LANES - embed * piece, 1)
            far_ref[pl.ds(pl.multiple_of(owner * stride + piece * third, 16), third), :] = rolled
        return carry

    owners = far_ref.shape[0] // stride
    lax.fori_loop(0, owners, unpack, 0, unroll=4)
    counts = jnp.zeros((16, LANES), F32)
    for peer in range(owners // groups):
        start = peer * groups * third
        counts = counts + rows_ref[start : start + 16, :].astype(F32)
    count_ref[...] = 64.0 * counts[0:1, LANES - 2 : LANES - 1] + counts[0:1, LANES - 1 : LANES]
    sum_ref[...] = jnp.zeros_like(sum_ref)
    sum_ref[:, :LANES] = dense_ref[...].astype(F32)
    ones = width - width // LANES * LANES
    end = slice(width // LANES * LANES, width // LANES * LANES + LANES)
    sum_ref[:, end] += (iota((half, LANES), 1) == ones).astype(F32)
    odd_ref[...] = jnp.zeros_like(odd_ref)

    def add(ref, at, spread):
        start, spread = spread
        here = slice(at, at + CHUNK)
        sum_ref[here, pl.ds(start, 2 * LANES)] += contract(ref[here, :].astype(BF16), spread, 1, 0)

    def fetch(feat, ref, at):
        rows = [far_ref[pl.ds(place_ref[feat * half + at + k], 1), :] for k in range(CHUNK)]
        for k in range(CHUNK):
            ref[at + k : at + k + 1, :] = rows[k]

    def step(pair, carry):
        spread = column_map(jnp.maximum(2 * pair - 1, 0), dense_width, embed, 0)
        for at in range(0, half, CHUNK):
            add(odd_ref, at, spread)
            fetch(2 * pair, even_ref, at)
        spread = column_map(2 * pair, dense_width, embed, 0)
        for at in range(0, half, CHUNK):
            add(even_ref, at, spread)
            fetch(2 * pair + 1, odd_ref, at)
        return carry

    lax.fori_loop(0, feats // 2, step, 0)
    spread = column_map(feats - 1, dense_width, embed, 0)
    for at in range(0, half, CHUNK):
        add(odd_ref, at, spread)
    x_ref[...] = sum_ref[...].astype(BF16)


def send_kernel(feats, slots, stride, embed, dense_width, place_ref, dx_ref, rows_ref, far_ref, even_ref, odd_ref):
    half = even_ref.shape[0]
    third = stride // 3
    owners = far_ref.shape[0] // stride

    def clear(owner, carry):
        gap = stride - slots
        far_ref[pl.ds(pl.multiple_of(owner * stride + slots, 8), gap), :] = jnp.zeros((gap, LANES), F32)
        return carry

    lax.fori_loop(0, owners, clear, 0, unroll=8)

    def cut(ref, at, spread):
        start, spread = spread
        here = slice(at, at + CHUNK)
        ref[here, :] = contract(dx_ref[here, pl.ds(start, 2 * LANES)], spread, 1, 0)

    def put(feat, ref, at):
        rows = [ref[at + k : at + k + 1, :] for k in range(CHUNK)]
        for k in range(CHUNK):
            far_ref[pl.ds(place_ref[feat * half + at + k], 1), :] = rows[k]

    spread = column_map(0, dense_width, embed, 1)
    for at in range(0, half, CHUNK):
        cut(even_ref, at, spread)

    def step(pair, carry):
        spread = column_map(2 * pair + 1, dense_width, embed, 1)
        for at in range(0, half, CHUNK):
            cut(odd_ref, at, spread)
            put(2 * pair, even_ref, at)
        spread = column_map(jnp.minimum(2 * pair + 2, feats - 1), dense_width, embed, 1)
        for at in range(0, half, CHUNK):
            cut(even_ref, at, spread)
            put(2 * pair + 1, odd_ref, at)
        return carry

    lax.fori_loop(0, feats // 2, step, 0)

    def pack(owner, carry):
        packed = jnp.zeros((third, LANES), F32)
        for piece in range(3):
            block = far_ref[pl.ds(pl.multiple_of(owner * stride + piece * third, 8), third), :]
            packed = packed + (block if piece == 0 else pltpu.roll(block, embed * piece, 1))
        rows_ref[pl.ds(pl.multiple_of(owner * third, 16), third), :] = packed.astype(BF16)
        return carry

    lax.fori_loop(0, owners, pack, 0, unroll=4)


def table_kernel(embed, slots, stride, spot_ref, ids_ref, rows_ref, own_ref, other_ref, total_ref):
    groups, size = total_ref.shape[:2]
    tall = round_up(embed, 8)
    parts = size // tall
    wide = ids_ref.shape[1]
    third = stride // 3
    low_of = iota((256, wide), 0)
    lane = iota((1, wide), 1)
    total_ref[...] = jnp.zeros_like(total_ref)

    def step(peer, carry):
        for group in range(groups):
            at = peer * groups + group
            ids = jnp.where(lane < slots, ids_ref[pl.ds(at, 1), :], -1)
            high = lax.shift_right_arithmetic(ids, 8)
            pick = (low_of == (ids & 255)).astype(F32).astype(BF16)
            block = rows_ref[pl.ds(pl.multiple_of(at * third, 16), third), :].astype(F32)
            pieces = [block if k == 0 else pltpu.roll(block, LANES - embed * k, 1) for k in range(3)]
            if wide > stride:
                pieces.append(jnp.zeros((wide - stride, LANES), F32))
            square = jnp.concatenate(pieces, axis=0)[:wide].T
            mine = jnp.where(iota((tall, wide), 0) < embed, square[:tall], 0.0)
            spread = [jnp.where(high == part, mine, 0.0) for part in range(parts)]
            total_ref[group] += contract(jnp.concatenate(spread, axis=0).astype(BF16), pick, 1, 1)
        return carry

    lax.fori_loop(0, ids_ref.shape[0] // groups, step, 0)
    own_ref[...] = total_ref[spot_ref[1]]
    for k in range(1, groups):
        other_ref[k - 1] = total_ref[spot_ref[1] ^ k].astype(BF16)


def update_kernel(*refs):
    own_ref, table_ref, first_ref, second_ref = refs[:4]
    others = refs[4:-4]
    grad_ref, first_new_ref, second_new_ref, table_new_ref = refs[-4:]
    embed, rows_own = table_ref.shape
    tall = round_up(embed, 8)
    total = own_ref[...]
    for ref in others:
        total = total + ref[...].astype(F32)
    for part in range(rows_own // 256):
        here = slice(part * 256, part * 256 + 256)
        grad = total[part * tall : part * tall + embed, :]
        one, two, new = adamw(table_ref[:, here], grad, first_ref[:, here], second_ref[:, here], 0.25)
        grad_ref[:, here] = grad
        first_new_ref[:, here] = one
        second_new_ref[:, here] = two
        table_new_ref[:, here] = new


def tiles(size):
    return [(at, min(256, size - at)) for at in range(0, size, 256)]


def towers_kernel(
    spot_ref, count_ref, bias_ref, x_ref, vec_ref, labels_ref,
    own_ref, half_ref, half_core_ref, here_ref, here_core_ref, near_ref, near_core_ref,
    one_ref, d_second_ref, d_first_ref, d_deep_ref, dx_ref, head_ref,
    cross_ref, all_deep_ref, pre_first_ref, layer_ref, pre_second_ref, two_ref, slope_ref, hidden_ref, arrival,
):
    half, wide = x_ref.shape
    groups, _, deep_rows = here_ref.shape[:3]
    hidden = 8 * groups * deep_rows
    tower, near, core = spot_ref[0], spot_ref[2], spot_ref[3]
    middle = half_ref.shape[0]
    moves = [(own_ref, cross_ref.at[tower, pl.ds(0, 2 * middle), :])]
    for ref, at_core in ((half_ref, core), (half_core_ref, 1 - core)):
        moves.append((ref, cross_ref.at[1 - tower, pl.ds(pl.multiple_of(at_core * middle, 16), middle), :]))
    for ref, at_near, at_core in (
        (here_ref, near, core), (here_core_ref, near, 1 - core), (near_ref, 1 - near, core), (near_core_ref, 1 - near, 1 - core)
    ):
        for k in range(2):
            moves.append((ref.at[:, k], all_deep_ref.at[k, :, at_near, at_core]))
    copies = []
    for k, (source, target) in enumerate(moves):
        copies.append(pltpu.make_async_copy(source, target, arrival.at[k]))
        copies[-1].start()

    def deep_block(at, size):
        tower, at = at // (hidden // 2), at % (hidden // 2)
        block = all_deep_ref[tower, pl.ds(at // (4 * deep_rows), size // (4 * deep_rows))]
        return block.reshape(size, wide)

    def lanes(x):
        total = x[:, :LANES]
        for at in range(LANES, x.shape[1], LANES):
            total = total + x[:, at : at + LANES]
        return total

    if 2 * middle < wide:
        cross_ref[:, 2 * middle :, :] = jnp.zeros((2, wide - 2 * middle, wide), BF16)
    for copy in copies[:3]:
        copy.wait()
    for at, size in tiles(wide):
        here = slice(at, at + size)
        base = x_ref[:, here].astype(F32)
        pre = contract(x_ref[...], cross_ref[0, :, here], 1, 0) + vec_ref[0:1, here]
        layer = base * pre + base
        pre_first_ref[:, here] = pre
        layer_ref[:, here] = layer
        one_ref[:, here] = layer.astype(BF16)
    score = jnp.zeros((half, LANES), F32)
    for at, size in tiles(wide):
        here = slice(at, at + size)
        base = x_ref[:, here].astype(F32)
        pre = contract(one_ref[...], cross_ref[1, :, here], 1, 0) + vec_ref[1:2, here]
        two = (base * pre + layer_ref[:, here]).astype(BF16)
        pre_second_ref[:, here] = pre
        two_ref[:, here] = two
        score = score + lanes(two.astype(F32) * vec_ref[3:4, here])
    for copy in copies[3:]:
        copy.wait()
    for at, size in tiles(hidden):
        here = slice(at, at + size)
        pre = contract(x_ref[...], deep_block(at, size), 1, 1) + vec_ref[2:3, here]
        gate = jax.nn.sigmoid(pre)
        out = (pre * gate).astype(BF16)
        hidden_ref[:, here] = out
        slope_ref[:, here] = gate * (1.0 + pre * (1.0 - gate))
        score = score + lanes(out.astype(F32) * vec_ref[4:5, here])
    logit = jnp.sum(score, axis=1, keepdims=True) + bias_ref[0, 0]
    labels = jnp.concatenate([labels_ref[...], jnp.zeros((6, half), jnp.int32)], axis=0).astype(F32).T
    target, valid = labels[:, 0:1], labels[:, 1:2]
    softplus = jnp.maximum(logit, 0.0) + jnp.log1p(jnp.exp(-jnp.abs(logit)))
    loss = jnp.sum(valid * (softplus - target * logit), axis=0, keepdims=True)
    d_logit = valid * (jax.nn.sigmoid(logit) - target) / count_ref[0, 0]
    bias_grad = jnp.sum(d_logit, axis=0, keepdims=True)
    lane = iota((1, wide), 1)
    head_ref[...] = jnp.zeros_like(head_ref)
    head_ref[2:3, :] = jnp.where(lane == 0, bias_grad, jnp.where(lane == 1, loss, 0.0))
    for at, size in tiles(wide):
        here = slice(at, at + size)
        base = x_ref[:, here].astype(F32)
        d_second_ref[:, here] = (d_logit * vec_ref[3:4, here] * base).astype(BF16)
        head_ref[0:1, here] = jnp.sum(d_logit * two_ref[:, here].astype(F32), axis=0, keepdims=True)
    for at, size in tiles(hidden):
        here = slice(at, at + size)
        d_deep_ref[:, here] = (d_logit * vec_ref[4:5, here] * slope_ref[:, here]).astype(BF16)
        head_ref[1:2, here] = jnp.sum(d_logit * hidden_ref[:, here].astype(F32), axis=0, keepdims=True)
    for at, size in tiles(wide):
        here = slice(at, at + size)
        base = x_ref[:, here].astype(F32)
        d_two = d_logit * vec_ref[3:4, here]
        d_one = contract(d_second_ref[...], cross_ref[1, here, :], 1, 1) + d_two
        d_first_ref[:, here] = (d_one * base).astype(BF16)
        layer_ref[:, here] = d_one * (1.0 + pre_first_ref[:, here]) + d_two * pre_second_ref[:, here]
    for at, size in tiles(wide):
        here = slice(at, at + size)
        columns = all_deep_ref[:, :, :, :, :, here].reshape(hidden, size)
        dx = contract(d_first_ref[...], cross_ref[0, here, :], 1, 1) + contract(d_deep_ref[...], columns, 1, 0)
        dx_ref[:, here] = (dx + layer_ref[:, here]).astype(BF16)


def grads_kernel(
    deep_rows, spot_ref, x_ref, one_ref, d_second_ref, d_first_ref, d_deep_ref, head_ref,
    keep_ref, give_ref, rest_ref, turned_ref,
):
    half, wide = x_ref.shape
    hidden = d_deep_ref.shape[1]
    mid, rows, main = keep_ref.shape[3:]
    towers, groups, pairs = 2, 2 * mid, 2
    rows_c = rows - deep_rows
    even = spot_ref[3] == 0

    def share(value, tower, at, size, chunk, first):
        by_tower = tower ^ spot_ref[0]
        for group in range(groups):
            by_far = group ^ spot_ref[1]
            upper = by_far // mid
            for pair in range(pairs):
                by_near = pair ^ spot_ref[2]
                one = by_tower + upper * (by_near - by_tower)
                two = by_near + upper * (by_tower - by_near)
                start = (group * pairs + pair) * 2 * chunk
                low, high = value[start : start + chunk], value[start + chunk : start + 2 * chunk]
                place = (upper, one, two, by_far % mid, slice(first, first + chunk), slice(at, at + size))
                keep_ref[place] = jnp.where(even, low, high).astype(BF16)
                give_ref[place] = jnp.where(even, high, low).astype(BF16)

    rest_ref[...] = jnp.zeros_like(rest_ref)
    for tower, (left, right) in enumerate(((one_ref, d_second_ref), (x_ref, d_first_ref))):
        tower = 1 - tower
        turned_ref[...] = left[...].T
        for at, size in tiles(main):
            value = contract(turned_ref[...], right[:, at : at + size], 1, 0)
            share(value, tower, at, size, rows_c, 0)
            rest_ref[16 * tower : 16 * tower + 3, at : at + size] = value[main : main + 3]
            rest_ref[6 + tower : 7 + tower, at : at + size] = value[main + 3 : main + 4]
        value = contract(turned_ref[...], right[:, main:wide], 1, 0)
        rest_ref[16 * tower : 16 * tower + 3, main:wide] = value[main : main + 3]
        rest_ref[6 + tower : 7 + tower, main:wide] = value[main + 3 : main + 4]
        rest_ref[16 * tower + 3 : 16 * tower + 6, :main] = value[:main].T[:3]
    bias = contract(turned_ref[main:wide, :], d_deep_ref[...], 1, 0)
    rest_ref[8:12, :hidden] = bias[:4]
    rest_ref[12:15, :] = head_ref[0:3, :]
    mine, other = rest_ref[0:8, :], rest_ref[16:24, :]
    swap = (iota((8, wide), 0) < 6) & (iota((8, wide), 1) >= wide * (1 - spot_ref[0]))
    rest_ref[0:8, :] = jnp.where(swap, other, mine)
    rest_ref[16:24, :] = jnp.where(swap, mine, other)
    turned_ref[:hidden, :] = d_deep_ref[...].T
    for at, size in tiles(main):
        value = contract(turned_ref[:hidden, :], x_ref[:, at : at + size], 1, 0)
        for tower in range(towers):
            share(value[tower * (hidden // towers) : (tower + 1) * (hidden // towers)], tower, at, size, deep_rows, rows_c)


def cross_kernel(
    other, blocks, place_ref, near_ref, far_ref, rest_ref, weight_ref, first_ref, second_ref, *refs
):
    held_ref, made_ref, arrival, departure = refs[-4:]
    sources, targets, copy_ref = (weight_ref, first_ref, second_ref), refs[-9:-5], refs[-5]
    step, full = pl.program_id(0), blocks // 2
    width = weight_ref.shape[2]
    half, main = near_ref.shape[1:]
    rows = 2 * half
    even = (place_ref[0] & 1) == 0

    def moves(at, size, inward):
        start = pl.multiple_of(cross_block(other, blocks, at, place_ref) * rows, 8)
        pairs = []
        for k, ref in enumerate(sources if inward else targets):
            outside = ref.at[pl.ds(start, size), 0, :]
            inside = (held_ref if inward else made_ref).at[k, at, pl.ds(0, size), :]
            if inward:
                pairs.append(pltpu.make_async_copy(outside, inside, arrival.at[k, at]))
            else:
                pairs.append(pltpu.make_async_copy(inside, outside, departure.at[k, at]))
        return pairs

    spans = [(at, rows) for at in range(full)] + [(full, width - main)] * other

    @pl.when(step == 0)
    def _():
        for at, size in spans:
            for move in moves(at, size, True):
                move.start()

    def update(at, columns, grad):
        here = (slice(at, at + grad.shape[0]), columns)
        weight, first, second = (held_ref[(k, step) + here] for k in range(3))
        one, two, new = adamw(weight, grad, first, second, 0.03)
        for k, value in enumerate((grad, one, two, new)):
            made_ref[(k, step) + here] = value
        copy_ref[here] = new.astype(BF16)

    @pl.when(step < full)
    def _():
        for move in moves(step, rows, True):
            move.wait()
        for at in range(0, main, 256):
            columns = slice(at, min(at + 256, main))
            near, far = near_ref[0, :, columns].astype(F32), far_ref[0, :, columns].astype(F32)
            update(0, columns, jnp.where(even, near, far))
            update(half, columns, jnp.where(even, far, near))
        block = cross_block(other, blocks, step, place_ref)
        lane = pl.multiple_of(block * rows // LANES * LANES, LANES)
        side = rest_ref[0, :, pl.ds(lane, LANES)]
        side = jnp.concatenate([side, jnp.zeros((LANES - 8, LANES), F32)], axis=0).T
        parts = [side[at : at + rows] for at in range(0, LANES, rows)]
        side = parts[0]
        for k, part in enumerate(parts):
            side = jnp.where(block % len(parts) == k, part, side)
        update(0, slice(main, width), side[:, 3 : 3 + width - main])
        for move in moves(step, rows, False):
            move.start()

    if other:

        @pl.when(step == full)
        def _():
            for move in moves(full, width - main, True):
                move.wait()
            update(0, slice(0, width), rest_ref[0, :, :width])
            for move in moves(full, width - main, False):
                move.start()

    @pl.when(step == pl.num_programs(0) - 1)
    def _():
        for at, size in spans:
            for move in moves(at, size, False):
                move.wait()


def cross_block(other, blocks, step, place_ref):
    block = step * 2 + (((place_ref[0] >> 1) & 1) ^ other)
    return jnp.where(step == blocks // 2, blocks, block)


def flip(x, axis, bit, size):
    return lax.ppermute(x, axis, [(i, i ^ bit) for i in range(size)])


def pick(x, axis, index):
    return lax.dynamic_index_in_dim(x, index, axis, keepdims=False)


def join(mine, other, axis, index):
    return jnp.where(index == 0, jnp.stack([mine, other], axis), jnp.stack([other, mine], axis))


def flip_far(x, batch, groups):
    return jnp.stack([x] + [flip(x, "batch", k * 4, batch) for k in range(1, groups)])


def in_order(parts, groups):
    far = lax.axis_index("batch") // 4
    return jnp.stack([pick(parts, 0, k ^ far) for k in range(groups)])


def local(
    dense_feats,
    category_ids,
    labels,
    valid_mask,
    embed_table,
    table_first,
    table_second,
    cross_weight,
    cross_first,
    cross_second,
    deep_weight,
    deep_first,
    deep_second,
    vectors,
    vector_first,
    vector_second,
):
    towers, batch = lax.axis_size("tower"), lax.axis_size("batch")
    owners = towers * batch
    tower, place = lax.axis_index("tower"), lax.axis_index("batch")
    core, near, far = place & 1, (place >> 1) & 1, place >> 2
    groups = batch // 4
    spot = jnp.stack([tower, far, near, core])
    rows_own, embed = embed_table.shape
    examples, feats = category_ids.shape
    half = examples // towers
    width = cross_weight.shape[1]
    deep_rows = deep_weight.shape[0]
    hidden = deep_rows * owners
    dense_width = dense_feats.shape[1]
    wide = round_up(width, LANES)
    slots = half * feats // owners
    third = round_up(-(-slots // 3), 16)
    stride = 3 * third
    shift = rows_own.bit_length() - 1
    asked_wide = round_up(stride, LANES)

    def mine(x, dim):
        return lax.dynamic_slice_in_dim(x, tower * half, half, dim)

    ids = mine(category_ids.T, 1)
    valid = mine(valid_mask, 0)
    target = mine(labels, 0)
    dense = jnp.pad(mine(dense_feats, 0), ((0, 0), (0, LANES - dense_width)))

    table_t = embed_table.T
    tall = round_up(embed, 8)
    asked, slot, table_low = pl.pallas_call(
        functools.partial(slots_kernel, shift, slots, stride, groups),
        out_shape=(
            jax.ShapeDtypeStruct((owners, asked_wide), jnp.int32),
            jax.ShapeDtypeStruct((feats * half // LANES, LANES), jnp.int32),
            jax.ShapeDtypeStruct((tall, rows_own), BF16),
        ),
        in_specs=[in_vmem()] * 3,
        out_specs=(in_vmem(),) * 3,
        compiler_params=params(32),
        name="slots",
    )(ids, valid.reshape(1, half), table_t)
    slot = slot.reshape(-1)
    planes = [[t * batch + z * 4 + k for t in range(towers) for k in range(4)] for z in range(groups)]

    def in_plane(x):
        return lax.all_to_all(
            x, ("tower", "batch"), split_axis=0, concat_axis=0, axis_index_groups=planes, tiled=True
        )

    tables = [table_low] + [flip(table_low, "batch", k * 4, batch) for k in range(1, groups)]

    main = width // LANES * LANES
    rows_c = main // batch
    middle = round_up(-(-width // 2), 16)
    own_low = jnp.pad(cross_weight[0].astype(BF16), ((0, 2 * middle - width), (0, wide - width)))
    deep_own = jnp.pad(deep_weight.astype(BF16), ((0, 0), (0, wide - width)))
    asked, deep_own = lax.optimization_barrier((asked, deep_own))
    arrived = in_plane(asked)
    deep_pair = join(deep_own, flip(deep_own, "tower", 1, towers), 0, tower)
    tables[1:], own_low, arrived = lax.optimization_barrier((tables[1:], own_low, arrived))
    got_low = flip(lax.dynamic_slice_in_dim(own_low, core * middle, middle, 0), "tower", 1, towers)
    weights = flip_far(deep_pair, batch, groups)
    found = pl.pallas_call(
        functools.partial(lookup_kernel, embed, stride),
        out_shape=jax.ShapeDtypeStruct((owners * third, LANES), BF16),
        in_specs=[in_smem()] + [in_vmem()] * (1 + groups),
        out_specs=in_vmem(),
        scratch_shapes=[pltpu.VMEM((groups, rows_own // 256 * tall, 256), BF16)],
        compiler_params=params(32),
        name="lookup",
    )(spot, arrived, *tables)
    returned = in_plane(found)
    weights = in_order(weights, groups)

    def widen(x):
        return jnp.pad(x, (0, wide - x.shape[0]))

    vec = jnp.stack(
        [
            widen(vectors[:width]),
            widen(vectors[width : 2 * width]),
            widen(vectors[2 * width : 2 * width + hidden]),
            widen(vectors[2 * width + hidden : 3 * width + hidden]).astype(BF16).astype(F32),
            widen(vectors[3 * width + hidden : 3 * width + 2 * hidden]).astype(BF16).astype(F32),
        ]
        + [jnp.zeros((wide,), F32)] * 3
    )
    returned, own_low, got_low, weights, vec = lax.optimization_barrier((returned, own_low, got_low, weights, vec))
    got_core = flip(got_low, "batch", 1, batch)
    weights_core = flip(weights, "batch", 1, batch)
    weights_near = flip(weights, "batch", 2, batch)
    inputs, count = pl.pallas_call(
        functools.partial(inputs_kernel, feats, stride, groups, embed, dense_width),
        out_shape=(jax.ShapeDtypeStruct((half, wide), BF16), jax.ShapeDtypeStruct((1, 1), F32)),
        in_specs=[in_smem(), in_vmem(), in_vmem()],
        out_specs=(in_vmem(), in_vmem()),
        scratch_shapes=[
            pltpu.VMEM((owners * stride, LANES), F32),
            pltpu.VMEM((half, LANES), F32),
            pltpu.VMEM((half, LANES), F32),
            pltpu.VMEM((half, wide), F32),
        ],
        compiler_params=params(48),
        name="inputs",
    )(slot, returned, dense)

    inputs, count, weights_near = lax.optimization_barrier((inputs, count, weights_near))
    weights_both = flip(weights_near, "batch", 1, batch)
    low = jax.ShapeDtypeStruct((half, wide), BF16)
    low_deep = jax.ShapeDtypeStruct((half, hidden), BF16)
    one_low, d_second, d_first, d_deep, d_inputs, heads = pl.pallas_call(
        towers_kernel,
        out_shape=(low, low, low, low_deep, low, jax.ShapeDtypeStruct((8, wide), F32)),
        in_specs=[in_smem()] * 3 + [in_vmem()] * 3 + [pl.BlockSpec(memory_space=pl.ANY)] * 7,
        out_specs=(in_vmem(),) * 6,
        scratch_shapes=[
            pltpu.VMEM((2, wide, wide), BF16),
            pltpu.VMEM((2, groups, 2, 2, deep_rows, wide), BF16),
            pltpu.VMEM((half, wide), F32),
            pltpu.VMEM((half, wide), F32),
            pltpu.VMEM((half, wide), F32),
            pltpu.VMEM((half, wide), BF16),
            pltpu.VMEM((half, hidden), F32),
            pltpu.VMEM((half, hidden), BF16),
            pltpu.SemaphoreType.DMA((11,)),
        ],
        compiler_params=params(56),
        name="towers",
    )(
        spot, count, vectors[-1:].reshape(1, 1), inputs, vec, jnp.stack([target, valid]),
        own_low, got_low, got_core, weights, weights_core, weights_near, weights_both,
    )
    parts = jax.ShapeDtypeStruct((2, 2, 2, groups // 2, rows_c + deep_rows, main), BF16)
    keep, give, rest = pl.pallas_call(
        functools.partial(grads_kernel, deep_rows),
        out_shape=(parts, parts, jax.ShapeDtypeStruct((24, wide), F32)),
        in_specs=[in_smem()] + [in_vmem()] * 6,
        out_specs=(in_vmem(),) * 3,
        scratch_shapes=[pltpu.VMEM((wide, half), BF16)],
        compiler_params=params(56),
        name="grads",
    )(spot, inputs, one_low, d_second, d_first, d_deep, heads)
    got = flip(give, "batch", 1, batch)
    rest = rest + flip(rest, "batch", 1, batch)

    def by_tower(x):
        return flip(x, "tower", 1, towers)

    def by_near(x):
        return flip(x, "batch", 2, batch)

    to_one, rest, d_inputs = lax.optimization_barrier(([keep[k, 1] + got[k, 1] for k in range(2)], rest, d_inputs))
    from_one = [by_tower(to_one[0]), by_near(to_one[1])]
    rest, cross_rest = rest[:16], jnp.concatenate([rest[16:22], rest[6:16]])
    diagonal = [(i, i ^ batch ^ 2) for i in range(owners)]
    diagonal = lax.ppermute(cross_rest, ("tower", "batch"), diagonal)
    rest = (rest + by_tower(cross_rest)) + (by_near(rest) + diagonal)
    sent = pl.pallas_call(
        functools.partial(send_kernel, feats, slots, stride, embed, dense_width),
        out_shape=jax.ShapeDtypeStruct((owners * third, LANES), BF16),
        in_specs=[in_smem(), in_vmem()],
        out_specs=in_vmem(),
        scratch_shapes=[
            pltpu.VMEM((owners * stride, LANES), F32),
            pltpu.VMEM((half, LANES), F32),
            pltpu.VMEM((half, LANES), F32),
        ],
        compiler_params=params(48),
        name="send",
    )(slot, d_inputs)
    from_one, rest, sent = lax.optimization_barrier((from_one, rest, sent))
    back = in_plane(sent)
    to_two = lax.optimization_barrier([keep[k, 0, 1] + got[k, 0, 1] + from_one[k][1] for k in range(2)])
    from_two = [by_near(to_two[0]), by_tower(to_two[1])]
    by_far = [flip(rest, "batch", k * 4, batch) for k in range(1, 4)]
    rest = (rest + by_far[0]) + (by_far[1] + by_far[2])
    for bit in [16 << k for k in range(groups.bit_length() - 3)]:
        rest = rest + flip(rest, "batch", bit, batch)
    from_two, rest, back = lax.optimization_barrier((from_two, rest, back))
    blocks_t = (rows_own // 256 * tall, 256)
    both = [keep[k, 0, 0] + got[k, 0, 0] + from_one[k][0] + from_two[k] for k in range(2)]
    both = lax.optimization_barrier([part[k] for part in both for k in range(groups // 2)])
    from_far = [flip(both[k], "batch", k * 4, batch) for k in range(1, groups)]
    both, back = lax.optimization_barrier((both, back))
    table_own, table_other = pl.pallas_call(
        functools.partial(table_kernel, embed, slots, stride),
        out_shape=(jax.ShapeDtypeStruct(blocks_t, F32), jax.ShapeDtypeStruct((groups - 1,) + blocks_t, BF16)),
        in_specs=[in_smem()] + [in_vmem()] * 2,
        out_specs=(in_vmem(),) * 2,
        scratch_shapes=[pltpu.VMEM((groups,) + blocks_t, F32)],
        compiler_params=params(32),
        name="table",
    )(spot, arrived, back)
    vector_grad = jnp.concatenate(
        [rest[6, :width], rest[7, :width], rest[11, :hidden], rest[12, :width], rest[13, :hidden], rest[14, :1]]
    )
    vector_one, vector_two, vector_new = adamw(vectors, vector_grad, vector_first, vector_second, 0.03)
    tail = lax.dynamic_slice_in_dim(rest[8 : 8 + width - main], (tower * batch + place) * deep_rows, deep_rows, 1).T
    from_far, table_own, table_other, tail, vector_grad, vector_one, vector_two, vector_new = lax.optimization_barrier(
        (from_far, table_own, table_other, tail, vector_grad, vector_one, vector_two, vector_new)
    )
    summed = both[0].astype(F32)
    for part in from_far:
        summed = summed + part.astype(F32)
    chunk = flip_far(summed[:rows_c].astype(BF16), batch, groups)
    deep_grad = jnp.concatenate([summed[rows_c:], tail], axis=1)
    deep_one, deep_two, deep_new = adamw(deep_weight, deep_grad, deep_first, deep_second, 0.03)
    deep_copy = deep_new.astype(BF16)
    chunk, deep_grad, deep_one, deep_two, deep_new, deep_copy = lax.optimization_barrier(
        (chunk, deep_grad, deep_one, deep_two, deep_new, deep_copy)
    )
    across = flip(chunk, "batch", 2, batch)
    side = rest[:8][None]
    table_got = [flip(table_other[k - 1], "batch", k * 4, batch) for k in range(1, groups)]
    cross_t = [x.transpose(1, 0, 2) for x in (cross_weight, cross_first, cross_second)]
    blocks = batch // 2
    rows = 2 * rows_c
    shape_c = jax.ShapeDtypeStruct((width, 1, width), F32)

    def update_cross(other, chunk, partner, done):
        def from_far(step, at):
            return (jnp.minimum(step, groups - 1) ^ (at[0] >> 2), 0, 0)

        piece = pl.BlockSpec((1, rows_c, main), from_far)
        low = pl.BlockSpec((rows, width), lambda step, at: (cross_block(other, blocks, step, at), 0))
        return pl.pallas_call(
            functools.partial(cross_kernel, other, blocks),
            grid_spec=pltpu.PrefetchScalarGridSpec(
                num_scalar_prefetch=1,
                grid=(groups + other,),
                in_specs=[piece, piece, pl.BlockSpec((1, 8, wide), lambda step, at: (0, 0, 0))]
                + [pl.BlockSpec(memory_space=pl.ANY)] * (3 + len(done)),
                out_specs=(pl.BlockSpec(memory_space=pl.ANY),) * 4 + (low,),
                scratch_shapes=[
                    pltpu.VMEM((3, groups + other, rows, width), F32),
                    pltpu.VMEM((4, groups + other, rows, width), F32),
                    pltpu.SemaphoreType.DMA((3, groups + other)),
                    pltpu.SemaphoreType.DMA((4, groups + other)),
                ],
            ),
            out_shape=(shape_c,) * 4 + (jax.ShapeDtypeStruct((width, width), BF16),),
            input_output_aliases={7 + k: k for k in range(len(done))},
            compiler_params=params(60),
            name="cross_other" if other else "cross",
        )(place.reshape(1), chunk, partner, side, *cross_t, *done)

    cross_out = update_cross(0, chunk, flip(chunk, "batch", 1, batch), ())
    cross_out, across, table_got = lax.optimization_barrier((cross_out, across, table_got))
    across_core = flip(across, "batch", 1, batch)
    shape_t = jax.ShapeDtypeStruct((embed, rows_own), F32)
    table_grad, table_one, table_two, table_new = pl.pallas_call(
        update_kernel,
        out_shape=(shape_t,) * 4,
        in_specs=[in_vmem()] * (3 + groups),
        out_specs=(in_vmem(),) * 4,
        compiler_params=params(32),
        name="update",
    )(table_own, table_t, table_first.T, table_second.T, *table_got)
    across_core, table_grad, table_one, table_two, table_new = lax.optimization_barrier(
        (across_core, table_grad, table_one, table_two, table_new)
    )
    cross_out = update_cross(1, across, across_core, cross_out)
    cross_grad, cross_one, cross_two, cross_new = (x.transpose(1, 0, 2) for x in cross_out[:4])
    loss_sum = rest[14, 1]
    return (
        loss_sum,
        count[0, 0],
        cross_grad,
        cross_one,
        cross_two,
        cross_new,
        cross_out[4][None],
        deep_grad,
        deep_one,
        deep_two,
        deep_new,
        deep_copy,
        table_grad.T,
        table_one.T,
        table_two.T,
        table_new.T,
        vector_grad,
        vector_one,
        vector_two,
        vector_new,
    )


def solution(mesh):
    both = P(("tower", "batch"), None)
    cross = P("tower", None, None)
    return jax.shard_map(
        local,
        mesh=mesh,
        in_specs=(
            P("batch", None),
            P("batch", None),
            P("batch"),
            P("batch"),
            both,
            both,
            both,
            cross,
            cross,
            cross,
            both,
            both,
            both,
            P(),
            P(),
            P(),
        ),
        out_specs=(P(), P()) + (cross,) * 5 + (both,) * 9 + (P(),) * 4,
        check_vma=False,
    )
```

```python
import functools

import jax
import jax.numpy as jnp
from jax import lax
from jax.experimental import pallas as pl
from jax.experimental.pallas import tpu as pltpu
from jax.sharding import PartitionSpec as P

STEP = 5
LANES = 128
CHUNK = 128
BF16 = jnp.bfloat16
F32 = jnp.float32


def round_up(value, unit):
    return -(-value // unit) * unit


def adamw(weight, grad, first, second, rate):
    first_new = 0.9 * first + 0.1 * grad
    second_new = 0.999 * second + 0.001 * grad * grad
    update = (
        first_new / (1.0 - 0.9**STEP) / (jnp.sqrt(second_new / (1.0 - 0.999**STEP)) + 1e-08)
        + 0.01 * weight
    )
    return (first_new, second_new, weight - rate * update)


def contract(left, right, left_dim, right_dim):
    return lax.dot_general(
        left, right, (((left_dim,), (right_dim,)), ((), ())), preferred_element_type=F32
    )


def iota(shape, dim):
    return lax.broadcasted_iota(jnp.int32, shape, dim)


def in_vmem():
    return pl.BlockSpec(memory_space=pltpu.VMEM)


def in_smem():
    return pl.BlockSpec(memory_space=pltpu.SMEM)


def params(mib):
    return pltpu.CompilerParams(vmem_limit_bytes=mib * 2**20)


def takes(micros):
    return pl.CostEstimate(flops=0, bytes_accessed=micros * 3_000_000, transcendentals=0)


def slots_kernel(shift, slots, stride, groups, ids_ref, valid_ref, table_ref, asked_ref, place_ref, low_ref):
    feats, half = ids_ref.shape
    owners = asked_ref.shape[0]
    embed, rows_own = table_ref.shape
    real = jnp.sum(valid_ref[...].astype(F32), axis=1, keepdims=True)
    high_real = jnp.floor(real * (1.0 / 64.0))
    spare = (low_ref.shape[0] - embed, rows_own)
    lane = iota(spare, 1)
    counts = jnp.where(lane == 0, high_real, jnp.where(lane == 1, real - 64.0 * high_real, 0.0))
    low_ref[...] = jnp.concatenate([table_ref[...], counts], axis=0).astype(BF16)
    before = (iota((half, half), 0) < iota((half, half), 1)).astype(BF16)
    owner_of = iota((owners, half), 0)
    slot_of = iota((slots, half), 0)
    base = jnp.zeros((owners, 1), F32)
    total = jnp.zeros((slots, 2 * owners), F32)
    for feat in range(feats):
        ids = ids_ref[feat : feat + 1, :]
        owner = lax.shift_right_logical(ids, shift)
        plane = lax.shift_right_logical(owner, (4 * groups).bit_length() - 1) * 4 + (owner & 3)
        owner = plane * groups + (lax.shift_right_logical(owner, 2) & (groups - 1))
        row = ids & ((1 << shift) - 1)
        hit = (owner_of == owner).astype(F32)
        earlier = contract(hit.astype(BF16), before, 1, 0) + base
        rank = jnp.sum(hit * earlier, axis=0, keepdims=True)
        base = base + jnp.sum(hit, axis=1, keepdims=True)
        rank = rank.astype(jnp.int32)
        spot = owner * stride + rank
        for k in range(half // LANES):
            at = feat * (half // LANES) + k
            place_ref[at : at + 1, :] = spot[:, k * LANES : k * LANES + LANES]
        high = lax.shift_right_logical(row, 8).astype(F32)
        low = (row & 255).astype(F32)
        values = jnp.concatenate([hit * high, hit * low], axis=0).astype(BF16)
        put = (slot_of == rank).astype(F32).astype(BF16)
        total = total + contract(put, values, 1, 1)
    rows = total[:, :owners] * 256.0 + total[:, owners:]
    tall = round_up(slots, LANES)
    if tall > slots:
        rows = jnp.concatenate([rows, jnp.zeros((tall - slots, owners), F32)], axis=0)
    wide = asked_ref.shape[1]
    flat = rows.T
    if wide > tall:
        flat = jnp.concatenate([flat, jnp.zeros((owners, wide - tall), F32)], axis=1)
    asked_ref[...] = flat.astype(jnp.int32)


def lookup_kernel(embed, stride, spot_ref, ids_ref, *refs):
    tables, (rows_ref, blocks_ref) = refs[:-2], refs[-2:]
    groups = len(tables)
    tall, rows_own = tables[0].shape
    parts = rows_own // 256
    wide = ids_ref.shape[1]
    third = stride // 3
    count = jnp.zeros((1, 1), F32)
    for k, table_ref in enumerate(tables):
        table = table_ref[...].astype(F32)
        count = count + 64.0 * table[embed : embed + 1, 0:1] + table[embed : embed + 1, 1:2]
        table = jnp.where(iota((tall, rows_own), 0) < embed, table, 0.0)
        block = jnp.concatenate([table[:, part * 256 : part * 256 + 256] for part in range(parts)], axis=0)
        blocks_ref[spot_ref[1] ^ k] = block.astype(BF16)
    low_of = iota((256, wide), 0)
    high_count = jnp.floor(count * (1.0 / 64.0))
    row, lane = iota((third, LANES), 0), iota((third, LANES), 1)
    counts = jnp.where(lane == LANES - 2, high_count, jnp.where(lane == LANES - 1, count - 64.0 * high_count, 0.0))
    counts = jnp.where(row == 0, counts, 0.0)

    def step(peer, carry):
        for group in range(groups):
            block = peer * groups + group
            ids = ids_ref[pl.ds(block, 1), :]
            high = lax.shift_right_logical(ids, 8)
            pick = (low_of == (ids & 255)).astype(F32).astype(BF16)
            found = contract(blocks_ref[group], pick, 1, 0)
            mine = jnp.zeros((tall, wide), F32)
            for part in range(parts):
                mine = jnp.where(high == part, found[part * tall : part * tall + tall], mine)
            square = jnp.concatenate([mine, jnp.zeros((LANES - tall, wide), F32)], axis=0).T
            packed = square[:third] if group else square[:third] + counts
            for piece in (1, 2):
                packed = packed + pltpu.roll(square[piece * third : piece * third + third], embed * piece, 1)
            rows_ref[pl.ds(pl.multiple_of(block * third, 16), third), :] = packed.astype(BF16)
        return carry

    lax.fori_loop(0, ids_ref.shape[0] // groups, step, 0)


def column_map(feat, dense_width, embed, turned):
    start = dense_width + embed * feat
    tile = start // LANES
    shape = (2 * LANES, LANES) if turned else (LANES, 2 * LANES)
    column, lane = iota(shape, 1 - turned), iota(shape, turned)
    hit = (column == lane + (start - tile * LANES)) & (lane < embed)
    return pl.multiple_of(tile * LANES, LANES), hit.astype(F32).astype(BF16)


def inputs_kernel(
    feats, stride, groups, embed, dense_width, place_ref, rows_ref, dense_ref, x_ref, count_ref, far_ref, even_ref, odd_ref, sum_ref
):
    half = even_ref.shape[0]
    third = stride // 3
    width = dense_width + embed * feats

    def unpack(owner, carry):
        block = rows_ref[pl.ds(pl.multiple_of(owner * third, 16), third), :].astype(F32)
        for piece in range(3):
            rolled = block if piece == 0 else pltpu.roll(block, LANES - embed * piece, 1)
            far_ref[pl.ds(pl.multiple_of(owner * stride + piece * third, 16), third), :] = rolled
        return carry

    owners = far_ref.shape[0] // stride
    lax.fori_loop(0, owners, unpack, 0, unroll=4)
    counts = jnp.zeros((16, LANES), F32)
    for peer in range(owners // groups):
        start = peer * groups * third
        counts = counts + rows_ref[start : start + 16, :].astype(F32)
    count_ref[...] = 64.0 * counts[0:1, LANES - 2 : LANES - 1] + counts[0:1, LANES - 1 : LANES]
    sum_ref[...] = jnp.zeros_like(sum_ref)
    sum_ref[:, :LANES] = dense_ref[...].astype(F32)
    ones = width - width // LANES * LANES
    end = slice(width // LANES * LANES, width // LANES * LANES + LANES)
    sum_ref[:, end] += (iota((half, LANES), 1) == ones).astype(F32)
    odd_ref[...] = jnp.zeros_like(odd_ref)

    def add(ref, at, spread):
        start, spread = spread
        here = slice(at, at + CHUNK)
        sum_ref[here, pl.ds(start, 2 * LANES)] += contract(ref[here, :].astype(BF16), spread, 1, 0)

    def fetch(feat, ref, at):
        rows = [far_ref[pl.ds(place_ref[feat * half + at + k], 1), :] for k in range(CHUNK)]
        for k in range(CHUNK):
            ref[at + k : at + k + 1, :] = rows[k]

    def step(pair, carry):
        spread = column_map(jnp.maximum(2 * pair - 1, 0), dense_width, embed, 0)
        for at in range(0, half, CHUNK):
            add(odd_ref, at, spread)
            fetch(2 * pair, even_ref, at)
        spread = column_map(2 * pair, dense_width, embed, 0)
        for at in range(0, half, CHUNK):
            add(even_ref, at, spread)
            fetch(2 * pair + 1, odd_ref, at)
        return carry

    lax.fori_loop(0, feats // 2, step, 0)
    spread = column_map(feats - 1, dense_width, embed, 0)
    for at in range(0, half, CHUNK):
        add(odd_ref, at, spread)
    x_ref[...] = sum_ref[...].astype(BF16)


def send_kernel(feats, slots, stride, embed, dense_width, place_ref, dx_ref, rows_ref, far_ref, even_ref, odd_ref):
    half = even_ref.shape[0]
    third = stride // 3
    owners = far_ref.shape[0] // stride

    def clear(owner, carry):
        gap = stride - slots
        far_ref[pl.ds(pl.multiple_of(owner * stride + slots, 8), gap), :] = jnp.zeros((gap, LANES), F32)
        return carry

    lax.fori_loop(0, owners, clear, 0, unroll=8)

    def cut(ref, at, spread):
        start, spread = spread
        here = slice(at, at + CHUNK)
        ref[here, :] = contract(dx_ref[here, pl.ds(start, 2 * LANES)], spread, 1, 0)

    def put(feat, ref, at):
        rows = [ref[at + k : at + k + 1, :] for k in range(CHUNK)]
        for k in range(CHUNK):
            far_ref[pl.ds(place_ref[feat * half + at + k], 1), :] = rows[k]

    spread = column_map(0, dense_width, embed, 1)
    for at in range(0, half, CHUNK):
        cut(even_ref, at, spread)

    def step(pair, carry):
        spread = column_map(2 * pair + 1, dense_width, embed, 1)
        for at in range(0, half, CHUNK):
            cut(odd_ref, at, spread)
            put(2 * pair, even_ref, at)
        spread = column_map(jnp.minimum(2 * pair + 2, feats - 1), dense_width, embed, 1)
        for at in range(0, half, CHUNK):
            cut(even_ref, at, spread)
            put(2 * pair + 1, odd_ref, at)
        return carry

    lax.fori_loop(0, feats // 2, step, 0)

    def pack(owner, carry):
        packed = jnp.zeros((third, LANES), F32)
        for piece in range(3):
            block = far_ref[pl.ds(pl.multiple_of(owner * stride + piece * third, 8), third), :]
            packed = packed + (block if piece == 0 else pltpu.roll(block, embed * piece, 1))
        rows_ref[pl.ds(pl.multiple_of(owner * third, 16), third), :] = packed.astype(BF16)
        return carry

    lax.fori_loop(0, owners, pack, 0, unroll=4)


def table_kernel(embed, slots, stride, spot_ref, ids_ref, rows_ref, own_ref, other_ref, total_ref):
    groups, size = total_ref.shape[:2]
    tall = round_up(embed, 8)
    parts = size // tall
    wide = ids_ref.shape[1]
    third = stride // 3
    low_of = iota((256, wide), 0)
    lane = iota((1, wide), 1)
    total_ref[...] = jnp.zeros_like(total_ref)

    def step(peer, carry):
        for group in range(groups):
            at = peer * groups + group
            ids = jnp.where(lane < slots, ids_ref[pl.ds(at, 1), :], -1)
            high = lax.shift_right_arithmetic(ids, 8)
            pick = (low_of == (ids & 255)).astype(F32).astype(BF16)
            block = rows_ref[pl.ds(pl.multiple_of(at * third, 16), third), :].astype(F32)
            pieces = [block if k == 0 else pltpu.roll(block, LANES - embed * k, 1) for k in range(3)]
            if wide > stride:
                pieces.append(jnp.zeros((wide - stride, LANES), F32))
            square = jnp.concatenate(pieces, axis=0)[:wide].T
            mine = jnp.where(iota((tall, wide), 0) < embed, square[:tall], 0.0)
            spread = [jnp.where(high == part, mine, 0.0) for part in range(parts)]
            total_ref[group] += contract(jnp.concatenate(spread, axis=0).astype(BF16), pick, 1, 1)
        return carry

    lax.fori_loop(0, ids_ref.shape[0] // groups, step, 0)
    own_ref[...] = total_ref[spot_ref[1]]
    for k in range(1, groups):
        other_ref[k - 1] = total_ref[spot_ref[1] ^ k].astype(BF16)


def update_kernel(*refs):
    own_ref, table_ref, first_ref, second_ref = refs[:4]
    others = refs[4:-4]
    grad_ref, first_new_ref, second_new_ref, table_new_ref = refs[-4:]
    embed, rows_own = table_ref.shape
    tall = round_up(embed, 8)
    total = own_ref[...]
    for ref in others:
        total = total + ref[...].astype(F32)
    for part in range(rows_own // 256):
        here = slice(part * 256, part * 256 + 256)
        grad = total[part * tall : part * tall + embed, :]
        one, two, new = adamw(table_ref[:, here], grad, first_ref[:, here], second_ref[:, here], 0.25)
        grad_ref[:, here] = grad
        first_new_ref[:, here] = one
        second_new_ref[:, here] = two
        table_new_ref[:, here] = new


def tiles(size):
    return [(at, min(256, size - at)) for at in range(0, size, 256)]


def towers_kernel(
    spot_ref, count_ref, bias_ref, x_ref, vec_ref, labels_ref,
    own_ref, half_ref, half_core_ref, here_ref, here_core_ref, near_ref, near_core_ref,
    one_ref, d_second_ref, d_first_ref, d_deep_ref, dx_ref, head_ref,
    cross_ref, all_deep_ref, pre_first_ref, layer_ref, pre_second_ref, two_ref, slope_ref, hidden_ref, arrival,
):
    half, wide = x_ref.shape
    groups, _, deep_rows = here_ref.shape[:3]
    hidden = 8 * groups * deep_rows
    tower, near, core = spot_ref[0], spot_ref[2], spot_ref[3]
    middle = half_ref.shape[0]
    moves = [(own_ref, cross_ref.at[tower, pl.ds(0, 2 * middle), :])]
    for ref, at_core in ((half_ref, core), (half_core_ref, 1 - core)):
        moves.append((ref, cross_ref.at[1 - tower, pl.ds(pl.multiple_of(at_core * middle, 16), middle), :]))
    for ref, at_near, at_core in (
        (here_ref, near, core), (here_core_ref, near, 1 - core), (near_ref, 1 - near, core), (near_core_ref, 1 - near, 1 - core)
    ):
        for k in range(2):
            moves.append((ref.at[:, k], all_deep_ref.at[k, :, at_near, at_core]))
    copies = []
    for k, (source, target) in enumerate(moves):
        copies.append(pltpu.make_async_copy(source, target, arrival.at[k]))
        copies[-1].start()

    def deep_block(at, size):
        tower, at = at // (hidden // 2), at % (hidden // 2)
        block = all_deep_ref[tower, pl.ds(at // (4 * deep_rows), size // (4 * deep_rows))]
        return block.reshape(size, wide)

    def lanes(x):
        total = x[:, :LANES]
        for at in range(LANES, x.shape[1], LANES):
            total = total + x[:, at : at + LANES]
        return total

    if 2 * middle < wide:
        cross_ref[:, 2 * middle :, :] = jnp.zeros((2, wide - 2 * middle, wide), BF16)
    for copy in copies[:3]:
        copy.wait()
    for at, size in tiles(wide):
        here = slice(at, at + size)
        base = x_ref[:, here].astype(F32)
        pre = contract(x_ref[...], cross_ref[0, :, here], 1, 0) + vec_ref[0:1, here]
        layer = base * pre + base
        pre_first_ref[:, here] = pre
        layer_ref[:, here] = layer
        one_ref[:, here] = layer.astype(BF16)
    score = jnp.zeros((half, LANES), F32)
    for at, size in tiles(wide):
        here = slice(at, at + size)
        base = x_ref[:, here].astype(F32)
        pre = contract(one_ref[...], cross_ref[1, :, here], 1, 0) + vec_ref[1:2, here]
        two = (base * pre + layer_ref[:, here]).astype(BF16)
        pre_second_ref[:, here] = pre
        two_ref[:, here] = two
        score = score + lanes(two.astype(F32) * vec_ref[3:4, here])
    for copy in copies[3:]:
        copy.wait()
    for at, size in tiles(hidden):
        here = slice(at, at + size)
        pre = contract(x_ref[...], deep_block(at, size), 1, 1) + vec_ref[2:3, here]
        gate = jax.nn.sigmoid(pre)
        out = (pre * gate).astype(BF16)
        hidden_ref[:, here] = out
        slope_ref[:, here] = gate * (1.0 + pre * (1.0 - gate))
        score = score + lanes(out.astype(F32) * vec_ref[4:5, here])
    logit = jnp.sum(score, axis=1, keepdims=True) + bias_ref[0, 0]
    labels = jnp.concatenate([labels_ref[...], jnp.zeros((6, half), jnp.int32)], axis=0).astype(F32).T
    target, valid = labels[:, 0:1], labels[:, 1:2]
    softplus = jnp.maximum(logit, 0.0) + jnp.log1p(jnp.exp(-jnp.abs(logit)))
    loss = jnp.sum(valid * (softplus - target * logit), axis=0, keepdims=True)
    d_logit = valid * (jax.nn.sigmoid(logit) - target) / count_ref[0, 0]
    bias_grad = jnp.sum(d_logit, axis=0, keepdims=True)
    lane = iota((1, wide), 1)
    head_ref[...] = jnp.zeros_like(head_ref)
    head_ref[2:3, :] = jnp.where(lane == 0, bias_grad, jnp.where(lane == 1, loss, 0.0))
    for at, size in tiles(wide):
        here = slice(at, at + size)
        base = x_ref[:, here].astype(F32)
        d_second_ref[:, here] = (d_logit * vec_ref[3:4, here] * base).astype(BF16)
        head_ref[0:1, here] = jnp.sum(d_logit * two_ref[:, here].astype(F32), axis=0, keepdims=True)
    for at, size in tiles(hidden):
        here = slice(at, at + size)
        d_deep_ref[:, here] = (d_logit * vec_ref[4:5, here] * slope_ref[:, here]).astype(BF16)
        head_ref[1:2, here] = jnp.sum(d_logit * hidden_ref[:, here].astype(F32), axis=0, keepdims=True)
    for at, size in tiles(wide):
        here = slice(at, at + size)
        base = x_ref[:, here].astype(F32)
        d_two = d_logit * vec_ref[3:4, here]
        d_one = contract(d_second_ref[...], cross_ref[1, here, :], 1, 1) + d_two
        d_first_ref[:, here] = (d_one * base).astype(BF16)
        layer_ref[:, here] = d_one * (1.0 + pre_first_ref[:, here]) + d_two * pre_second_ref[:, here]
    for at, size in tiles(wide):
        here = slice(at, at + size)
        columns = all_deep_ref[:, :, :, :, :, here].reshape(hidden, size)
        dx = contract(d_first_ref[...], cross_ref[0, here, :], 1, 1) + contract(d_deep_ref[...], columns, 1, 0)
        dx_ref[:, here] = (dx + layer_ref[:, here]).astype(BF16)


def grads_kernel(
    deep_rows, spot_ref, x_ref, one_ref, d_second_ref, d_first_ref, d_deep_ref, head_ref,
    keep_ref, give_ref, rest_ref, turned_ref,
):
    half, wide = x_ref.shape
    hidden = d_deep_ref.shape[1]
    mid, rows, main = keep_ref.shape[3:]
    towers, groups, pairs = 2, 2 * mid, 2
    rows_c = rows - deep_rows
    even = spot_ref[3] == 0

    def share(value, tower, at, size, chunk, first):
        by_tower = tower ^ spot_ref[0]
        for group in range(groups):
            by_far = group ^ spot_ref[1]
            upper = by_far // mid
            for pair in range(pairs):
                by_near = pair ^ spot_ref[2]
                one = by_tower + upper * (by_near - by_tower)
                two = by_near + upper * (by_tower - by_near)
                start = (group * pairs + pair) * 2 * chunk
                low, high = value[start : start + chunk], value[start + chunk : start + 2 * chunk]
                place = (upper, one, two, by_far % mid, slice(first, first + chunk), slice(at, at + size))
                keep_ref[place] = jnp.where(even, low, high).astype(BF16)
                give_ref[place] = jnp.where(even, high, low).astype(BF16)

    rest_ref[...] = jnp.zeros_like(rest_ref)
    for tower, (left, right) in enumerate(((one_ref, d_second_ref), (x_ref, d_first_ref))):
        tower = 1 - tower
        turned_ref[...] = left[...].T
        for at, size in tiles(main):
            value = contract(turned_ref[...], right[:, at : at + size], 1, 0)
            share(value, tower, at, size, rows_c, 0)
            rest_ref[16 * tower : 16 * tower + 3, at : at + size] = value[main : main + 3]
            rest_ref[6 + tower : 7 + tower, at : at + size] = value[main + 3 : main + 4]
        value = contract(turned_ref[...], right[:, main:wide], 1, 0)
        rest_ref[16 * tower : 16 * tower + 3, main:wide] = value[main : main + 3]
        rest_ref[6 + tower : 7 + tower, main:wide] = value[main + 3 : main + 4]
        rest_ref[16 * tower + 3 : 16 * tower + 6, :main] = value[:main].T[:3]
    bias = contract(turned_ref[main:wide, :], d_deep_ref[...], 1, 0)
    rest_ref[8:12, :hidden] = bias[:4]
    rest_ref[12:15, :] = head_ref[0:3, :]
    mine, other = rest_ref[0:8, :], rest_ref[16:24, :]
    swap = (iota((8, wide), 0) < 6) & (iota((8, wide), 1) >= wide * (1 - spot_ref[0]))
    rest_ref[0:8, :] = jnp.where(swap, other, mine)
    rest_ref[16:24, :] = jnp.where(swap, mine, other)
    turned_ref[:hidden, :] = d_deep_ref[...].T
    for at, size in tiles(main):
        value = contract(turned_ref[:hidden, :], x_ref[:, at : at + size], 1, 0)
        for tower in range(towers):
            share(value[tower * (hidden // towers) : (tower + 1) * (hidden // towers)], tower, at, size, deep_rows, rows_c)


def cross_kernel(
    other, blocks, place_ref, near_ref, far_ref, rest_ref, weight_ref, first_ref, second_ref, *refs
):
    held_ref, made_ref, arrival, departure = refs[-4:]
    sources, targets, copy_ref = (weight_ref, first_ref, second_ref), refs[-9:-5], refs[-5]
    step, full = pl.program_id(0), blocks // 2
    width = weight_ref.shape[2]
    half, main = near_ref.shape[1:]
    rows = 2 * half
    even = (place_ref[0] & 1) == 0

    def moves(at, size, inward):
        start = pl.multiple_of(cross_block(other, blocks, at, place_ref) * rows, 8)
        pairs = []
        for k, ref in enumerate(sources if inward else targets):
            outside = ref.at[pl.ds(start, size), 0, :]
            inside = (held_ref if inward else made_ref).at[k, at, pl.ds(0, size), :]
            if inward:
                pairs.append(pltpu.make_async_copy(outside, inside, arrival.at[k, at]))
            else:
                pairs.append(pltpu.make_async_copy(inside, outside, departure.at[k, at]))
        return pairs

    spans = [(at, rows) for at in range(full)] + [(full, width - main)] * other

    @pl.when(step == 0)
    def _():
        for at, size in spans:
            for move in moves(at, size, True):
                move.start()

    def update(at, columns, grad):
        here = (slice(at, at + grad.shape[0]), columns)
        weight, first, second = (held_ref[(k, step) + here] for k in range(3))
        one, two, new = adamw(weight, grad, first, second, 0.03)
        for k, value in enumerate((grad, one, two, new)):
            made_ref[(k, step) + here] = value
        copy_ref[here] = new.astype(BF16)

    @pl.when(step < full)
    def _():
        for move in moves(step, rows, True):
            move.wait()
        for at in range(0, main, 256):
            columns = slice(at, min(at + 256, main))
            near, far = near_ref[0, :, columns].astype(F32), far_ref[0, :, columns].astype(F32)
            update(0, columns, jnp.where(even, near, far))
            update(half, columns, jnp.where(even, far, near))
        block = cross_block(other, blocks, step, place_ref)
        lane = pl.multiple_of(block * rows // LANES * LANES, LANES)
        side = rest_ref[0, :, pl.ds(lane, LANES)]
        side = jnp.concatenate([side, jnp.zeros((LANES - 8, LANES), F32)], axis=0).T
        parts = [side[at : at + rows] for at in range(0, LANES, rows)]
        side = parts[0]
        for k, part in enumerate(parts):
            side = jnp.where(block % len(parts) == k, part, side)
        update(0, slice(main, width), side[:, 3 : 3 + width - main])
        for move in moves(step, rows, False):
            move.start()

    if other:

        @pl.when(step == full)
        def _():
            for move in moves(full, width - main, True):
                move.wait()
            update(0, slice(0, width), rest_ref[0, :, :width])
            for move in moves(full, width - main, False):
                move.start()

    @pl.when(step == pl.num_programs(0) - 1)
    def _():
        for at, size in spans:
            for move in moves(at, size, False):
                move.wait()


def cross_block(other, blocks, step, place_ref):
    block = step * 2 + (((place_ref[0] >> 1) & 1) ^ other)
    return jnp.where(step == blocks // 2, blocks, block)


def flip(x, axis, bit, size):
    return lax.ppermute(x, axis, [(i, i ^ bit) for i in range(size)])


def pick(x, axis, index):
    return lax.dynamic_index_in_dim(x, index, axis, keepdims=False)


def join(mine, other, axis, index):
    return jnp.where(index == 0, jnp.stack([mine, other], axis), jnp.stack([other, mine], axis))


def flip_far(x, batch, groups):
    return jnp.stack([x] + [flip(x, "batch", k * 4, batch) for k in range(1, groups)])


def in_order(parts, groups):
    far = lax.axis_index("batch") // 4
    return jnp.stack([pick(parts, 0, k ^ far) for k in range(groups)])


def local(
    dense_feats,
    category_ids,
    labels,
    valid_mask,
    embed_table,
    table_first,
    table_second,
    cross_weight,
    cross_first,
    cross_second,
    deep_weight,
    deep_first,
    deep_second,
    vectors,
    vector_first,
    vector_second,
):
    towers, batch = lax.axis_size("tower"), lax.axis_size("batch")
    owners = towers * batch
    tower, place = lax.axis_index("tower"), lax.axis_index("batch")
    core, near, far = place & 1, (place >> 1) & 1, place >> 2
    groups = batch // 4
    spot = jnp.stack([tower, far, near, core])
    rows_own, embed = embed_table.shape
    examples, feats = category_ids.shape
    half = examples // towers
    width = cross_weight.shape[1]
    deep_rows = deep_weight.shape[0]
    hidden = deep_rows * owners
    dense_width = dense_feats.shape[1]
    wide = round_up(width, LANES)
    slots = half * feats // owners
    third = round_up(-(-slots // 3), 16)
    stride = 3 * third
    shift = rows_own.bit_length() - 1
    asked_wide = round_up(stride, LANES)

    def mine(x, dim):
        return lax.dynamic_slice_in_dim(x, tower * half, half, dim)

    ids = mine(category_ids.T, 1)
    valid = mine(valid_mask, 0)
    target = mine(labels, 0)
    dense = jnp.pad(mine(dense_feats, 0), ((0, 0), (0, LANES - dense_width)))

    table_t = embed_table.T
    tall = round_up(embed, 8)
    asked, slot, table_low = pl.pallas_call(
        functools.partial(slots_kernel, shift, slots, stride, groups),
        out_shape=(
            jax.ShapeDtypeStruct((owners, asked_wide), jnp.int32),
            jax.ShapeDtypeStruct((feats * half // LANES, LANES), jnp.int32),
            jax.ShapeDtypeStruct((tall, rows_own), BF16),
        ),
        in_specs=[in_vmem()] * 3,
        out_specs=(in_vmem(),) * 3,
        compiler_params=params(32),
        name="slots",
    )(ids, valid.reshape(1, half), table_t)
    slot = slot.reshape(-1)
    planes = [[t * batch + z * 4 + k for t in range(towers) for k in range(4)] for z in range(groups)]

    def in_plane(x):
        return lax.all_to_all(
            x, ("tower", "batch"), split_axis=0, concat_axis=0, axis_index_groups=planes, tiled=True
        )

    tables = [table_low] + [flip(table_low, "batch", k * 4, batch) for k in range(1, groups)]

    main = width // LANES * LANES
    rows_c = main // batch
    middle = round_up(-(-width // 2), 16)
    own_low = jnp.pad(cross_weight[0].astype(BF16), ((0, 2 * middle - width), (0, wide - width)))
    deep_own = jnp.pad(deep_weight.astype(BF16), ((0, 0), (0, wide - width)))
    asked, deep_own = lax.optimization_barrier((asked, deep_own))
    arrived = in_plane(asked)
    deep_pair = join(deep_own, flip(deep_own, "tower", 1, towers), 0, tower)
    tables[1:], own_low, arrived = lax.optimization_barrier((tables[1:], own_low, arrived))
    got_low = flip(lax.dynamic_slice_in_dim(own_low, core * middle, middle, 0), "tower", 1, towers)
    weights = flip_far(deep_pair, batch, groups)
    found = pl.pallas_call(
        functools.partial(lookup_kernel, embed, stride),
        out_shape=jax.ShapeDtypeStruct((owners * third, LANES), BF16),
        in_specs=[in_smem()] + [in_vmem()] * (1 + groups),
        out_specs=in_vmem(),
        scratch_shapes=[pltpu.VMEM((groups, rows_own // 256 * tall, 256), BF16)],
        compiler_params=params(32),
        name="lookup",
    )(spot, arrived, *tables)
    returned = in_plane(found)
    weights = in_order(weights, groups)

    def widen(x):
        return jnp.pad(x, (0, wide - x.shape[0]))

    vec = jnp.stack(
        [
            widen(vectors[:width]),
            widen(vectors[width : 2 * width]),
            widen(vectors[2 * width : 2 * width + hidden]),
            widen(vectors[2 * width + hidden : 3 * width + hidden]).astype(BF16).astype(F32),
            widen(vectors[3 * width + hidden : 3 * width + 2 * hidden]).astype(BF16).astype(F32),
        ]
        + [jnp.zeros((wide,), F32)] * 3
    )
    returned, own_low, got_low, weights, vec = lax.optimization_barrier((returned, own_low, got_low, weights, vec))
    got_core = flip(got_low, "batch", 1, batch)
    weights_core = flip(weights, "batch", 1, batch)
    weights_near = flip(weights, "batch", 2, batch)
    inputs, count = pl.pallas_call(
        functools.partial(inputs_kernel, feats, stride, groups, embed, dense_width),
        out_shape=(jax.ShapeDtypeStruct((half, wide), BF16), jax.ShapeDtypeStruct((1, 1), F32)),
        in_specs=[in_smem(), in_vmem(), in_vmem()],
        out_specs=(in_vmem(), in_vmem()),
        scratch_shapes=[
            pltpu.VMEM((owners * stride, LANES), F32),
            pltpu.VMEM((half, LANES), F32),
            pltpu.VMEM((half, LANES), F32),
            pltpu.VMEM((half, wide), F32),
        ],
        compiler_params=params(48),
        name="inputs",
    )(slot, returned, dense)

    inputs, count, weights_near = lax.optimization_barrier((inputs, count, weights_near))
    weights_both = flip(weights_near, "batch", 1, batch)
    low = jax.ShapeDtypeStruct((half, wide), BF16)
    low_deep = jax.ShapeDtypeStruct((half, hidden), BF16)
    one_low, d_second, d_first, d_deep, d_inputs, heads = pl.pallas_call(
        towers_kernel,
        out_shape=(low, low, low, low_deep, low, jax.ShapeDtypeStruct((8, wide), F32)),
        in_specs=[in_smem()] * 3 + [in_vmem()] * 3 + [pl.BlockSpec(memory_space=pl.ANY)] * 7,
        out_specs=(in_vmem(),) * 6,
        scratch_shapes=[
            pltpu.VMEM((2, wide, wide), BF16),
            pltpu.VMEM((2, groups, 2, 2, deep_rows, wide), BF16),
            pltpu.VMEM((half, wide), F32),
            pltpu.VMEM((half, wide), F32),
            pltpu.VMEM((half, wide), F32),
            pltpu.VMEM((half, wide), BF16),
            pltpu.VMEM((half, hidden), F32),
            pltpu.VMEM((half, hidden), BF16),
            pltpu.SemaphoreType.DMA((11,)),
        ],
        compiler_params=params(56),
        name="towers",
    )(
        spot, count, vectors[-1:].reshape(1, 1), inputs, vec, jnp.stack([target, valid]),
        own_low, got_low, got_core, weights, weights_core, weights_near, weights_both,
    )
    parts = jax.ShapeDtypeStruct((2, 2, 2, groups // 2, rows_c + deep_rows, main), BF16)
    keep, give, rest = pl.pallas_call(
        functools.partial(grads_kernel, deep_rows),
        out_shape=(parts, parts, jax.ShapeDtypeStruct((24, wide), F32)),
        in_specs=[in_smem()] + [in_vmem()] * 6,
        out_specs=(in_vmem(),) * 3,
        scratch_shapes=[pltpu.VMEM((wide, half), BF16)],
        compiler_params=params(56),
        name="grads",
    )(spot, inputs, one_low, d_second, d_first, d_deep, heads)
    got = flip(give, "batch", 1, batch)
    rest = rest + flip(rest, "batch", 1, batch)

    def by_tower(x):
        return flip(x, "tower", 1, towers)

    def by_near(x):
        return flip(x, "batch", 2, batch)

    to_one, rest, d_inputs = lax.optimization_barrier(([keep[k, 1] + got[k, 1] for k in range(2)], rest, d_inputs))
    from_one = [by_tower(to_one[0]), by_near(to_one[1])]
    rest, cross_rest = rest[:16], jnp.concatenate([rest[16:22], rest[6:16]])
    diagonal = [(i, i ^ batch ^ 2) for i in range(owners)]
    diagonal = lax.ppermute(cross_rest, ("tower", "batch"), diagonal)
    rest = (rest + by_tower(cross_rest)) + (by_near(rest) + diagonal)
    sent = pl.pallas_call(
        functools.partial(send_kernel, feats, slots, stride, embed, dense_width),
        out_shape=jax.ShapeDtypeStruct((owners * third, LANES), BF16),
        in_specs=[in_smem(), in_vmem()],
        out_specs=in_vmem(),
        scratch_shapes=[
            pltpu.VMEM((owners * stride, LANES), F32),
            pltpu.VMEM((half, LANES), F32),
            pltpu.VMEM((half, LANES), F32),
        ],
        compiler_params=params(48),
        name="send",
    )(slot, d_inputs)
    from_one, rest, sent = lax.optimization_barrier((from_one, rest, sent))
    to_two = lax.optimization_barrier([keep[k, 0, 1] + got[k, 0, 1] + from_one[k][1] for k in range(2)])
    from_two = [by_near(to_two[0]), by_tower(to_two[1])]
    by_far = [flip(rest, "batch", k * 4, batch) for k in range(1, 4)]
    rest = (rest + by_far[0]) + (by_far[1] + by_far[2])
    for bit in [16 << k for k in range(groups.bit_length() - 3)]:
        rest = rest + flip(rest, "batch", bit, batch)
    from_two, rest, sent = lax.optimization_barrier((from_two, rest, sent))
    back = in_plane(sent)
    blocks_t = (rows_own // 256 * tall, 256)
    both = [keep[k, 0, 0] + got[k, 0, 0] + from_one[k][0] + from_two[k] for k in range(2)]
    both = lax.optimization_barrier([part[k] for part in both for k in range(groups // 2)])
    from_far = [flip(both[k], "batch", k * 4, batch) for k in range(1, groups)]
    table_own, table_other = pl.pallas_call(
        functools.partial(table_kernel, embed, slots, stride),
        out_shape=(jax.ShapeDtypeStruct(blocks_t, F32), jax.ShapeDtypeStruct((groups - 1,) + blocks_t, BF16)),
        in_specs=[in_smem()] + [in_vmem()] * 2,
        out_specs=(in_vmem(),) * 2,
        scratch_shapes=[pltpu.VMEM((groups,) + blocks_t, F32)],
        compiler_params=params(32),
        name="table",
    )(spot, arrived, back)
    vector_grad = jnp.concatenate(
        [rest[6, :width], rest[7, :width], rest[11, :hidden], rest[12, :width], rest[13, :hidden], rest[14, :1]]
    )
    vector_one, vector_two, vector_new = adamw(vectors, vector_grad, vector_first, vector_second, 0.03)
    tail = lax.dynamic_slice_in_dim(rest[8 : 8 + width - main], (tower * batch + place) * deep_rows, deep_rows, 1).T
    from_far, tail, vector_grad, vector_one, vector_two, vector_new = lax.optimization_barrier(
        (from_far, tail, vector_grad, vector_one, vector_two, vector_new)
    )
    summed = both[0].astype(F32)
    for part in from_far:
        summed = summed + part.astype(F32)
    chunk = flip_far(summed[:rows_c].astype(BF16), batch, groups)
    deep_grad = jnp.concatenate([summed[rows_c:], tail], axis=1)
    deep_one, deep_two, deep_new = adamw(deep_weight, deep_grad, deep_first, deep_second, 0.03)
    deep_copy = deep_new.astype(BF16)
    chunk, table_own, table_other, deep_grad, deep_one, deep_two, deep_new, deep_copy = lax.optimization_barrier(
        (chunk, table_own, table_other, deep_grad, deep_one, deep_two, deep_new, deep_copy)
    )
    across = flip(chunk, "batch", 2, batch)
    side = rest[:8][None]
    table_got = [flip(table_other[k - 1], "batch", k * 4, batch) for k in range(1, groups)]
    cross_t = [x.transpose(1, 0, 2) for x in (cross_weight, cross_first, cross_second)]
    blocks = batch // 2
    rows = 2 * rows_c
    shape_c = jax.ShapeDtypeStruct((width, 1, width), F32)

    def update_cross(other, chunk, partner, done):
        def from_far(step, at):
            return (jnp.minimum(step, groups - 1) ^ (at[0] >> 2), 0, 0)

        piece = pl.BlockSpec((1, rows_c, main), from_far)
        low = pl.BlockSpec((rows, width), lambda step, at: (cross_block(other, blocks, step, at), 0))
        return pl.pallas_call(
            functools.partial(cross_kernel, other, blocks),
            grid_spec=pltpu.PrefetchScalarGridSpec(
                num_scalar_prefetch=1,
                grid=(groups + other,),
                in_specs=[piece, piece, pl.BlockSpec((1, 8, wide), lambda step, at: (0, 0, 0))]
                + [pl.BlockSpec(memory_space=pl.ANY)] * (3 + len(done)),
                out_specs=(pl.BlockSpec(memory_space=pl.ANY),) * 4 + (low,),
                scratch_shapes=[
                    pltpu.VMEM((3, groups + other, rows, width), F32),
                    pltpu.VMEM((4, groups + other, rows, width), F32),
                    pltpu.SemaphoreType.DMA((3, groups + other)),
                    pltpu.SemaphoreType.DMA((4, groups + other)),
                ],
            ),
            out_shape=(shape_c,) * 4 + (jax.ShapeDtypeStruct((width, width), BF16),),
            input_output_aliases={7 + k: k for k in range(len(done))},
            compiler_params=params(60),
            name="cross_other" if other else "cross",
        )(place.reshape(1), chunk, partner, side, *cross_t, *done)

    cross_out = update_cross(0, chunk, flip(chunk, "batch", 1, batch), ())
    cross_out, across, table_got = lax.optimization_barrier((cross_out, across, table_got))
    across_core = flip(across, "batch", 1, batch)
    shape_t = jax.ShapeDtypeStruct((embed, rows_own), F32)
    table_grad, table_one, table_two, table_new = pl.pallas_call(
        update_kernel,
        out_shape=(shape_t,) * 4,
        in_specs=[in_vmem()] * (3 + groups),
        out_specs=(in_vmem(),) * 4,
        compiler_params=params(32),
        name="update",
    )(table_own, table_t, table_first.T, table_second.T, *table_got)
    across_core, table_grad, table_one, table_two, table_new = lax.optimization_barrier(
        (across_core, table_grad, table_one, table_two, table_new)
    )
    cross_out = update_cross(1, across, across_core, cross_out)
    cross_grad, cross_one, cross_two, cross_new = (x.transpose(1, 0, 2) for x in cross_out[:4])
    loss_sum = rest[14, 1]
    return (
        loss_sum,
        count[0, 0],
        cross_grad,
        cross_one,
        cross_two,
        cross_new,
        cross_out[4][None],
        deep_grad,
        deep_one,
        deep_two,
        deep_new,
        deep_copy,
        table_grad.T,
        table_one.T,
        table_two.T,
        table_new.T,
        vector_grad,
        vector_one,
        vector_two,
        vector_new,
    )


def solution(mesh):
    both = P(("tower", "batch"), None)
    cross = P("tower", None, None)
    return jax.shard_map(
        local,
        mesh=mesh,
        in_specs=(
            P("batch", None),
            P("batch", None),
            P("batch"),
            P("batch"),
            both,
            both,
            both,
            cross,
            cross,
            cross,
            both,
            both,
            both,
            P(),
            P(),
            P(),
        ),
        out_specs=(P(), P()) + (cross,) * 5 + (both,) * 9 + (P(),) * 4,
        check_vma=False,
    )
```

```python
import functools

import jax
import jax.numpy as jnp
from jax import lax
from jax.experimental import pallas as pl
from jax.experimental.pallas import tpu as pltpu
from jax.sharding import PartitionSpec as P

STEP = 5
LANES = 128
CHUNK = 128
BF16 = jnp.bfloat16
F32 = jnp.float32


def round_up(value, unit):
    return -(-value // unit) * unit


def adamw(weight, grad, first, second, rate):
    first_new = 0.9 * first + 0.1 * grad
    second_new = 0.999 * second + 0.001 * grad * grad
    update = (
        first_new / (1.0 - 0.9**STEP) / (jnp.sqrt(second_new / (1.0 - 0.999**STEP)) + 1e-08)
        + 0.01 * weight
    )
    return (first_new, second_new, weight - rate * update)


def contract(left, right, left_dim, right_dim):
    return lax.dot_general(
        left, right, (((left_dim,), (right_dim,)), ((), ())), preferred_element_type=F32
    )


def iota(shape, dim):
    return lax.broadcasted_iota(jnp.int32, shape, dim)


def in_vmem():
    return pl.BlockSpec(memory_space=pltpu.VMEM)


def in_smem():
    return pl.BlockSpec(memory_space=pltpu.SMEM)


def params(mib):
    return pltpu.CompilerParams(vmem_limit_bytes=mib * 2**20)


def takes(micros):
    return pl.CostEstimate(flops=0, bytes_accessed=micros * 3_000_000, transcendentals=0)


def slots_kernel(shift, slots, stride, groups, ids_ref, valid_ref, table_ref, asked_ref, place_ref, low_ref):
    feats, half = ids_ref.shape
    owners = asked_ref.shape[0]
    embed, rows_own = table_ref.shape
    real = jnp.sum(valid_ref[...].astype(F32), axis=1, keepdims=True)
    high_real = jnp.floor(real * (1.0 / 64.0))
    spare = (low_ref.shape[0] - embed, rows_own)
    lane = iota(spare, 1)
    counts = jnp.where(lane == 0, high_real, jnp.where(lane == 1, real - 64.0 * high_real, 0.0))
    low_ref[...] = jnp.concatenate([table_ref[...], counts], axis=0).astype(BF16)
    before = (iota((half, half), 0) < iota((half, half), 1)).astype(BF16)
    owner_of = iota((owners, half), 0)
    slot_of = iota((slots, half), 0)
    base = jnp.zeros((owners, 1), F32)
    total = jnp.zeros((slots, 2 * owners), F32)
    for feat in range(feats):
        ids = ids_ref[feat : feat + 1, :]
        owner = lax.shift_right_logical(ids, shift)
        plane = lax.shift_right_logical(owner, (4 * groups).bit_length() - 1) * 4 + (owner & 3)
        owner = plane * groups + (lax.shift_right_logical(owner, 2) & (groups - 1))
        row = ids & ((1 << shift) - 1)
        hit = (owner_of == owner).astype(F32)
        earlier = contract(hit.astype(BF16), before, 1, 0) + base
        rank = jnp.sum(hit * earlier, axis=0, keepdims=True)
        base = base + jnp.sum(hit, axis=1, keepdims=True)
        rank = rank.astype(jnp.int32)
        spot = owner * stride + rank
        for k in range(half // LANES):
            at = feat * (half // LANES) + k
            place_ref[at : at + 1, :] = spot[:, k * LANES : k * LANES + LANES]
        high = lax.shift_right_logical(row, 8).astype(F32)
        low = (row & 255).astype(F32)
        values = jnp.concatenate([hit * high, hit * low], axis=0).astype(BF16)
        put = (slot_of == rank).astype(F32).astype(BF16)
        total = total + contract(put, values, 1, 1)
    rows = total[:, :owners] * 256.0 + total[:, owners:]
    tall = round_up(slots, LANES)
    if tall > slots:
        rows = jnp.concatenate([rows, jnp.zeros((tall - slots, owners), F32)], axis=0)
    wide = asked_ref.shape[1]
    flat = rows.T
    if wide > tall:
        flat = jnp.concatenate([flat, jnp.zeros((owners, wide - tall), F32)], axis=1)
    asked_ref[...] = flat.astype(jnp.int32)


def lookup_kernel(embed, stride, spot_ref, ids_ref, *refs):
    tables, (rows_ref, blocks_ref) = refs[:-2], refs[-2:]
    groups = len(tables)
    tall, rows_own = tables[0].shape
    parts = rows_own // 256
    wide = ids_ref.shape[1]
    third = stride // 3
    count = jnp.zeros((1, 1), F32)
    for k, table_ref in enumerate(tables):
        table = table_ref[...].astype(F32)
        count = count + 64.0 * table[embed : embed + 1, 0:1] + table[embed : embed + 1, 1:2]
        table = jnp.where(iota((tall, rows_own), 0) < embed, table, 0.0)
        block = jnp.concatenate([table[:, part * 256 : part * 256 + 256] for part in range(parts)], axis=0)
        blocks_ref[spot_ref[1] ^ k] = block.astype(BF16)
    low_of = iota((256, wide), 0)
    high_count = jnp.floor(count * (1.0 / 64.0))
    row, lane = iota((third, LANES), 0), iota((third, LANES), 1)
    counts = jnp.where(lane == LANES - 2, high_count, jnp.where(lane == LANES - 1, count - 64.0 * high_count, 0.0))
    counts = jnp.where(row == 0, counts, 0.0)

    def step(peer, carry):
        for group in range(groups):
            block = peer * groups + group
            ids = ids_ref[pl.ds(block, 1), :]
            high = lax.shift_right_logical(ids, 8)
            pick = (low_of == (ids & 255)).astype(F32).astype(BF16)
            found = contract(blocks_ref[group], pick, 1, 0)
            mine = jnp.zeros((tall, wide), F32)
            for part in range(parts):
                mine = jnp.where(high == part, found[part * tall : part * tall + tall], mine)
            square = jnp.concatenate([mine, jnp.zeros((LANES - tall, wide), F32)], axis=0).T
            packed = square[:third] if group else square[:third] + counts
            for piece in (1, 2):
                packed = packed + pltpu.roll(square[piece * third : piece * third + third], embed * piece, 1)
            rows_ref[pl.ds(pl.multiple_of(block * third, 16), third), :] = packed.astype(BF16)
        return carry

    lax.fori_loop(0, ids_ref.shape[0] // groups, step, 0, unroll=2)


def column_map(feat, dense_width, embed, turned):
    start = dense_width + embed * feat
    tile = start // LANES
    shape = (2 * LANES, LANES) if turned else (LANES, 2 * LANES)
    column, lane = iota(shape, 1 - turned), iota(shape, turned)
    hit = (column == lane + (start - tile * LANES)) & (lane < embed)
    return pl.multiple_of(tile * LANES, LANES), hit.astype(F32).astype(BF16)


def inputs_kernel(
    feats, stride, groups, embed, dense_width, place_ref, rows_ref, dense_ref, x_ref, count_ref, far_ref, even_ref, odd_ref, sum_ref
):
    half = even_ref.shape[0]
    third = stride // 3
    width = dense_width + embed * feats

    def unpack(owner, carry):
        block = rows_ref[pl.ds(pl.multiple_of(owner * third, 16), third), :].astype(F32)
        for piece in range(3):
            rolled = block if piece == 0 else pltpu.roll(block, LANES - embed * piece, 1)
            far_ref[pl.ds(pl.multiple_of(owner * stride + piece * third, 16), third), :] = rolled
        return carry

    owners = far_ref.shape[0] // stride
    lax.fori_loop(0, owners, unpack, 0, unroll=4)
    counts = jnp.zeros((16, LANES), F32)
    for peer in range(owners // groups):
        start = peer * groups * third
        counts = counts + rows_ref[start : start + 16, :].astype(F32)
    count_ref[...] = 64.0 * counts[0:1, LANES - 2 : LANES - 1] + counts[0:1, LANES - 1 : LANES]
    sum_ref[...] = jnp.zeros_like(sum_ref)
    sum_ref[:, :LANES] = dense_ref[...].astype(F32)
    ones = width - width // LANES * LANES
    end = slice(width // LANES * LANES, width // LANES * LANES + LANES)
    sum_ref[:, end] += (iota((half, LANES), 1) == ones).astype(F32)
    odd_ref[...] = jnp.zeros_like(odd_ref)

    def add(ref, at, spread):
        start, spread = spread
        here = slice(at, at + CHUNK)
        sum_ref[here, pl.ds(start, 2 * LANES)] += contract(ref[here, :].astype(BF16), spread, 1, 0)

    def fetch(feat, ref, at):
        rows = [far_ref[pl.ds(place_ref[feat * half + at + k], 1), :] for k in range(CHUNK)]
        for k in range(CHUNK):
            ref[at + k : at + k + 1, :] = rows[k]

    def step(pair, carry):
        spread = column_map(jnp.maximum(2 * pair - 1, 0), dense_width, embed, 0)
        for at in range(0, half, CHUNK):
            add(odd_ref, at, spread)
            fetch(2 * pair, even_ref, at)
        spread = column_map(2 * pair, dense_width, embed, 0)
        for at in range(0, half, CHUNK):
            add(even_ref, at, spread)
            fetch(2 * pair + 1, odd_ref, at)
        return carry

    lax.fori_loop(0, feats // 2, step, 0)
    spread = column_map(feats - 1, dense_width, embed, 0)
    for at in range(0, half, CHUNK):
        add(odd_ref, at, spread)
    x_ref[...] = sum_ref[...].astype(BF16)


def send_kernel(feats, slots, stride, embed, dense_width, place_ref, dx_ref, rows_ref, far_ref, even_ref, odd_ref):
    half = even_ref.shape[0]
    third = stride // 3
    owners = far_ref.shape[0] // stride

    def clear(owner, carry):
        gap = stride - slots
        far_ref[pl.ds(pl.multiple_of(owner * stride + slots, 8), gap), :] = jnp.zeros((gap, LANES), F32)
        return carry

    lax.fori_loop(0, owners, clear, 0, unroll=8)

    def cut(ref, at, spread):
        start, spread = spread
        here = slice(at, at + half)
        ref[here, :] = contract(dx_ref[here, pl.ds(start, 2 * LANES)], spread, 1, 0)

    def put(feat, ref, at):
        rows = [ref[at + k : at + k + 1, :] for k in range(half)]
        for k in range(half):
            far_ref[pl.ds(place_ref[feat * half + at + k], 1), :] = rows[k]

    spread = column_map(0, dense_width, embed, 1)
    for at in range(0, half, half):
        cut(even_ref, at, spread)

    def step(pair, carry):
        spread = column_map(2 * pair + 1, dense_width, embed, 1)
        for at in range(0, half, half):
            cut(odd_ref, at, spread)
            put(2 * pair, even_ref, at)
        spread = column_map(jnp.minimum(2 * pair + 2, feats - 1), dense_width, embed, 1)
        for at in range(0, half, half):
            cut(even_ref, at, spread)
            put(2 * pair + 1, odd_ref, at)
        return carry

    lax.fori_loop(0, feats // 2, step, 0)

    def pack(owner, carry):
        packed = jnp.zeros((third, LANES), F32)
        for piece in range(3):
            block = far_ref[pl.ds(pl.multiple_of(owner * stride + piece * third, 8), third), :]
            packed = packed + (block if piece == 0 else pltpu.roll(block, embed * piece, 1))
        rows_ref[pl.ds(pl.multiple_of(owner * third, 16), third), :] = packed.astype(BF16)
        return carry

    lax.fori_loop(0, owners, pack, 0, unroll=4)


def table_kernel(embed, slots, stride, spot_ref, ids_ref, rows_ref, own_ref, other_ref, total_ref):
    groups, size = total_ref.shape[:2]
    tall = round_up(embed, 8)
    parts = size // tall
    wide = ids_ref.shape[1]
    third = stride // 3
    low_of = iota((256, wide), 0)
    lane = iota((1, wide), 1)
    total_ref[...] = jnp.zeros_like(total_ref)

    def step(peer, carry):
        for group in range(groups):
            at = peer * groups + group
            ids = jnp.where(lane < slots, ids_ref[pl.ds(at, 1), :], -1)
            high = lax.shift_right_arithmetic(ids, 8)
            pick = (low_of == (ids & 255)).astype(F32).astype(BF16)
            block = rows_ref[pl.ds(pl.multiple_of(at * third, 16), third), :].astype(F32)
            pieces = [block if k == 0 else pltpu.roll(block, LANES - embed * k, 1) for k in range(3)]
            if wide > stride:
                pieces.append(jnp.zeros((wide - stride, LANES), F32))
            square = jnp.concatenate(pieces, axis=0)[:wide].T
            mine = jnp.where(iota((tall, wide), 0) < embed, square[:tall], 0.0)
            spread = [jnp.where(high == part, mine, 0.0) for part in range(parts)]
            total_ref[group] += contract(jnp.concatenate(spread, axis=0).astype(BF16), pick, 1, 1)
        return carry

    lax.fori_loop(0, ids_ref.shape[0] // groups, step, 0, unroll=2)
    own_ref[...] = total_ref[spot_ref[1]]
    for k in range(1, groups):
        other_ref[k - 1] = total_ref[spot_ref[1] ^ k].astype(BF16)


def update_kernel(*refs):
    own_ref, table_ref, first_ref, second_ref = refs[:4]
    others = refs[4:-4]
    grad_ref, first_new_ref, second_new_ref, table_new_ref = refs[-4:]
    embed, rows_own = table_ref.shape
    tall = round_up(embed, 8)
    total = own_ref[...]
    for ref in others:
        total = total + ref[...].astype(F32)
    for part in range(rows_own // 256):
        here = slice(part * 256, part * 256 + 256)
        grad = total[part * tall : part * tall + embed, :]
        one, two, new = adamw(table_ref[:, here], grad, first_ref[:, here], second_ref[:, here], 0.25)
        grad_ref[:, here] = grad
        first_new_ref[:, here] = one
        second_new_ref[:, here] = two
        table_new_ref[:, here] = new


def tiles(size):
    return [(at, min(256, size - at)) for at in range(0, size, 256)]


def towers_kernel(
    spot_ref, count_ref, bias_ref, x_ref, vec_ref, labels_ref,
    own_ref, half_ref, half_core_ref, here_ref, here_core_ref, near_ref, near_core_ref,
    one_ref, d_second_ref, d_first_ref, d_deep_ref, dx_ref, head_ref,
    cross_ref, all_deep_ref, pre_first_ref, layer_ref, pre_second_ref, two_ref, slope_ref, hidden_ref, arrival,
):
    half, wide = x_ref.shape
    groups, _, deep_rows = here_ref.shape[:3]
    hidden = 8 * groups * deep_rows
    tower, near, core = spot_ref[0], spot_ref[2], spot_ref[3]
    middle = half_ref.shape[0]
    moves = [(own_ref, cross_ref.at[tower, pl.ds(0, 2 * middle), :])]
    for ref, at_core in ((half_ref, core), (half_core_ref, 1 - core)):
        moves.append((ref, cross_ref.at[1 - tower, pl.ds(pl.multiple_of(at_core * middle, 16), middle), :]))
    for ref, at_near, at_core in (
        (here_ref, near, core), (here_core_ref, near, 1 - core), (near_ref, 1 - near, core), (near_core_ref, 1 - near, 1 - core)
    ):
        for k in range(2):
            moves.append((ref.at[:, k], all_deep_ref.at[k, :, at_near, at_core]))
    copies = []
    for k, (source, target) in enumerate(moves):
        copies.append(pltpu.make_async_copy(source, target, arrival.at[k]))
        copies[-1].start()

    def deep_block(at, size):
        tower, at = at // (hidden // 2), at % (hidden // 2)
        block = all_deep_ref[tower, pl.ds(at // (4 * deep_rows), size // (4 * deep_rows))]
        return block.reshape(size, wide)

    def lanes(x):
        total = x[:, :LANES]
        for at in range(LANES, x.shape[1], LANES):
            total = total + x[:, at : at + LANES]
        return total

    if 2 * middle < wide:
        cross_ref[:, 2 * middle :, :] = jnp.zeros((2, wide - 2 * middle, wide), BF16)
    for copy in copies[:3]:
        copy.wait()
    for at, size in tiles(wide):
        here = slice(at, at + size)
        base = x_ref[:, here].astype(F32)
        pre = contract(x_ref[...], cross_ref[0, :, here], 1, 0) + vec_ref[0:1, here]
        layer = base * pre + base
        pre_first_ref[:, here] = pre
        layer_ref[:, here] = layer
        one_ref[:, here] = layer.astype(BF16)
    score = jnp.zeros((half, LANES), F32)
    for at, size in tiles(wide):
        here = slice(at, at + size)
        base = x_ref[:, here].astype(F32)
        pre = contract(one_ref[...], cross_ref[1, :, here], 1, 0) + vec_ref[1:2, here]
        two = (base * pre + layer_ref[:, here]).astype(BF16)
        pre_second_ref[:, here] = pre
        two_ref[:, here] = two
        score = score + lanes(two.astype(F32) * vec_ref[3:4, here])
    for copy in copies[3:]:
        copy.wait()
    for at, size in tiles(hidden):
        here = slice(at, at + size)
        pre = contract(x_ref[...], deep_block(at, size), 1, 1) + vec_ref[2:3, here]
        gate = jax.nn.sigmoid(pre)
        out = (pre * gate).astype(BF16)
        hidden_ref[:, here] = out
        slope_ref[:, here] = gate * (1.0 + pre * (1.0 - gate))
        score = score + lanes(out.astype(F32) * vec_ref[4:5, here])
    logit = jnp.sum(score, axis=1, keepdims=True) + bias_ref[0, 0]
    labels = jnp.concatenate([labels_ref[...], jnp.zeros((6, half), jnp.int32)], axis=0).astype(F32).T
    target, valid = labels[:, 0:1], labels[:, 1:2]
    softplus = jnp.maximum(logit, 0.0) + jnp.log1p(jnp.exp(-jnp.abs(logit)))
    loss = jnp.sum(valid * (softplus - target * logit), axis=0, keepdims=True)
    d_logit = valid * (jax.nn.sigmoid(logit) - target) / count_ref[0, 0]
    bias_grad = jnp.sum(d_logit, axis=0, keepdims=True)
    lane = iota((1, wide), 1)
    head_ref[...] = jnp.zeros_like(head_ref)
    head_ref[2:3, :] = jnp.where(lane == 0, bias_grad, jnp.where(lane == 1, loss, 0.0))
    for at, size in tiles(wide):
        here = slice(at, at + size)
        base = x_ref[:, here].astype(F32)
        d_second_ref[:, here] = (d_logit * vec_ref[3:4, here] * base).astype(BF16)
        head_ref[0:1, here] = jnp.sum(d_logit * two_ref[:, here].astype(F32), axis=0, keepdims=True)
    for at, size in tiles(hidden):
        here = slice(at, at + size)
        d_deep_ref[:, here] = (d_logit * vec_ref[4:5, here] * slope_ref[:, here]).astype(BF16)
        head_ref[1:2, here] = jnp.sum(d_logit * hidden_ref[:, here].astype(F32), axis=0, keepdims=True)
    for at, size in tiles(wide):
        here = slice(at, at + size)
        base = x_ref[:, here].astype(F32)
        d_two = d_logit * vec_ref[3:4, here]
        d_one = contract(d_second_ref[...], cross_ref[1, here, :], 1, 1) + d_two
        d_first_ref[:, here] = (d_one * base).astype(BF16)
        layer_ref[:, here] = d_one * (1.0 + pre_first_ref[:, here]) + d_two * pre_second_ref[:, here]
    for at, size in tiles(wide):
        here = slice(at, at + size)
        columns = all_deep_ref[:, :, :, :, :, here].reshape(hidden, size)
        dx = contract(d_first_ref[...], cross_ref[0, here, :], 1, 1) + contract(d_deep_ref[...], columns, 1, 0)
        dx_ref[:, here] = (dx + layer_ref[:, here]).astype(BF16)


def grads_kernel(
    deep_rows, spot_ref, x_ref, one_ref, d_second_ref, d_first_ref, d_deep_ref, head_ref,
    keep_ref, give_ref, rest_ref, turned_ref,
):
    half, wide = x_ref.shape
    hidden = d_deep_ref.shape[1]
    mid, rows, main = keep_ref.shape[3:]
    towers, groups, pairs = 2, 2 * mid, 2
    rows_c = rows - deep_rows
    even = spot_ref[3] == 0

    def share(value, tower, at, size, chunk, first):
        by_tower = tower ^ spot_ref[0]
        for group in range(groups):
            by_far = group ^ spot_ref[1]
            upper = by_far // mid
            for pair in range(pairs):
                by_near = pair ^ spot_ref[2]
                one = by_tower + upper * (by_near - by_tower)
                two = by_near + upper * (by_tower - by_near)
                start = (group * pairs + pair) * 2 * chunk
                low, high = value[start : start + chunk], value[start + chunk : start + 2 * chunk]
                place = (upper, one, two, by_far % mid, slice(first, first + chunk), slice(at, at + size))
                keep_ref[place] = jnp.where(even, low, high).astype(BF16)
                give_ref[place] = jnp.where(even, high, low).astype(BF16)

    rest_ref[...] = jnp.zeros_like(rest_ref)
    for tower, (left, right) in enumerate(((one_ref, d_second_ref), (x_ref, d_first_ref))):
        tower = 1 - tower
        turned_ref[...] = left[...].T
        for at, size in tiles(main):
            value = contract(turned_ref[...], right[:, at : at + size], 1, 0)
            share(value, tower, at, size, rows_c, 0)
            rest_ref[16 * tower : 16 * tower + 3, at : at + size] = value[main : main + 3]
            rest_ref[6 + tower : 7 + tower, at : at + size] = value[main + 3 : main + 4]
        value = contract(turned_ref[...], right[:, main:wide], 1, 0)
        rest_ref[16 * tower : 16 * tower + 3, main:wide] = value[main : main + 3]
        rest_ref[6 + tower : 7 + tower, main:wide] = value[main + 3 : main + 4]
        rest_ref[16 * tower + 3 : 16 * tower + 6, :main] = value[:main].T[:3]
    bias = contract(turned_ref[main:wide, :], d_deep_ref[...], 1, 0)
    rest_ref[8:12, :hidden] = bias[:4]
    rest_ref[12:15, :] = head_ref[0:3, :]
    mine, other = rest_ref[0:8, :], rest_ref[16:24, :]
    swap = (iota((8, wide), 0) < 6) & (iota((8, wide), 1) >= wide * (1 - spot_ref[0]))
    rest_ref[0:8, :] = jnp.where(swap, other, mine)
    rest_ref[16:24, :] = jnp.where(swap, mine, other)
    turned_ref[:hidden, :] = d_deep_ref[...].T
    for at, size in tiles(main):
        value = contract(turned_ref[:hidden, :], x_ref[:, at : at + size], 1, 0)
        for tower in range(towers):
            share(value[tower * (hidden // towers) : (tower + 1) * (hidden // towers)], tower, at, size, deep_rows, rows_c)


def cross_kernel(
    other, blocks, place_ref, near_ref, far_ref, rest_ref, weight_ref, first_ref, second_ref, *refs
):
    held_ref, made_ref, arrival, departure = refs[-4:]
    sources, targets, copy_ref = (weight_ref, first_ref, second_ref), refs[-9:-5], refs[-5]
    step, full = pl.program_id(0), blocks // 2
    width = weight_ref.shape[2]
    half, main = near_ref.shape[1:]
    rows = 2 * half
    even = (place_ref[0] & 1) == 0

    def moves(at, size, inward):
        start = pl.multiple_of(cross_block(other, blocks, at, place_ref) * rows, 8)
        pairs = []
        for k, ref in enumerate(sources if inward else targets):
            outside = ref.at[pl.ds(start, size), 0, :]
            inside = (held_ref if inward else made_ref).at[k, at, pl.ds(0, size), :]
            if inward:
                pairs.append(pltpu.make_async_copy(outside, inside, arrival.at[k, at]))
            else:
                pairs.append(pltpu.make_async_copy(inside, outside, departure.at[k, at]))
        return pairs

    spans = [(at, rows) for at in range(full)] + [(full, width - main)] * other

    @pl.when(step == 0)
    def _():
        for at, size in spans:
            for move in moves(at, size, True):
                move.start()

    def update(at, columns, grad):
        here = (slice(at, at + grad.shape[0]), columns)
        weight, first, second = (held_ref[(k, step) + here] for k in range(3))
        one, two, new = adamw(weight, grad, first, second, 0.03)
        for k, value in enumerate((grad, one, two, new)):
            made_ref[(k, step) + here] = value
        copy_ref[here] = new.astype(BF16)

    @pl.when(step < full)
    def _():
        for move in moves(step, rows, True):
            move.wait()
        for at in range(0, main, 256):
            columns = slice(at, min(at + 256, main))
            near, far = near_ref[0, :, columns].astype(F32), far_ref[0, :, columns].astype(F32)
            update(0, columns, jnp.where(even, near, far))
            update(half, columns, jnp.where(even, far, near))
        block = cross_block(other, blocks, step, place_ref)
        lane = pl.multiple_of(block * rows // LANES * LANES, LANES)
        side = rest_ref[0, :, pl.ds(lane, LANES)]
        side = jnp.concatenate([side, jnp.zeros((LANES - 8, LANES), F32)], axis=0).T
        parts = [side[at : at + rows] for at in range(0, LANES, rows)]
        side = parts[0]
        for k, part in enumerate(parts):
            side = jnp.where(block % len(parts) == k, part, side)
        update(0, slice(main, width), side[:, 3 : 3 + width - main])
        for move in moves(step, rows, False):
            move.start()

    if other:

        @pl.when(step == full)
        def _():
            for move in moves(full, width - main, True):
                move.wait()
            update(0, slice(0, width), rest_ref[0, :, :width])
            for move in moves(full, width - main, False):
                move.start()

    @pl.when(step == pl.num_programs(0) - 1)
    def _():
        for at, size in spans:
            for move in moves(at, size, False):
                move.wait()


def cross_block(other, blocks, step, place_ref):
    block = step * 2 + (((place_ref[0] >> 1) & 1) ^ other)
    return jnp.where(step == blocks // 2, blocks, block)


def flip(x, axis, bit, size):
    return lax.ppermute(x, axis, [(i, i ^ bit) for i in range(size)])


def pick(x, axis, index):
    return lax.dynamic_index_in_dim(x, index, axis, keepdims=False)


def join(mine, other, axis, index):
    return jnp.where(index == 0, jnp.stack([mine, other], axis), jnp.stack([other, mine], axis))


def flip_far(x, batch, groups):
    return jnp.stack([x] + [flip(x, "batch", k * 4, batch) for k in range(1, groups)])


def in_order(parts, groups):
    far = lax.axis_index("batch") // 4
    return jnp.stack([pick(parts, 0, k ^ far) for k in range(groups)])


def local(
    dense_feats,
    category_ids,
    labels,
    valid_mask,
    embed_table,
    table_first,
    table_second,
    cross_weight,
    cross_first,
    cross_second,
    deep_weight,
    deep_first,
    deep_second,
    vectors,
    vector_first,
    vector_second,
):
    towers, batch = lax.axis_size("tower"), lax.axis_size("batch")
    owners = towers * batch
    tower, place = lax.axis_index("tower"), lax.axis_index("batch")
    core, near, far = place & 1, (place >> 1) & 1, place >> 2
    groups = batch // 4
    spot = jnp.stack([tower, far, near, core])
    rows_own, embed = embed_table.shape
    examples, feats = category_ids.shape
    half = examples // towers
    width = cross_weight.shape[1]
    deep_rows = deep_weight.shape[0]
    hidden = deep_rows * owners
    dense_width = dense_feats.shape[1]
    wide = round_up(width, LANES)
    slots = half * feats // owners
    third = round_up(-(-slots // 3), 16)
    stride = 3 * third
    shift = rows_own.bit_length() - 1
    asked_wide = round_up(stride, LANES)

    def mine(x, dim):
        return lax.dynamic_slice_in_dim(x, tower * half, half, dim)

    ids = mine(category_ids.T, 1)
    valid = mine(valid_mask, 0)
    target = mine(labels, 0)
    dense = jnp.pad(mine(dense_feats, 0), ((0, 0), (0, LANES - dense_width)))

    table_t = embed_table.T
    tall = round_up(embed, 8)
    asked, slot, table_low = pl.pallas_call(
        functools.partial(slots_kernel, shift, slots, stride, groups),
        out_shape=(
            jax.ShapeDtypeStruct((owners, asked_wide), jnp.int32),
            jax.ShapeDtypeStruct((feats * half // LANES, LANES), jnp.int32),
            jax.ShapeDtypeStruct((tall, rows_own), BF16),
        ),
        in_specs=[in_vmem()] * 3,
        out_specs=(in_vmem(),) * 3,
        compiler_params=params(32),
        name="slots",
    )(ids, valid.reshape(1, half), table_t)
    slot = slot.reshape(-1)
    planes = [[t * batch + z * 4 + k for t in range(towers) for k in range(4)] for z in range(groups)]

    def in_plane(x):
        return lax.all_to_all(
            x, ("tower", "batch"), split_axis=0, concat_axis=0, axis_index_groups=planes, tiled=True
        )

    tables = [table_low] + [flip(table_low, "batch", k * 4, batch) for k in range(1, groups)]

    main = width // LANES * LANES
    rows_c = main // batch
    middle = round_up(-(-width // 2), 16)
    own_low = jnp.pad(cross_weight[0].astype(BF16), ((0, 2 * middle - width), (0, wide - width)))
    deep_own = jnp.pad(deep_weight.astype(BF16), ((0, 0), (0, wide - width)))
    asked, deep_own = lax.optimization_barrier((asked, deep_own))
    arrived = in_plane(asked)
    deep_pair = join(deep_own, flip(deep_own, "tower", 1, towers), 0, tower)
    tables[1:], own_low, arrived = lax.optimization_barrier((tables[1:], own_low, arrived))
    got_low = flip(lax.dynamic_slice_in_dim(own_low, core * middle, middle, 0), "tower", 1, towers)
    weights = flip_far(deep_pair, batch, groups)
    found = pl.pallas_call(
        functools.partial(lookup_kernel, embed, stride),
        out_shape=jax.ShapeDtypeStruct((owners * third, LANES), BF16),
        in_specs=[in_smem()] + [in_vmem()] * (1 + groups),
        out_specs=in_vmem(),
        scratch_shapes=[pltpu.VMEM((groups, rows_own // 256 * tall, 256), BF16)],
        compiler_params=params(32),
        name="lookup",
    )(spot, arrived, *tables)
    returned = in_plane(found)
    weights = in_order(weights, groups)

    def widen(x):
        return jnp.pad(x, (0, wide - x.shape[0]))

    vec = jnp.stack(
        [
            widen(vectors[:width]),
            widen(vectors[width : 2 * width]),
            widen(vectors[2 * width : 2 * width + hidden]),
            widen(vectors[2 * width + hidden : 3 * width + hidden]).astype(BF16).astype(F32),
            widen(vectors[3 * width + hidden : 3 * width + 2 * hidden]).astype(BF16).astype(F32),
        ]
        + [jnp.zeros((wide,), F32)] * 3
    )
    returned, own_low, got_low, weights, vec = lax.optimization_barrier((returned, own_low, got_low, weights, vec))
    got_core = flip(got_low, "batch", 1, batch)
    weights_core = flip(weights, "batch", 1, batch)
    weights_near = flip(weights, "batch", 2, batch)
    inputs, count = pl.pallas_call(
        functools.partial(inputs_kernel, feats, stride, groups, embed, dense_width),
        out_shape=(jax.ShapeDtypeStruct((half, wide), BF16), jax.ShapeDtypeStruct((1, 1), F32)),
        in_specs=[in_smem(), in_vmem(), in_vmem()],
        out_specs=(in_vmem(), in_vmem()),
        scratch_shapes=[
            pltpu.VMEM((owners * stride, LANES), F32),
            pltpu.VMEM((half, LANES), F32),
            pltpu.VMEM((half, LANES), F32),
            pltpu.VMEM((half, wide), F32),
        ],
        compiler_params=params(48),
        name="inputs",
    )(slot, returned, dense)

    inputs, count, weights_near = lax.optimization_barrier((inputs, count, weights_near))
    weights_both = flip(weights_near, "batch", 1, batch)
    low = jax.ShapeDtypeStruct((half, wide), BF16)
    low_deep = jax.ShapeDtypeStruct((half, hidden), BF16)
    one_low, d_second, d_first, d_deep, d_inputs, heads = pl.pallas_call(
        towers_kernel,
        out_shape=(low, low, low, low_deep, low, jax.ShapeDtypeStruct((8, wide), F32)),
        in_specs=[in_smem()] * 3 + [in_vmem()] * 3 + [pl.BlockSpec(memory_space=pl.ANY)] * 7,
        out_specs=(in_vmem(),) * 6,
        scratch_shapes=[
            pltpu.VMEM((2, wide, wide), BF16),
            pltpu.VMEM((2, groups, 2, 2, deep_rows, wide), BF16),
            pltpu.VMEM((half, wide), F32),
            pltpu.VMEM((half, wide), F32),
            pltpu.VMEM((half, wide), F32),
            pltpu.VMEM((half, wide), BF16),
            pltpu.VMEM((half, hidden), F32),
            pltpu.VMEM((half, hidden), BF16),
            pltpu.SemaphoreType.DMA((11,)),
        ],
        compiler_params=params(56),
        name="towers",
    )(
        spot, count, vectors[-1:].reshape(1, 1), inputs, vec, jnp.stack([target, valid]),
        own_low, got_low, got_core, weights, weights_core, weights_near, weights_both,
    )
    parts = jax.ShapeDtypeStruct((2, 2, 2, groups // 2, rows_c + deep_rows, main), BF16)
    keep, give, rest = pl.pallas_call(
        functools.partial(grads_kernel, deep_rows),
        out_shape=(parts, parts, jax.ShapeDtypeStruct((24, wide), F32)),
        in_specs=[in_smem()] + [in_vmem()] * 6,
        out_specs=(in_vmem(),) * 3,
        scratch_shapes=[pltpu.VMEM((wide, half), BF16)],
        compiler_params=params(56),
        name="grads",
    )(spot, inputs, one_low, d_second, d_first, d_deep, heads)
    got = flip(give, "batch", 1, batch)
    rest = rest + flip(rest, "batch", 1, batch)

    def by_tower(x):
        return flip(x, "tower", 1, towers)

    def by_near(x):
        return flip(x, "batch", 2, batch)

    to_one, rest, d_inputs = lax.optimization_barrier(([keep[k, 1] + got[k, 1] for k in range(2)], rest, d_inputs))
    from_one = [by_tower(to_one[0]), by_near(to_one[1])]
    rest, cross_rest = rest[:16], jnp.concatenate([rest[16:22], rest[6:16]])
    diagonal = [(i, i ^ batch ^ 2) for i in range(owners)]
    diagonal = lax.ppermute(cross_rest, ("tower", "batch"), diagonal)
    rest = (rest + by_tower(cross_rest)) + (by_near(rest) + diagonal)
    sent = pl.pallas_call(
        functools.partial(send_kernel, feats, slots, stride, embed, dense_width),
        out_shape=jax.ShapeDtypeStruct((owners * third, LANES), BF16),
        in_specs=[in_smem(), in_vmem()],
        out_specs=in_vmem(),
        scratch_shapes=[
            pltpu.VMEM((owners * stride, LANES), F32),
            pltpu.VMEM((half, LANES), F32),
            pltpu.VMEM((half, LANES), F32),
        ],
        compiler_params=params(48),
        name="send",
    )(slot, d_inputs)
    from_one, rest, sent = lax.optimization_barrier((from_one, rest, sent))
    to_two = lax.optimization_barrier([keep[k, 0, 1] + got[k, 0, 1] + from_one[k][1] for k in range(2)])
    from_two = [by_near(to_two[0]), by_tower(to_two[1])]
    by_far = [flip(rest, "batch", k * 4, batch) for k in range(1, 4)]
    rest = (rest + by_far[0]) + (by_far[1] + by_far[2])
    for bit in [16 << k for k in range(groups.bit_length() - 3)]:
        rest = rest + flip(rest, "batch", bit, batch)
    from_two, rest, sent = lax.optimization_barrier((from_two, rest, sent))
    back = in_plane(sent)
    blocks_t = (rows_own // 256 * tall, 256)
    both = [keep[k, 0, 0] + got[k, 0, 0] + from_one[k][0] + from_two[k] for k in range(2)]
    both = lax.optimization_barrier([part[k] for part in both for k in range(groups // 2)])
    from_far = [flip(both[k], "batch", k * 4, batch) for k in range(1, groups)]
    table_own, table_other = pl.pallas_call(
        functools.partial(table_kernel, embed, slots, stride),
        out_shape=(jax.ShapeDtypeStruct(blocks_t, F32), jax.ShapeDtypeStruct((groups - 1,) + blocks_t, BF16)),
        in_specs=[in_smem()] + [in_vmem()] * 2,
        out_specs=(in_vmem(),) * 2,
        scratch_shapes=[pltpu.VMEM((groups,) + blocks_t, F32)],
        compiler_params=params(32),
        name="table",
    )(spot, arrived, back)
    vector_grad = jnp.concatenate(
        [rest[6, :width], rest[7, :width], rest[11, :hidden], rest[12, :width], rest[13, :hidden], rest[14, :1]]
    )
    vector_one, vector_two, vector_new = adamw(vectors, vector_grad, vector_first, vector_second, 0.03)
    tail = lax.dynamic_slice_in_dim(rest[8 : 8 + width - main], (tower * batch + place) * deep_rows, deep_rows, 1).T
    from_far, tail, vector_grad, vector_one, vector_two, vector_new = lax.optimization_barrier(
        (from_far, tail, vector_grad, vector_one, vector_two, vector_new)
    )
    summed = both[0].astype(F32)
    for part in from_far:
        summed = summed + part.astype(F32)
    chunk = flip_far(summed[:rows_c].astype(BF16), batch, groups)
    deep_grad = jnp.concatenate([summed[rows_c:], tail], axis=1)
    deep_one, deep_two, deep_new = adamw(deep_weight, deep_grad, deep_first, deep_second, 0.03)
    deep_copy = deep_new.astype(BF16)
    chunk, table_own, table_other, deep_grad, deep_one, deep_two, deep_new, deep_copy = lax.optimization_barrier(
        (chunk, table_own, table_other, deep_grad, deep_one, deep_two, deep_new, deep_copy)
    )
    across = flip(chunk, "batch", 2, batch)
    side = rest[:8][None]
    table_got = [flip(table_other[k - 1], "batch", k * 4, batch) for k in range(1, groups)]
    cross_t = [x.transpose(1, 0, 2) for x in (cross_weight, cross_first, cross_second)]
    blocks = batch // 2
    rows = 2 * rows_c
    shape_c = jax.ShapeDtypeStruct((width, 1, width), F32)

    def update_cross(other, chunk, partner, done):
        def from_far(step, at):
            return (jnp.minimum(step, groups - 1) ^ (at[0] >> 2), 0, 0)

        piece = pl.BlockSpec((1, rows_c, main), from_far)
        low = pl.BlockSpec((rows, width), lambda step, at: (cross_block(other, blocks, step, at), 0))
        return pl.pallas_call(
            functools.partial(cross_kernel, other, blocks),
            grid_spec=pltpu.PrefetchScalarGridSpec(
                num_scalar_prefetch=1,
                grid=(groups + other,),
                in_specs=[piece, piece, pl.BlockSpec((1, 8, wide), lambda step, at: (0, 0, 0))]
                + [pl.BlockSpec(memory_space=pl.ANY)] * (3 + len(done)),
                out_specs=(pl.BlockSpec(memory_space=pl.ANY),) * 4 + (low,),
                scratch_shapes=[
                    pltpu.VMEM((3, groups + other, rows, width), F32),
                    pltpu.VMEM((4, groups + other, rows, width), F32),
                    pltpu.SemaphoreType.DMA((3, groups + other)),
                    pltpu.SemaphoreType.DMA((4, groups + other)),
                ],
            ),
            out_shape=(shape_c,) * 4 + (jax.ShapeDtypeStruct((width, width), BF16),),
            input_output_aliases={7 + k: k for k in range(len(done))},
            compiler_params=params(60),
            name="cross_other" if other else "cross",
        )(place.reshape(1), chunk, partner, side, *cross_t, *done)

    cross_out = update_cross(0, chunk, flip(chunk, "batch", 1, batch), ())
    cross_out, across, table_got = lax.optimization_barrier((cross_out, across, table_got))
    across_core = flip(across, "batch", 1, batch)
    shape_t = jax.ShapeDtypeStruct((embed, rows_own), F32)
    table_grad, table_one, table_two, table_new = pl.pallas_call(
        update_kernel,
        out_shape=(shape_t,) * 4,
        in_specs=[in_vmem()] * (3 + groups),
        out_specs=(in_vmem(),) * 4,
        compiler_params=params(32),
        name="update",
    )(table_own, table_t, table_first.T, table_second.T, *table_got)
    across_core, table_grad, table_one, table_two, table_new = lax.optimization_barrier(
        (across_core, table_grad, table_one, table_two, table_new)
    )
    cross_out = update_cross(1, across, across_core, cross_out)
    cross_grad, cross_one, cross_two, cross_new = (x.transpose(1, 0, 2) for x in cross_out[:4])
    loss_sum = rest[14, 1]
    return (
        loss_sum,
        count[0, 0],
        cross_grad,
        cross_one,
        cross_two,
        cross_new,
        cross_out[4][None],
        deep_grad,
        deep_one,
        deep_two,
        deep_new,
        deep_copy,
        table_grad.T,
        table_one.T,
        table_two.T,
        table_new.T,
        vector_grad,
        vector_one,
        vector_two,
        vector_new,
    )


def solution(mesh):
    both = P(("tower", "batch"), None)
    cross = P("tower", None, None)
    return jax.shard_map(
        local,
        mesh=mesh,
        in_specs=(
            P("batch", None),
            P("batch", None),
            P("batch"),
            P("batch"),
            both,
            both,
            both,
            cross,
            cross,
            cross,
            both,
            both,
            both,
            P(),
            P(),
            P(),
        ),
        out_specs=(P(), P()) + (cross,) * 5 + (both,) * 9 + (P(),) * 4,
        check_vma=False,
    )
```
